32 devices in a mesh: fsdp: 32 (over z, y, x, core).
Axes of the slice: x: 2, y: 2, z: 4, core: 2. Of those that a mesh axis runs over, the one named last changes fastest.
Arguments:
- tokens: bfloat16 [512, 16, 1024], P('fsdp'), may hold values from -6 to 6
- depth_count: int32 [512], P('fsdp'), may hold values from 8 to 16, as said below
- cotangent: bfloat16 [512, 16, 1024], P('fsdp'), may hold values from -6.5 to 6.5
- joint_weight: float32 [2048, 3072], P('fsdp'), may hold values from -0.1875 to 0.1875
- output_weight: float32 [2048, 1024], P('fsdp'), may hold values from -0.5 to 0.5
- expand_weight: float32 [2048, 8192], P('fsdp'), may hold values from -0.1875 to 0.1875
- shrink_weight: float32 [2, 4096, 1024], P(None, 'fsdp'), may hold values from -0.09375 to 0.09375
- norm_gains: float32 [2, 1024], P(None, 'fsdp'), may hold values from 0.25 to 2.05
- joint_mean: float32 [2048, 3072], P('fsdp'), may hold values from -0.00012207031 to 0.00012207031
- joint_square: float32 [2048, 3072], P('fsdp'), may hold values from 1.1920201e-10 to 1.9966337e-09
- output_mean: float32 [2048, 1024], P('fsdp'), may hold values from -0.00024414062 to 0.00024414062
- output_square: float32 [2048, 1024], P('fsdp'), may hold values from 7.748131e-10 to 1.2516211e-08
- expand_mean: float32 [2048, 8192], P('fsdp'), may hold values from -0.00024414062 to 0.00024414062
- expand_square: float32 [2048, 8192], P('fsdp'), may hold values from 7.748131e-10 to 1.2516211e-08
- shrink_mean: float32 [2, 4096, 1024], P(None, 'fsdp'), may hold values from -0.00024414062 to 0.00024414062
- shrink_square: float32 [2, 4096, 1024], P(None, 'fsdp'), may hold values from 7.748131e-10 to 1.2516211e-08
- gains_mean: float32 [2, 1024], P(None, 'fsdp'), may hold values from -0.0008544922 to 0.0008544922
- gains_square: float32 [2, 1024], P(None, 'fsdp'), may hold values from 7.1521207e-09 to 1.1324191e-07
Outputs:
- result: bfloat16 [512, 16, 1024], P('fsdp')
- tokens_grad: bfloat16 [512, 16, 1024], P('fsdp')
- grad_norm: float32 [], replicated
- joint_updated: float32 [2048, 3072], P('fsdp')
- joint_mean_out: float32 [2048, 3072], P('fsdp')
- joint_square_out: float32 [2048, 3072], P('fsdp')
- output_updated: float32 [2048, 1024], P('fsdp')
- output_mean_out: float32 [2048, 1024], P('fsdp')
- output_square_out: float32 [2048, 1024], P('fsdp')
- expand_updated: float32 [2048, 8192], P('fsdp')
- expand_mean_out: float32 [2048, 8192], P('fsdp')
- expand_square_out: float32 [2048, 8192], P('fsdp')
- shrink_updated: float32 [2, 4096, 1024], P(None, 'fsdp')
- shrink_mean_out: float32 [2, 4096, 1024], P(None, 'fsdp')
- shrink_square_out: float32 [2, 4096, 1024], P(None, 'fsdp')
- gains_updated: float32 [2, 1024], P(None, 'fsdp')
- gains_mean_out: float32 [2, 1024], P(None, 'fsdp')
- gains_square_out: float32 [2, 1024], P(None, 'fsdp')
The draws below stay inside these ranges and needn't reach their ends.
Inputs may be any that keep to these rules, and one draw needn't show every extreme that they name: `depth_count`: each frame has either half of 16 or 16 live positions.
All inputs are finite; a program needn't handle non-finite values.
Results may differ from the reference program's by a relative error of at most 0.012.
The reference program's roundings to bfloat16 on the way count: a program that leaves them out, or rounds other values in their place, can miss the bound.
Values may be sent and summed in bfloat16 or wider, within the bound.
No kernel may reach another device: no remote copies, remote signals or barrier semaphores. Data moves between devices by JAX's collectives and lax.ppermute only.
A program may use at most 320 MiB of HBM per device.

```python
import math
import jax
import jax.numpy as jnp
from jax import lax

D = 1024
HEADS = 16
FF = 4096
DEPTH = 16
SETS = 2
STEP = 10
FRAMES = 512
NPARAMS = 33556480


def draw_depth_count(key, part):
    key = jax.random.fold_in(key, 11)
    frame_index = jnp.arange(FRAMES).astype(jnp.int32)
    ticket = jax.random.randint(key, (FRAMES,), 0, FRAMES - 1).astype(jnp.int32)
    deep_flag = (ticket < frame_index).astype(jnp.int32)
    return (DEPTH // 2 + DEPTH // 2 * deep_flag).astype(jnp.int32)


def draw_cotangent(key, part):
    key = jax.random.fold_in(key, 13)
    place = jnp.arange(D).astype(jnp.float32) / D
    ramp_row = 0.5 + place
    noise_field = jax.random.truncated_normal(key, -4.0, 4.0, (FRAMES, DEPTH, D), jnp.float32)
    return (noise_field * ramp_row).astype(jnp.bfloat16)


def draw_norm_gains(key, part):
    key = jax.random.fold_in(key, 12)
    place = jnp.arange(D).astype(jnp.float32) / D
    ramp_row = 0.5 + place
    jitter_rows = jax.random.uniform(key, (2, D), jnp.float32, 0.8, 1.2)
    return (ramp_row[None, :] * jitter_rows).astype(jnp.float32)


def shard_levels(rng, dims, cuts, low, top_value):
    loudness = 1.0
    for dim, parts in cuts:
        heights = jax.random.uniform(jax.random.fold_in(jax.random.fold_in(rng, 6), dim), (parts,), jnp.float32, low / len(cuts), top_value / len(cuts))
        loudness = loudness * jnp.repeat(jnp.exp(heights), dims[dim] // parts).reshape((-1,) + (1,) * (len(dims) - 1 - dim))
    return loudness


def gaussian(key, shape, deviation, most, shards=(), held_as=jnp.bfloat16):
    factor_of = shard_levels(key, shape, shards, -0.22, 0.18) if shards else 1.0
    drawn = jax.random.normal(key, shape, jnp.float32) * deviation * factor_of
    return jnp.minimum(jnp.maximum(drawn, -most), most).astype(held_as)


def setup_inputs(seed: int = 0) -> dict:
    key_of = jax.random.split(jax.random.key(seed), 19)
    tokens = gaussian(key_of[0], (FRAMES, DEPTH, D), 1.0, 6.0, ((0, 32),))
    depth_count = draw_depth_count(jax.random.fold_in(key_of[18], 71), 0)
    cotangent = draw_cotangent(jax.random.fold_in(key_of[18], 71), 0)
    joint_weight = gaussian(key_of[3], (SETS * D, 3 * D), D ** -0.5, 0.1875, ((0, 32),), jnp.float32)
    output_weight = gaussian(key_of[4], (SETS * D, D), (D // 8) ** -0.5, 0.5, ((0, 32),), jnp.float32)
    expand_weight = gaussian(key_of[5], (SETS * D, 2 * FF), D ** -0.5, 0.1875, ((0, 32),), jnp.float32)
    shrink_weight = gaussian(key_of[6], (SETS, FF, D), FF ** -0.5, 0.09375, ((1, 32),), jnp.float32)
    norm_gains = draw_norm_gains(jax.random.fold_in(key_of[18], 71), 0)
    joint_mean = gaussian(key_of[8], (SETS * D, 3 * D), (0.045 * NPARAMS ** -0.5), 0.00012207031, ((0, 32),), jnp.float32)
    joint_square = jnp.clip(jnp.exp(math.log(1.9966337472254736e-09) - 2.8183983 * jax.random.uniform(key_of[9], (SETS * D, 3 * D), jnp.float32) ** shard_levels(key_of[9], (SETS * D, 3 * D), ((0, 32),), -0.2, 0.2)), 1.1920200937431957e-10, 1.9966337472254736e-09)
    output_mean = gaussian(key_of[10], (SETS * D, D), (0.11 * NPARAMS ** -0.5), 0.00024414062, ((0, 32),), jnp.float32)
    output_square = jnp.clip(jnp.exp(math.log(1.2516211178592584e-08) - 2.7821581 * jax.random.uniform(key_of[11], (SETS * D, D), jnp.float32) ** shard_levels(key_of[11], (SETS * D, D), ((0, 32),), -0.2, 0.2)), 7.748131025664406e-10, 1.2516211178592584e-08)
    expand_mean = gaussian(key_of[12], (SETS * D, 2 * FF), (0.11 * NPARAMS ** -0.5), 0.00024414062, ((0, 32),), jnp.float32)
    expand_square = jnp.clip(jnp.exp(math.log(1.2516211178592584e-08) - 2.7821581 * jax.random.uniform(key_of[13], (SETS * D, 2 * FF), jnp.float32) ** shard_levels(key_of[13], (SETS * D, 2 * FF), ((0, 32),), -0.2, 0.2)), 7.748131025664406e-10, 1.2516211178592584e-08)
    shrink_mean = gaussian(key_of[14], (SETS, FF, D), (0.11 * NPARAMS ** -0.5), 0.00024414062, ((1, 32),), jnp.float32)
    shrink_square = jnp.clip(jnp.exp(math.log(1.2516211178592584e-08) - 2.7821581 * jax.random.uniform(key_of[15], (SETS, FF, D), jnp.float32) ** shard_levels(key_of[15], (SETS, FF, D), ((1, 32),), -0.2, 0.2)), 7.748131025664406e-10, 1.2516211178592584e-08)
    gains_mean = gaussian(key_of[16], (2, D), (0.33 * NPARAMS ** -0.5), 0.0008544922, ((1, 32),), jnp.float32)
    gains_square = jnp.clip(jnp.exp(math.log(1.1324191007133777e-07) - 2.7621174 * jax.random.uniform(key_of[17], (2, D), jnp.float32) ** shard_levels(key_of[17], (2, D), ((1, 32),), -0.2, 0.2)), 7.152120673481477e-09, 1.1324191007133777e-07)
    return dict(tokens=tokens, depth_count=depth_count, cotangent=cotangent, joint_weight=joint_weight, output_weight=output_weight, expand_weight=expand_weight, shrink_weight=shrink_weight, norm_gains=norm_gains, joint_mean=joint_mean, joint_square=joint_square, output_mean=output_mean, output_square=output_square, expand_mean=expand_mean, expand_square=expand_square, shrink_mean=shrink_mean, shrink_square=shrink_square, gains_mean=gains_mean, gains_square=gains_square)


NORM_EPS = 1e-05
BETA_ONE = 0.9
BETA_TWO = 0.95
ADAM_EPS = 1e-08
MATRIX_RATE = 0.08
GAIN_RATE = 1.0
MATRIX_DECAY = 0.1
CLIP_LIMIT = 1.0

@jax.custom_vjp
def low(v):
    return lax.optimization_barrier(v.astype(jnp.bfloat16)).astype(jnp.float32)

@jax.custom_vjp
def low_back(v):
    return v

def low_keep(v):
    return (low(v), None)

def low_pass(kept, grad):
    return (grad,)

def back_keep(v):
    return (v, None)

def back_low(kept, grad):
    return (low(grad),)
low.defvjp(low_keep, low_pass)
low_back.defvjp(back_keep, back_low)

def per_set_ref(values, weight):
    frame_count, positions, features = values.shape
    grouped = values.reshape(frame_count, SETS, positions // SETS, features)
    product = jnp.einsum('fspd,sde->fspe', grouped, weight, precision=lax.Precision.HIGHEST)
    return product.reshape(frame_count, positions, weight.shape[2])

def attention_ref(mixed):
    frame_count, positions, triple = mixed.shape
    features = triple // 3
    head_dim = features // HEADS
    split = mixed.reshape(frame_count, positions, 3, HEADS, head_dim)
    queries = split[:, :, 0]
    key_rows = split[:, :, 1]
    value_rows = split[:, :, 2]
    raw_scores = jnp.einsum('fphd,fkhd->fhpk', queries, key_rows, precision=lax.Precision.HIGHEST)
    scores = low_back(raw_scores * head_dim ** (-0.5))
    index_row = jnp.arange(positions)
    scores = jnp.where(index_row[:, None] >= index_row[None, :], scores, -1e+30)
    highest = lax.optimization_barrier(jnp.max(scores, axis=-1, keepdims=True))
    exp_scores = jnp.exp(scores - highest)
    attention = exp_scores / lax.optimization_barrier(jnp.sum(exp_scores, axis=-1, keepdims=True))
    context = jnp.einsum('fhpk,fkhd->fphd', low(attention), value_rows, precision=lax.Precision.HIGHEST)
    return low(low_back(context.reshape(frame_count, positions, features)))

def forward_ref(inputs, live_mask, params):
    joint_low = low(params[0])
    output_low = low(params[1])
    expand_low = low(params[2])
    shrink_low = low(params[3])
    gains_low = low(params[4])
    inverse_one = lax.rsqrt(lax.optimization_barrier(jnp.mean(inputs * inputs, axis=-1, keepdims=True)) + NORM_EPS)
    first = low(inputs * inverse_one * gains_low[0])
    mixed = low(low_back(per_set_ref(first, joint_low)))
    context = attention_ref(mixed)
    branch = low_back(per_set_ref(context, output_low))
    middle = inputs + live_mask * branch
    inverse_two = lax.rsqrt(lax.optimization_barrier(jnp.mean(middle * middle, axis=-1, keepdims=True)) + NORM_EPS)
    second = low(middle * inverse_two * gains_low[1])
    gate_values = low_back(per_set_ref(second, expand_low))
    half_width = gate_values.shape[2] // 2
    hidden = low(jax.nn.silu(gate_values[..., :half_width]) * gate_values[..., half_width:])
    shrunk = low_back(per_set_ref(hidden, shrink_low))
    return middle + live_mask * shrunk

def adam_step(weight, grad_value, mean_old, square_old, learn_rate, weight_decay):
    mean_new = BETA_ONE * mean_old + (1.0 - BETA_ONE) * grad_value
    square_new = BETA_TWO * square_old + (1.0 - BETA_TWO) * grad_value * grad_value
    mean_hat = mean_new / (1.0 - BETA_ONE ** STEP)
    square_hat = square_new / (1.0 - BETA_TWO ** STEP)
    weight_new = weight - learn_rate * (mean_hat / (jnp.sqrt(square_hat) + ADAM_EPS) + weight_decay * weight)
    return (weight_new, mean_new, square_new)

def reference(tokens, depth_count, cotangent, joint_weight, output_weight, expand_weight, shrink_weight, norm_gains, joint_mean, joint_square, output_mean, output_square, expand_mean, expand_square, shrink_mean, shrink_square, gains_mean, gains_square):
    frame_total = tokens.shape[0]
    block_size = min(128, frame_total)
    block_count = frame_total // block_size
    params = (joint_weight.reshape(SETS, D, 3 * D), output_weight.reshape(SETS, D, D), expand_weight.reshape(SETS, D, 2 * FF), shrink_weight, norm_gains)
    token_blocks = tokens.reshape(block_count, block_size, DEPTH, D)
    depth_blocks = depth_count.reshape(block_count, block_size)
    cot_blocks = cotangent.reshape(block_count, block_size, DEPTH, D)

    def block_step(totals, pieces):
        piece_tokens, piece_depth, piece_cot = pieces
        inputs = piece_tokens.astype(jnp.float32)
        index_row = jnp.arange(DEPTH).astype(jnp.int32)
        live_mask = (index_row[None, :] < piece_depth[:, None]).astype(jnp.float32)[:, :, None]

        def forward_fn(values, weights):
            return forward_ref(values, live_mask, weights)
        result_block, pullback = jax.vjp(forward_fn, inputs, params)
        grad_inputs, grad_params = pullback(piece_cot.astype(jnp.float32) * live_mask)
        totals = jax.tree.map(jnp.add, totals, grad_params)
        return (totals, (result_block.astype(jnp.bfloat16), grad_inputs.astype(jnp.bfloat16)))
    zero_grads = jax.tree.map(jnp.zeros_like, params)
    grads, outputs = lax.scan(block_step, zero_grads, (token_blocks, depth_blocks, cot_blocks))
    result = outputs[0].reshape(frame_total, DEPTH, D)
    tokens_grad = outputs[1].reshape(frame_total, DEPTH, D)
    grad_joint = grads[0].reshape(joint_weight.shape)
    grad_output = grads[1].reshape(output_weight.shape)
    grad_expand = grads[2].reshape(expand_weight.shape)
    total_sq = jnp.sum(grad_joint * grad_joint) + jnp.sum(grad_output * grad_output) + jnp.sum(grad_expand * grad_expand) + jnp.sum(grads[3] * grads[3]) + jnp.sum(grads[4] * grads[4])
    grad_norm = jnp.sqrt(total_sq)
    factor = CLIP_LIMIT / jnp.maximum(grad_norm, CLIP_LIMIT)
    joint_new = adam_step(joint_weight, factor * grad_joint, joint_mean, joint_square, MATRIX_RATE, MATRIX_DECAY)
    output_new = adam_step(output_weight, factor * grad_output, output_mean, output_square, MATRIX_RATE, MATRIX_DECAY)
    expand_new = adam_step(expand_weight, factor * grad_expand, expand_mean, expand_square, MATRIX_RATE, MATRIX_DECAY)
    shrink_new = adam_step(shrink_weight, factor * grads[3], shrink_mean, shrink_square, MATRIX_RATE, MATRIX_DECAY)
    gains_new = adam_step(norm_gains, factor * grads[4], gains_mean, gains_square, GAIN_RATE, 0.0)
    return (result, tokens_grad, grad_norm, joint_new[0], joint_new[1], joint_new[2], output_new[0], output_new[1], output_new[2], expand_new[0], expand_new[1], expand_new[2], shrink_new[0], shrink_new[1], shrink_new[2], gains_new[0], gains_new[1], gains_new[2])
```

```python
import jax
import jax.numpy as jnp
from jax import lax
from jax.sharding import PartitionSpec as P

HEADS = 16
SETS = 2
STEP = 10

NORM_EPS = 1e-05
BETA_ONE = 0.9
BETA_TWO = 0.95
ADAM_EPS = 1e-08
MATRIX_RATE = 0.08
GAIN_RATE = 1.0
MATRIX_DECAY = 0.1
CLIP_LIMIT = 1.0

BF = jnp.bfloat16
F32 = jnp.float32


def dot(a, b):
    return lax.dot_general(a, b, (((1,), (0,)), ((), ())), preferred_element_type=F32)


def dot_nt(a, b):
    return lax.dot_general(a, b, (((1,), (1,)), ((), ())), preferred_element_type=F32)


def dot_tn(a, b):
    return lax.dot_general(a, b, (((0,), (0,)), ((), ())), preferred_element_type=F32)


def adam_step(weight, grad_value, mean_old, square_old, learn_rate, weight_decay):
    mean_new = BETA_ONE * mean_old + (1.0 - BETA_ONE) * grad_value
    square_new = BETA_TWO * square_old + (1.0 - BETA_TWO) * grad_value * grad_value
    mean_hat = mean_new / (1.0 - BETA_ONE**STEP)
    square_hat = square_new / (1.0 - BETA_TWO**STEP)
    weight_new = weight - learn_rate * (
        mean_hat / (jnp.sqrt(square_hat) + ADAM_EPS) + weight_decay * weight
    )
    return (weight_new, mean_new, square_new)


class Cube:
    def __init__(self, count):
        self.count = count
        self.bits = count.bit_length() - 1
        self.top = self.bits - 1
        self.index = lax.axis_index("fsdp")
        chip = list(range(1, self.top))
        third = max(1, len(chip) // 3)
        self.orders = [chip[third * k :] + chip[: third * k] for k in range(3)]

    def bit(self, b):
        return (self.index >> b) & 1

    def swap(self, value, b):
        pairs = [(i, i ^ (1 << b)) for i in range(self.count)]
        return lax.ppermute(value, "fsdp", pairs)

    def gather(self, value, bits, lead=0):
        have = []
        for b in bits:
            other = self.swap(value, b)
            mine = self.bit(b) == 1
            axis = lead + sum(1 for h in have if h > b)
            low = jnp.where(mine, other, value)
            high = jnp.where(mine, value, other)
            value = jnp.stack([low, high], axis=axis)
            have.append(b)
        return value

    def reduce(self, value, have, bits, lead=0, last=F32):
        have = list(have)
        for step, b in enumerate(bits):
            axis = lead + sum(1 for h in have if h > b)
            mine = self.bit(b)
            send = lax.dynamic_index_in_dim(value, 1 - mine, axis, keepdims=False).astype(BF)
            keep = lax.dynamic_index_in_dim(value, mine, axis, keepdims=False)
            other = self.swap(send, b)
            value = keep.astype(F32) + other.astype(F32)
            if step < len(bits) - 1:
                value = value.astype(BF)
            have.remove(b)
        return value.astype(last)

    def total(self, value):
        for b in range(self.bits):
            value = value + self.swap(value, b)
        return value


def cuts(width, parts=3, unit=128):
    units = width // unit
    sizes = [units // parts + (1 if k < units % parts else 0) for k in range(parts)]
    edges = [0]
    for size in sizes:
        edges.append(edges[-1] + size * unit)
    return edges


def local(
    count,
    tokens,
    depth_count,
    cotangent,
    joint_weight,
    output_weight,
    expand_weight,
    shrink_weight,
    norm_gains,
    joint_mean,
    joint_square,
    output_mean,
    output_square,
    expand_mean,
    expand_square,
    shrink_mean,
    shrink_square,
    gains_mean,
    gains_square,
):
    cube = Cube(count)
    half = count // 2
    own_bits = cube.top
    frames, positions, width = tokens.shape
    run = positions // SETS
    in_set = cube.bit(cube.top)
    upper = in_set == 1
    all_frames = 2 * frames
    rows = all_frames * run
    hidden_width = expand_weight.shape[1] // 2
    head_dim = width // HEADS

    def to_sets(value):
        first, second = value[:, :run], value[:, run:]
        other = cube.swap(jnp.where(upper, first, second), cube.top)
        own = jnp.where(upper, second, first)
        low = jnp.where(upper, other, own)
        high = jnp.where(upper, own, other)
        return jnp.concatenate([low, high], axis=0)

    def from_sets(value):
        value = value.reshape(2, frames, run, value.shape[-1])
        own = jnp.where(upper, value[1], value[0])
        other = cube.swap(jnp.where(upper, value[0], value[1]), cube.top)
        first = jnp.where(upper, other, own)
        second = jnp.where(upper, own, other)
        return jnp.concatenate([first, second], axis=1)

    position_index = jnp.arange(positions)
    live_here = (position_index[None, :] < depth_count[:, None]).astype(F32)[:, :, None]
    masked = (cotangent.astype(F32) * live_here).astype(BF)

    gains_local = norm_gains.astype(BF)
    gains_all = cube.gather(gains_local, range(cube.bits), lead=1)
    gains_all = gains_all.reshape(2, width).astype(F32)

    def gather_matrix(shard, order, lead=0):
        return cube.gather(shard, list(order) + [0], lead=lead)

    joint_low = joint_weight.astype(BF)
    joint_parts = [
        gather_matrix(joint_low[:, k * width : (k + 1) * width], cube.orders[k]).reshape(width, width)
        for k in range(3)
    ]
    x_rows = to_sets(tokens).reshape(rows, width).astype(F32)
    live = to_sets(live_here).reshape(rows, 1)
    cot = to_sets(masked).reshape(rows, width)

    output_low = output_weight.astype(BF)
    expand_low = expand_weight.astype(BF)
    wide = hidden_width // 4
    edge = [0, wide, (wide + hidden_width) // 2, hidden_width]
    expand_shards = []
    for k in range(3):
        gate_cols = expand_low[:, edge[k] : edge[k + 1]]
        up_cols = expand_low[:, hidden_width + edge[k] : hidden_width + edge[k + 1]]
        parts = ([output_low] if k == 0 else []) + [gate_cols, up_cols]
        expand_shards.append(jnp.concatenate(parts, axis=1))
    expand_parts = [
        gather_matrix(expand_shards[k], cube.orders[k]).reshape(width, -1) for k in range(3)
    ]
    output_full = expand_parts[0][:, :width]
    gate_full = [expand_parts[0][:, width : 2 * width]] + [
        expand_parts[k][:, : edge[k + 1] - edge[k]] for k in (1, 2)
    ]
    up_full = [expand_parts[0][:, 2 * width :]] + [
        expand_parts[k][:, edge[k + 1] - edge[k] :] for k in (1, 2)
    ]

    shrink_low = shrink_weight.astype(BF)
    shrink_mine = jnp.where(upper, shrink_low[1], shrink_low[0])
    shrink_send = jnp.where(upper, shrink_low[0], shrink_low[1])
    shrink_other = cube.swap(shrink_send, cube.top)
    shrink_pair = jnp.stack(
        [jnp.where(upper, shrink_other, shrink_mine), jnp.where(upper, shrink_mine, shrink_other)]
    )
    col = cuts(width)
    shrink_parts = [
        gather_matrix(shrink_pair[:, :, col[k] : col[k + 1]], cube.orders[k], lead=1).reshape(
            hidden_width, -1
        )
        for k in range(3)
    ]

    inv_one = lax.rsqrt(jnp.mean(x_rows * x_rows, axis=-1, keepdims=True) + NORM_EPS)
    first = (x_rows * inv_one * gains_all[0]).astype(BF)
    query, key_own, value_own = [dot(first, joint_parts[k]).astype(BF) for k in range(3)]
    key_value = cube.swap(jnp.concatenate([key_own, value_own], axis=1), cube.top)

    def heads(value):
        return value.reshape(all_frames, run, HEADS, head_dim)

    q_h = heads(query)
    k_h = jnp.concatenate([heads(key_value[:, :width]), heads(key_own)], axis=1)
    v_h = jnp.concatenate([heads(key_value[:, width:]), heads(value_own)], axis=1)
    scale = head_dim ** (-0.5)
    scores = jnp.einsum("fphd,fkhd->fhpk", q_h, k_h, preferred_element_type=F32) * scale
    row = jnp.arange(run)[:, None]
    column = jnp.arange(2 * run)[None, :]
    seen = jnp.where(column < run, upper, row >= column - run)
    scores = jnp.where(seen, scores, -1e30)
    exp_scores = jnp.exp(scores - jnp.max(scores, axis=-1, keepdims=True))
    attention = exp_scores / jnp.sum(exp_scores, axis=-1, keepdims=True)
    attention_low = attention.astype(BF)
    context = (
        jnp.einsum("fhpk,fkhd->fphd", attention_low, v_h, preferred_element_type=F32)
        .reshape(rows, width)
        .astype(BF)
    )
    middle = x_rows + live * dot(context, output_full)
    inv_two = lax.rsqrt(jnp.mean(middle * middle, axis=-1, keepdims=True) + NORM_EPS)
    second = (middle * inv_two * gains_all[1]).astype(BF)
    gate = [dot(second, w) for w in gate_full]
    up = [dot(second, w) for w in up_full]
    hidden = jnp.concatenate(
        [(jax.nn.silu(g) * u).astype(BF) for g, u in zip(gate, up)], axis=1
    )
    shrunk = jnp.concatenate([dot(hidden, w) for w in shrink_parts], axis=1)
    result = from_sets((middle + live * shrunk).astype(BF))

    def reduce_matrix(grad, order, lead=0, block=None):
        bits = list(range(own_bits))
        shape = grad.shape
        if lead:
            grad = grad.reshape((2,) + (2,) * own_bits + (shape[0] // 2 // half, shape[1]))
        else:
            grad = grad.reshape((2,) * own_bits + (shape[0] // half, shape[1]))
        return cube.reduce(grad, bits, [0] + list(order), lead=lead)

    grad_shrink_parts = [
        reduce_matrix(dot_tn(hidden, cot[:, col[k] : col[k + 1]]).astype(BF), cube.orders[k], lead=1)
        for k in range(3)
    ]
    grad_shrink_pair = jnp.concatenate(grad_shrink_parts, axis=-1)
    shrink_keep = jnp.where(upper, grad_shrink_pair[1], grad_shrink_pair[0])
    shrink_give = jnp.where(upper, grad_shrink_pair[0], grad_shrink_pair[1]).astype(BF)
    shrink_got = cube.swap(shrink_give, cube.top).astype(F32)
    grad_shrink = jnp.stack(
        [jnp.where(upper, shrink_got, shrink_keep), jnp.where(upper, shrink_keep, shrink_got)]
    )

    grad_hidden = sum(dot_nt(cot[:, col[k] : col[k + 1]], shrink_parts[k]) for k in range(3))
    grad_second = 0.0
    grad_expand_parts = []
    for k in range(3):
        d_hid = grad_hidden[:, edge[k] : edge[k + 1]]
        sig = jax.nn.sigmoid(gate[k])
        d_gate = (d_hid * up[k] * sig * (1.0 + gate[k] * (1.0 - sig))).astype(BF)
        d_up = (d_hid * gate[k] * sig).astype(BF)
        both = jnp.concatenate([d_gate, d_up], axis=1)
        weight_pair = jnp.concatenate([gate_full[k], up_full[k]], axis=1)
        grad_second = grad_second + dot_nt(both, weight_pair)
        grad_expand_parts.append(
            reduce_matrix(dot_tn(second, both).astype(BF), cube.orders[k])
        )
    grad_expand = jnp.concatenate(
        [grad_expand_parts[k][:, : edge[k + 1] - edge[k]] for k in range(3)]
        + [grad_expand_parts[k][:, edge[k + 1] - edge[k] :] for k in range(3)],
        axis=1,
    )

    def normalize_back(values, inverse, gain_row, grad_out):
        scaled = grad_out * gain_row
        grad_in = inverse * scaled - values * inverse * inverse * inverse * jnp.mean(
            scaled * values, axis=-1, keepdims=True
        )
        return (grad_in, jnp.sum(grad_out * values * inverse, axis=0))

    grad_mid_norm, grad_gain_two = normalize_back(middle, inv_two, gains_all[1], grad_second)
    grad_middle = cot.astype(F32) + grad_mid_norm
    grad_branch = (grad_middle * live).astype(BF)
    grad_context = dot_nt(grad_branch, output_full).astype(BF)

    g_h = heads(grad_context)
    grad_attention = jnp.einsum("fphd,fkhd->fhpk", g_h, v_h, preferred_element_type=F32)
    grad_value = jnp.einsum("fhpk,fphd->fkhd", attention_low, g_h, preferred_element_type=F32)
    grad_scores = attention * (
        grad_attention - jnp.sum(grad_attention * attention, axis=-1, keepdims=True)
    )
    grad_scores = grad_scores.astype(BF)
    grad_query = (
        jnp.einsum("fhpk,fkhd->fphd", grad_scores, k_h, preferred_element_type=F32) * scale
    )
    grad_key = jnp.einsum("fhpk,fphd->fkhd", grad_scores, q_h, preferred_element_type=F32) * scale
    give = jnp.concatenate(
        [grad_key[:, :run].reshape(rows, width), grad_value[:, :run].reshape(rows, width)], axis=1
    ).astype(BF)
    got = cube.swap(give, cube.top).astype(F32)
    got = jnp.where(upper, 0.0, got)
    d_query = grad_query.reshape(rows, width).astype(BF)
    d_key = (grad_key[:, run:].reshape(rows, width) + got[:, :width]).astype(BF)
    d_value = (grad_value[:, run:].reshape(rows, width) + got[:, width:]).astype(BF)

    grad_output = reduce_matrix(dot_tn(context, grad_branch).astype(BF), cube.orders[0])
    joint_grads = [
        reduce_matrix(dot_tn(first, d).astype(BF), cube.orders[k])
        for k, d in enumerate((d_query, d_key, d_value))
    ]
    grad_joint = jnp.concatenate(joint_grads, axis=1)
    grad_first = sum(
        dot_nt(d, w) for d, w in zip((d_query, d_key, d_value), joint_parts)
    )
    grad_in_norm, grad_gain_one = normalize_back(x_rows, inv_one, gains_all[0], grad_first)
    grad_inputs = from_sets((grad_middle + grad_in_norm).astype(BF))

    gains_term = jnp.stack([grad_gain_one, grad_gain_two]).reshape((2,) + (2,) * cube.bits + (-1,))
    bits = list(range(cube.bits))
    have = list(bits)
    for b in bits:
        axis = 1 + sum(1 for h in have if h > b)
        mine = cube.bit(b)
        send = lax.dynamic_index_in_dim(gains_term, 1 - mine, axis, keepdims=False)
        keep = lax.dynamic_index_in_dim(gains_term, mine, axis, keepdims=False)
        gains_term = keep + cube.swap(send, b)
        have.remove(b)
    grad_gains = gains_term

    reduced = (grad_joint, grad_output, grad_expand, grad_shrink, grad_gains)
    local_sq = sum(jnp.sum(g * g) for g in reduced)
    total_sq = cube.total(jnp.broadcast_to(local_sq, (8, 128)))[0, 0]
    grad_norm_value = jnp.sqrt(total_sq)
    factor = CLIP_LIMIT / jnp.maximum(grad_norm_value, CLIP_LIMIT)
    joint_new = adam_step(
        joint_weight, factor * reduced[0], joint_mean, joint_square, MATRIX_RATE, MATRIX_DECAY
    )
    output_new = adam_step(
        output_weight, factor * reduced[1], output_mean, output_square, MATRIX_RATE, MATRIX_DECAY
    )
    expand_new = adam_step(
        expand_weight, factor * reduced[2], expand_mean, expand_square, MATRIX_RATE, MATRIX_DECAY
    )
    shrink_new = adam_step(
        shrink_weight, factor * reduced[3], shrink_mean, shrink_square, MATRIX_RATE, MATRIX_DECAY
    )
    gains_new = adam_step(norm_gains, factor * reduced[4], gains_mean, gains_square, GAIN_RATE, 0.0)
    return (
        result,
        grad_inputs,
        grad_norm_value,
        *joint_new,
        *output_new,
        *expand_new,
        *shrink_new,
        *gains_new,
    )


def solution(mesh):
    rows = P("fsdp", None)
    cube = P("fsdp", None, None)
    inner = P(None, "fsdp", None)
    gains = P(None, "fsdp")
    count = mesh.shape["fsdp"]

    def body(*args):
        return local(count, *args)

    return jax.shard_map(
        body,
        mesh=mesh,
        in_specs=(cube, P("fsdp"), cube, rows, rows, rows, inner, gains)
        + (rows,) * 6
        + (inner, inner, gains, gains),
        out_specs=(cube, cube, P()) + (rows,) * 9 + (inner,) * 3 + (gains,) * 3,
        check_vma=False,
    )
```

```python
import functools

import jax
import jax.numpy as jnp
from jax import lax
from jax.experimental import pallas as pl
from jax.experimental.pallas import tpu as pltpu
from jax.sharding import PartitionSpec as P

HEADS = 16
SETS = 2
STEP = 10

NORM_EPS = 1e-05
BETA_ONE = 0.9
BETA_TWO = 0.95
ADAM_EPS = 1e-08
MATRIX_RATE = 0.08
GAIN_RATE = 1.0
MATRIX_DECAY = 0.1
CLIP_LIMIT = 1.0

BF = jnp.bfloat16
F32 = jnp.float32


def dot(a, b):
    return lax.dot_general(a, b, (((1,), (0,)), ((), ())), preferred_element_type=F32)


def dot_nt(a, b):
    return lax.dot_general(a, b, (((1,), (1,)), ((), ())), preferred_element_type=F32)


def dot_tn(a, b):
    return lax.dot_general(a, b, (((0,), (0,)), ((), ())), preferred_element_type=F32)


def adam_step(weight, grad_value, mean_old, square_old, learn_rate, weight_decay):
    mean_new = BETA_ONE * mean_old + (1.0 - BETA_ONE) * grad_value
    square_new = BETA_TWO * square_old + (1.0 - BETA_TWO) * grad_value * grad_value
    mean_hat = mean_new / (1.0 - BETA_ONE**STEP)
    square_hat = square_new / (1.0 - BETA_TWO**STEP)
    weight_new = weight - learn_rate * (
        mean_hat / (jnp.sqrt(square_hat) + ADAM_EPS) + weight_decay * weight
    )
    return (weight_new, mean_new, square_new)


class Cube:
    def __init__(self, count):
        self.count = count
        self.bits = count.bit_length() - 1
        self.top = self.bits - 1
        self.index = lax.axis_index("fsdp")
        chip = list(range(1, self.top))
        third = max(1, len(chip) // 3)
        self.orders = [chip[third * k :] + chip[: third * k] for k in range(3)]

    def bit(self, b):
        return (self.index >> b) & 1

    def swap(self, value, b):
        pairs = [(i, i ^ (1 << b)) for i in range(self.count)]
        return lax.ppermute(value, "fsdp", pairs)

    def gather(self, value, bits, lead=0):
        have = []
        for b in bits:
            other = self.swap(value, b)
            mine = self.bit(b) == 1
            axis = lead + sum(1 for h in have if h > b)
            low = jnp.where(mine, other, value)
            high = jnp.where(mine, value, other)
            value = jnp.stack([low, high], axis=axis)
            have.append(b)
        return value

    def reduce(self, value, have, bits, lead=0, last=F32):
        have = list(have)
        for step, b in enumerate(bits):
            axis = lead + sum(1 for h in have if h > b)
            mine = self.bit(b)
            send = lax.dynamic_index_in_dim(value, 1 - mine, axis, keepdims=False).astype(BF)
            keep = lax.dynamic_index_in_dim(value, mine, axis, keepdims=False)
            other = self.swap(send, b)
            value = keep.astype(F32) + other.astype(F32)
            if step < len(bits) - 1:
                value = value.astype(BF)
            have.remove(b)
        return value.astype(last)

    def total(self, value):
        for b in range(self.bits):
            value = value + self.swap(value, b)
        return value


def cuts(width, parts=3, unit=128):
    units = width // unit
    sizes = [units // parts + (1 if k < units % parts else 0) for k in range(parts)]
    edges = [0]
    for size in sizes:
        edges.append(edges[-1] + size * unit)
    return edges


def local_general(
    count,
    tokens,
    depth_count,
    cotangent,
    joint_weight,
    output_weight,
    expand_weight,
    shrink_weight,
    norm_gains,
    joint_mean,
    joint_square,
    output_mean,
    output_square,
    expand_mean,
    expand_square,
    shrink_mean,
    shrink_square,
    gains_mean,
    gains_square,
):
    cube = Cube(count)
    half = count // 2
    own_bits = cube.top
    frames, positions, width = tokens.shape
    run = positions // SETS
    in_set = cube.bit(cube.top)
    upper = in_set == 1
    all_frames = 2 * frames
    rows = all_frames * run
    hidden_width = expand_weight.shape[1] // 2
    head_dim = width // HEADS

    def to_sets(value):
        first, second = value[:, :run], value[:, run:]
        other = cube.swap(jnp.where(upper, first, second), cube.top)
        own = jnp.where(upper, second, first)
        low = jnp.where(upper, other, own)
        high = jnp.where(upper, own, other)
        return jnp.concatenate([low, high], axis=0)

    def from_sets(value):
        value = value.reshape(2, frames, run, value.shape[-1])
        own = jnp.where(upper, value[1], value[0])
        other = cube.swap(jnp.where(upper, value[0], value[1]), cube.top)
        first = jnp.where(upper, other, own)
        second = jnp.where(upper, own, other)
        return jnp.concatenate([first, second], axis=1)

    position_index = jnp.arange(positions)
    live_here = (position_index[None, :] < depth_count[:, None]).astype(F32)[:, :, None]
    masked = (cotangent.astype(F32) * live_here).astype(BF)

    gains_local = norm_gains.astype(BF)
    gains_all = cube.gather(gains_local, range(cube.bits), lead=1)
    gains_all = gains_all.reshape(2, width).astype(F32)

    def gather_matrix(shard, order, lead=0):
        return cube.gather(shard, list(order) + [0], lead=lead)

    joint_low = joint_weight.astype(BF)
    joint_parts = [
        gather_matrix(joint_low[:, k * width : (k + 1) * width], cube.orders[k]).reshape(width, width)
        for k in range(3)
    ]
    x_rows = to_sets(tokens).reshape(rows, width).astype(F32)
    live = to_sets(live_here).reshape(rows, 1)
    cot = to_sets(masked).reshape(rows, width)

    output_low = output_weight.astype(BF)
    expand_low = expand_weight.astype(BF)
    wide = hidden_width // 4
    edge = [0, wide, (wide + hidden_width) // 2, hidden_width]
    expand_shards = []
    for k in range(3):
        gate_cols = expand_low[:, edge[k] : edge[k + 1]]
        up_cols = expand_low[:, hidden_width + edge[k] : hidden_width + edge[k + 1]]
        parts = ([output_low] if k == 0 else []) + [gate_cols, up_cols]
        expand_shards.append(jnp.concatenate(parts, axis=1))
    expand_parts = [
        gather_matrix(expand_shards[k], cube.orders[k]).reshape(width, -1) for k in range(3)
    ]
    output_full = expand_parts[0][:, :width]
    gate_full = [expand_parts[0][:, width : 2 * width]] + [
        expand_parts[k][:, : edge[k + 1] - edge[k]] for k in (1, 2)
    ]
    up_full = [expand_parts[0][:, 2 * width :]] + [
        expand_parts[k][:, edge[k + 1] - edge[k] :] for k in (1, 2)
    ]

    shrink_low = shrink_weight.astype(BF)
    shrink_mine = jnp.where(upper, shrink_low[1], shrink_low[0])
    shrink_send = jnp.where(upper, shrink_low[0], shrink_low[1])
    shrink_other = cube.swap(shrink_send, cube.top)
    shrink_pair = jnp.stack(
        [jnp.where(upper, shrink_other, shrink_mine), jnp.where(upper, shrink_mine, shrink_other)]
    )
    col = cuts(width)
    shrink_parts = [
        gather_matrix(shrink_pair[:, :, col[k] : col[k + 1]], cube.orders[k], lead=1).reshape(
            hidden_width, -1
        )
        for k in range(3)
    ]

    inv_one = lax.rsqrt(jnp.mean(x_rows * x_rows, axis=-1, keepdims=True) + NORM_EPS)
    first = (x_rows * inv_one * gains_all[0]).astype(BF)
    query, key_own, value_own = [dot(first, joint_parts[k]).astype(BF) for k in range(3)]
    key_value = cube.swap(jnp.concatenate([key_own, value_own], axis=1), cube.top)

    def heads(value):
        return value.reshape(all_frames, run, HEADS, head_dim)

    q_h = heads(query)
    k_h = jnp.concatenate([heads(key_value[:, :width]), heads(key_own)], axis=1)
    v_h = jnp.concatenate([heads(key_value[:, width:]), heads(value_own)], axis=1)
    scale = head_dim ** (-0.5)
    scores = jnp.einsum("fphd,fkhd->fhpk", q_h, k_h, preferred_element_type=F32) * scale
    row = jnp.arange(run)[:, None]
    column = jnp.arange(2 * run)[None, :]
    seen = jnp.where(column < run, upper, row >= column - run)
    scores = jnp.where(seen, scores, -1e30)
    exp_scores = jnp.exp(scores - jnp.max(scores, axis=-1, keepdims=True))
    attention = exp_scores / jnp.sum(exp_scores, axis=-1, keepdims=True)
    attention_low = attention.astype(BF)
    context = (
        jnp.einsum("fhpk,fkhd->fphd", attention_low, v_h, preferred_element_type=F32)
        .reshape(rows, width)
        .astype(BF)
    )
    middle = x_rows + live * dot(context, output_full)
    inv_two = lax.rsqrt(jnp.mean(middle * middle, axis=-1, keepdims=True) + NORM_EPS)
    second = (middle * inv_two * gains_all[1]).astype(BF)
    gate = [dot(second, w) for w in gate_full]
    up = [dot(second, w) for w in up_full]
    hidden = jnp.concatenate(
        [(jax.nn.silu(g) * u).astype(BF) for g, u in zip(gate, up)], axis=1
    )
    shrunk = jnp.concatenate([dot(hidden, w) for w in shrink_parts], axis=1)
    result = from_sets((middle + live * shrunk).astype(BF))

    def reduce_matrix(grad, order, lead=0, block=None):
        bits = list(range(own_bits))
        shape = grad.shape
        if lead:
            grad = grad.reshape((2,) + (2,) * own_bits + (shape[0] // 2 // half, shape[1]))
        else:
            grad = grad.reshape((2,) * own_bits + (shape[0] // half, shape[1]))
        return cube.reduce(grad, bits, [0] + list(order), lead=lead)

    grad_shrink_parts = [
        reduce_matrix(dot_tn(hidden, cot[:, col[k] : col[k + 1]]).astype(BF), cube.orders[k], lead=1)
        for k in range(3)
    ]
    grad_shrink_pair = jnp.concatenate(grad_shrink_parts, axis=-1)
    shrink_keep = jnp.where(upper, grad_shrink_pair[1], grad_shrink_pair[0])
    shrink_give = jnp.where(upper, grad_shrink_pair[0], grad_shrink_pair[1]).astype(BF)
    shrink_got = cube.swap(shrink_give, cube.top).astype(F32)
    grad_shrink = jnp.stack(
        [jnp.where(upper, shrink_got, shrink_keep), jnp.where(upper, shrink_keep, shrink_got)]
    )

    grad_hidden = sum(dot_nt(cot[:, col[k] : col[k + 1]], shrink_parts[k]) for k in range(3))
    grad_second = 0.0
    grad_expand_parts = []
    for k in range(3):
        d_hid = grad_hidden[:, edge[k] : edge[k + 1]]
        sig = jax.nn.sigmoid(gate[k])
        d_gate = (d_hid * up[k] * sig * (1.0 + gate[k] * (1.0 - sig))).astype(BF)
        d_up = (d_hid * gate[k] * sig).astype(BF)
        both = jnp.concatenate([d_gate, d_up], axis=1)
        weight_pair = jnp.concatenate([gate_full[k], up_full[k]], axis=1)
        grad_second = grad_second + dot_nt(both, weight_pair)
        grad_expand_parts.append(
            reduce_matrix(dot_tn(second, both).astype(BF), cube.orders[k])
        )
    grad_expand = jnp.concatenate(
        [grad_expand_parts[k][:, : edge[k + 1] - edge[k]] for k in range(3)]
        + [grad_expand_parts[k][:, edge[k + 1] - edge[k] :] for k in range(3)],
        axis=1,
    )

    def normalize_back(values, inverse, gain_row, grad_out):
        scaled = grad_out * gain_row
        grad_in = inverse * scaled - values * inverse * inverse * inverse * jnp.mean(
            scaled * values, axis=-1, keepdims=True
        )
        return (grad_in, jnp.sum(grad_out * values * inverse, axis=0))

    grad_mid_norm, grad_gain_two = normalize_back(middle, inv_two, gains_all[1], grad_second)
    grad_middle = cot.astype(F32) + grad_mid_norm
    grad_branch = (grad_middle * live).astype(BF)
    grad_context = dot_nt(grad_branch, output_full).astype(BF)

    g_h = heads(grad_context)
    grad_attention = jnp.einsum("fphd,fkhd->fhpk", g_h, v_h, preferred_element_type=F32)
    grad_value = jnp.einsum("fhpk,fphd->fkhd", attention_low, g_h, preferred_element_type=F32)
    grad_scores = attention * (
        grad_attention - jnp.sum(grad_attention * attention, axis=-1, keepdims=True)
    )
    grad_scores = grad_scores.astype(BF)
    grad_query = (
        jnp.einsum("fhpk,fkhd->fphd", grad_scores, k_h, preferred_element_type=F32) * scale
    )
    grad_key = jnp.einsum("fhpk,fphd->fkhd", grad_scores, q_h, preferred_element_type=F32) * scale
    give = jnp.concatenate(
        [grad_key[:, :run].reshape(rows, width), grad_value[:, :run].reshape(rows, width)], axis=1
    ).astype(BF)
    got = cube.swap(give, cube.top).astype(F32)
    got = jnp.where(upper, 0.0, got)
    d_query = grad_query.reshape(rows, width).astype(BF)
    d_key = (grad_key[:, run:].reshape(rows, width) + got[:, :width]).astype(BF)
    d_value = (grad_value[:, run:].reshape(rows, width) + got[:, width:]).astype(BF)

    grad_output = reduce_matrix(dot_tn(context, grad_branch).astype(BF), cube.orders[0])
    joint_grads = [
        reduce_matrix(dot_tn(first, d).astype(BF), cube.orders[k])
        for k, d in enumerate((d_query, d_key, d_value))
    ]
    grad_joint = jnp.concatenate(joint_grads, axis=1)
    grad_first = sum(
        dot_nt(d, w) for d, w in zip((d_query, d_key, d_value), joint_parts)
    )
    grad_in_norm, grad_gain_one = normalize_back(x_rows, inv_one, gains_all[0], grad_first)
    grad_inputs = from_sets((grad_middle + grad_in_norm).astype(BF))

    gains_term = jnp.stack([grad_gain_one, grad_gain_two]).reshape((2,) + (2,) * cube.bits + (-1,))
    bits = list(range(cube.bits))
    have = list(bits)
    for b in bits:
        axis = 1 + sum(1 for h in have if h > b)
        mine = cube.bit(b)
        send = lax.dynamic_index_in_dim(gains_term, 1 - mine, axis, keepdims=False)
        keep = lax.dynamic_index_in_dim(gains_term, mine, axis, keepdims=False)
        gains_term = keep + cube.swap(send, b)
        have.remove(b)
    grad_gains = gains_term

    reduced = (grad_joint, grad_output, grad_expand, grad_shrink, grad_gains)
    local_sq = sum(jnp.sum(g * g) for g in reduced)
    total_sq = cube.total(jnp.broadcast_to(local_sq, (8, 128)))[0, 0]
    grad_norm_value = jnp.sqrt(total_sq)
    factor = CLIP_LIMIT / jnp.maximum(grad_norm_value, CLIP_LIMIT)
    joint_new = adam_step(
        joint_weight, factor * reduced[0], joint_mean, joint_square, MATRIX_RATE, MATRIX_DECAY
    )
    output_new = adam_step(
        output_weight, factor * reduced[1], output_mean, output_square, MATRIX_RATE, MATRIX_DECAY
    )
    expand_new = adam_step(
        expand_weight, factor * reduced[2], expand_mean, expand_square, MATRIX_RATE, MATRIX_DECAY
    )
    shrink_new = adam_step(
        shrink_weight, factor * reduced[3], shrink_mean, shrink_square, MATRIX_RATE, MATRIX_DECAY
    )
    gains_new = adam_step(norm_gains, factor * reduced[4], gains_mean, gains_square, GAIN_RATE, 0.0)
    return (
        result,
        grad_inputs,
        grad_norm_value,
        *joint_new,
        *output_new,
        *expand_new,
        *shrink_new,
        *gains_new,
    )


CHIPS = 8
CHAIN_BITS = [[(k + t) % 3 for t in range(3)] for k in range(3)]
CHAIN_MASKS = [
    [sum(((j >> t) & 1) << bits[t] for t in range(3)) for j in range(CHIPS)] for bits in CHAIN_BITS
]
VM = pl.BlockSpec(memory_space=pltpu.VMEM)
HB = pl.BlockSpec(memory_space=pltpu.HBM)
SM = pl.BlockSpec(memory_space=pltpu.SMEM)
MIB = 1 << 20
SMALL = pl.CostEstimate(flops=1, bytes_accessed=1, transcendentals=0)


def aligned(index, size):
    return pl.ds(pl.multiple_of(index * size, size), size)


def after(value, *earlier):
    return lax.optimization_barrier((value, earlier))[0]


def plus(a, b):
    return (a.astype(F32) + b.astype(F32)).astype(BF)


class Jobs:
    def __init__(self, width):
        self.width = width
        self.inputs, self.outputs, self.work = [], [], []

    def source(self, array):
        for i, known in enumerate(self.inputs):
            if known is array:
                return i
        self.inputs.append(array)
        return len(self.inputs) - 1

    def output(self, rows, dtype=BF):
        self.outputs.append(jax.ShapeDtypeStruct((rows, self.width), dtype))
        return len(self.outputs) - 1

    def copy(self, array, row, target, target_row, count):
        self.work.append((self.source(array), row, None, 0, target, target_row, count))

    def add(self, a, a_row, b, b_row, target, target_row, count):
        self.work.append((self.source(a), a_row, self.source(b), b_row, target, target_row, count))

    def run(self, meta, name, *earlier, squares=False):
        inputs = after(self.inputs, *earlier) if earlier else self.inputs
        adds = [w for w in self.work if w[2] is not None]
        rows = sum(w[6] for w in adds)
        moved = sum(w[6] for w in self.work if w[2] is None)
        scratch = [pltpu.SemaphoreType.DMA((3, len(self.work)))]
        scratch += [pltpu.VMEM((max(moved, 16), self.width), BF)]
        if adds:
            scratch += [pltpu.VMEM((rows, self.width), BF)] * 3
            scratch += [pltpu.VMEM((rows, self.width), F32)]
        shapes = list(self.outputs)
        if squares:
            shapes.append(jax.ShapeDtypeStruct((8, self.width), F32))
        return pl.pallas_call(
            functools.partial(jobs_kernel, self.work, len(inputs), self.outputs, squares),
            in_specs=[SM] + [HB] * len(inputs),
            out_specs=[HB] * len(self.outputs) + ([VM] if squares else []),
            out_shape=shapes,
            scratch_shapes=scratch,
            compiler_params=pltpu.CompilerParams(vmem_limit_bytes=60 * MIB),
            cost_estimate=SMALL,
            name=name,
        )(meta, *inputs)


def jobs_kernel(work, count, outputs, squares, meta, *refs):
    sources, targets = refs[:count], refs[count : count + len(outputs)]
    refs = refs[count + len(outputs) :]
    if squares:
        square_ref = refs[0]
        refs = refs[1:]
    sem = refs[0]
    core = meta[1]

    def part(ref, row, rows):
        if isinstance(row, tuple):
            start = pl.multiple_of(jnp.where(core == 0, row[0], row[1]), 16)
            return ref.at[pl.ds(start, rows)]
        return ref.at[row : row + rows]

    coming, leaving = [], []
    at, moved = 0, 0
    transit = refs[1]
    refs = refs[:1] + refs[2:]
    for i, (a, a_row, b, b_row, target, target_row, rows) in enumerate(work):
        if b is None:
            spot = slice(moved, moved + rows)
            copy = pltpu.make_async_copy(part(sources[a], a_row, rows), transit.at[spot], sem.at[0, i])
            copy.start()
            coming.append(((copy,), spot))
            moved += rows
            continue
        spot = slice(at, at + rows)
        pair = (
            pltpu.make_async_copy(part(sources[a], a_row, rows), refs[1].at[spot], sem.at[0, i]),
            pltpu.make_async_copy(part(sources[b], b_row, rows), refs[2].at[spot], sem.at[1, i]),
        )
        for copy in pair:
            copy.start()
        coming.append((pair, spot))
        at += rows
    if squares:
        square_ref[...] = jnp.zeros_like(square_ref)
    for i, (a, a_row, b, b_row, target, target_row, rows) in enumerate(work):
        pair, spot = coming[i]
        finish(pair)
        if b is None:
            copy = pltpu.make_async_copy(
                transit.at[spot], part(targets[target], target_row, rows), sem.at[2, i]
            )
            copy.start()
            leaving.append(copy)
            continue
        wide = outputs[target].dtype == F32
        store = refs[4] if wide else refs[3]
        if not wide and not squares:
            store[spot] = plus(refs[1][spot], refs[2][spot])
        else:
            total = refs[1][spot].astype(F32) + refs[2][spot].astype(F32)
            store[spot] = total.astype(store.dtype)
            if wide:
                square = (total * total).reshape(rows // 8, 8, total.shape[1])
                square_ref[...] += jnp.sum(square, axis=0)
        copy = pltpu.make_async_copy(
            store.at[spot], part(targets[target], target_row, rows), sem.at[2, i]
        )
        copy.start()
        leaving.append(copy)
    finish(leaving)


class Blocks:
    def __init__(self, own=None, rows=None):
        self.rows = own.shape[0] if rows is None else rows
        self.held = [] if own is None else [(own, 0)]

    def arrived(self, array, row, count):
        for j in range(count):
            self.held.append((array, row + j * self.rows))


def place(jobs, held, rows, target, target_row):
    start = 0
    while start < len(held):
        array, row = held[start]
        stop = start + 1
        while stop < len(held) and held[stop][0] is array and held[stop][1] == row + (stop - start) * rows:
            stop += 1
        jobs.copy(array, row, target, target_row + start * rows, (stop - start) * rows)
        start = stop


class Round:
    def __init__(self, cube, meta, width, name):
        self.cube, self.meta, self.name = cube, meta, name
        self.jobs = Jobs(width)
        self.axis_work = []
        self.core_work = []

    def gather(self, chains, level):
        self.axis_work.append((chains, level))
        return self

    def core(self, chains, others, start, stop):
        self.core_work.append((chains, others, start, stop))
        return self

    def run(self, *earlier, gate=()):
        jobs = self.jobs
        filled = []
        for axis in range(3):
            held = []
            for chains, level in self.axis_work:
                blocks = chains[(axis - level) % 3]
                if blocks is not None:
                    held.append((blocks, blocks.held[: 1 << level]))
            filled.append(held)
        core_held = []
        for chains, others, start, stop in self.core_work:
            for blocks, other in zip(chains, others):
                if blocks is not None:
                    core_held.append((blocks, other, blocks.held[start:stop]))
        direct = not core_held and all(len(h) == 1 and len(h[0][1]) == 1 for h in filled)
        if direct:
            payloads = [h[0][1][0][0] for h in filled]
            if earlier:
                payloads = after(payloads, *earlier)
        else:
            for held in filled:
                if held:
                    target = jobs.output(sum(b.rows * len(h) for b, h in held))
                    row = 0
                    for blocks, part in held:
                        place(jobs, part, blocks.rows, target, row)
                        row += blocks.rows * len(part)
            if core_held:
                target = jobs.output(sum(b.rows * len(h) for b, _, h in core_held))
                row = 0
                for blocks, _, part in core_held:
                    place(jobs, part, blocks.rows, target, row)
                    row += blocks.rows * len(part)
            payloads = jobs.run(self.meta, self.name, *earlier)
            self.packed = payloads
            if gate:
                axes = sum(1 for held in filled if held)
                payloads = after(list(payloads[:axes]), *gate) + list(payloads[axes:])
        got = []
        index = 0
        for axis, held in enumerate(filled):
            if not held:
                continue
            array = self.cube.swap(payloads[index], 1 + axis)
            index += 1
            row = 0
            for blocks, part in held:
                blocks.arrived(array, row, len(part))
                row += blocks.rows * len(part)
            got.append(array)
        self.got = got
        self.core_got = None
        if core_held:
            array = self.cube.swap(payloads[index], 0)
            row = 0
            for blocks, other, part in core_held:
                other.arrived(array, row, len(part))
                row += blocks.rows * len(part)
            self.core_got = array
        self.payloads = payloads
        return self


def operands(*chains):
    arrays, tables = [], []
    for blocks in chains:
        table = []
        for array, row in blocks.held:
            found = [i for i, a in enumerate(arrays) if a is array]
            if not found:
                arrays.append(array)
                found = [len(arrays) - 1]
            table.append((found[0], row))
        tables.append((blocks.rows, table))
    return arrays, tables


class Sums:
    def __init__(self, keep, send, rows, final):
        self.keep, self.send, self.rows, self.count, self.final = keep, send, rows, 4, final


def reduce_round(cube, meta, width, name, work, *earlier, squares=False, gate=()):
    jobs = Jobs(width)
    filled = []
    direct = all(step == 0 for _, step in work) and len(work) == 1
    for axis in range(3):
        parts = []
        for chains, step in work:
            if step < 3:
                chain = chains[(axis - (2 - step)) % 3]
                if chain is not None:
                    parts.append((chain, step))
        filled.append(parts)
    if direct:
        payloads = [parts[0][0].send[0] for parts in filled]
        if earlier:
            payloads = after(payloads, *earlier)
    else:
        layout = []
        for parts in filled:
            if not parts:
                continue
            rows = 0
            target = None
            sizes = []
            for chain, step in parts:
                size = chain.rows * (4 >> step)
                sizes.append((chain, step, rows, size))
                rows += size
            layout.append((jobs.output(rows), sizes))
        kept = {}
        for target, sizes in layout:
            for chain, step, row, size in sizes:
                if step == 0:
                    jobs.copy(chain.send[0], chain.send[1], target, row, size)
                else:
                    got, got_row = chain.got
                    array, keep_row = chain.keep
                    own = jobs.output(size)
                    jobs.add(got, got_row + size, array, keep_row + size, target, row, size)
                    jobs.add(got, got_row, array, keep_row, own, 0, size)
                    kept[own] = chain
        for chains, step in work:
            if step == 3:
                for chain in chains:
                    if chain is not None:
                        chain.final(jobs, chain.got, chain.keep, chain.rows)
        out = jobs.run(meta, name, *earlier, squares=squares)
        for own, chain in kept.items():
            chain.keep = (out[own], 0)
        payloads = [out[target] for target, _ in layout]
        if gate and payloads:
            payloads = after(payloads, *gate)
    got = []
    index = 0
    for axis, parts in enumerate(filled):
        if not parts:
            continue
        array = cube.swap(payloads[index], 1 + axis)
        index += 1
        row = 0
        for chain, step in parts:
            chain.got = (array, row)
            row += chain.rows * (4 >> step)
        got.append(array)
    return (got, out) if not direct else (got, None)


def first_kernel(joint, q, k, v):
    width = q.shape[1]
    q[...] = joint[:, :width].astype(BF)
    k[...] = joint[:, width : 2 * width].astype(BF)
    v[: joint.shape[0]] = joint[:, 2 * width :].astype(BF)


def first_shards(joint):
    rows, width = joint.shape[0], joint.shape[1] // 3
    return pl.pallas_call(
        first_kernel,
        in_specs=[VM],
        out_specs=[VM] * 3,
        out_shape=[jax.ShapeDtypeStruct((r, width), BF) for r in (rows, rows, rows + 16)],
        compiler_params=pltpu.CompilerParams(vmem_limit_bytes=60 * MIB),
        name="first_shards",
    )(joint)


def split_kernel(meta, expand, shrink, output, own, give, shrink_own, shrink_give, out_a, out_b):
    core, group = meta[1], meta[2]
    rows = expand.shape[0]
    block = expand.shape[1] // (2 * 2 * 2 * CHIPS)
    for turn in range(2):
        part = turn ^ (1 - group)
        for kind in range(2):
            for chip in range(CHIPS):
                base = ((kind * 2 + part) * CHIPS + chip) * 2
                cols = slice(chip * block, (chip + 1) * block)
                r = slice((turn * 2 + kind) * rows, (turn * 2 + kind + 1) * rows)
                own[r, cols] = expand[:, aligned(base + core, block)].astype(BF)
                give[r, cols] = expand[:, aligned(base + 1 - core, block)].astype(BF)
    shrink_own[...] = shrink[group].astype(BF)
    shrink_give[...] = shrink[1 - group].astype(BF)
    out_a[...] = output[: rows // 2].astype(BF)
    out_b[...] = output[rows // 2 :].astype(BF)


def split_weights(meta, expand, shrink, output):
    rows, width = output.shape
    four = jax.ShapeDtypeStruct((4 * rows, width), BF)
    two = jax.ShapeDtypeStruct(shrink.shape[1:], BF)
    half = jax.ShapeDtypeStruct((rows // 2, width), BF)
    return pl.pallas_call(
        split_kernel,
        in_specs=[SM, VM, VM, VM],
        out_specs=[VM] * 6,
        out_shape=[four, four, two, two, half, half],
        compiler_params=pltpu.CompilerParams(vmem_limit_bytes=60 * MIB),
        name="split_weights",
    )(meta, expand, shrink, output)


def load_blocks(table, refs, w, k, chip, sem):
    copies = []
    rows, places = table
    for j, (index, row) in enumerate(places):
        target = w.at[aligned(chip ^ CHAIN_MASKS[k][j], rows), :]
        copy = pltpu.make_async_copy(refs[index].at[row : row + rows], target, sem.at[j])
        copy.start()
        copies.append(copy)
    return copies


def store_blocks(w, pieces, rows, k, chip, sem):
    copies = []
    for j in range(CHIPS):
        source = w.at[aligned(chip ^ CHAIN_MASKS[k][j], rows), :]
        row = (j % 4) * rows
        copy = pltpu.make_async_copy(source, pieces[j // 4].at[row : row + rows], sem.at[j])
        copy.start()
        copies.append(copy)
    return copies


def finish(copies):
    for copy in copies:
        copy.wait()


TILE = 256


def ffn_rows_kernel(first, count, tables, meta, n2m, n2o, cm, co, *refs):
    pieces = refs[:count]
    refs = refs[count:]
    if not first:
        dn_in = refs[0]
        refs = refs[1:]
    if first:
        dn_out, hid, dg, du, n2, c, wg, wu, ws, sem = refs
    else:
        dn_out, dn_send, hid, dg, du, n2, c, wg, wu, ws, sem = refs
    chip = meta[0]
    mats = (wg, wu, ws)
    coming = [load_blocks(tables[k], pieces, mats[k], k, chip, sem.at[k]) for k in range(3)]
    rows = n2m.shape[0]
    n2[:rows] = n2m[...]
    n2[rows:] = n2o[...]
    c[:rows] = cm[...]
    c[rows:] = co[...]
    for copies in coming:
        finish(copies)
    width = wg.shape[1]

    def gates(t, _):
        cols = aligned(t, TILE)
        g = dot(n2[...], wg[:, cols])
        u = dot(n2[...], wu[:, cols])
        dh = dot_nt(c[...], ws[cols, :])
        sig = jax.nn.sigmoid(g)
        silu = g * sig
        hid[:, cols] = (silu * u).astype(BF)
        du[:, cols] = (dh * silu).astype(BF)
        dg[:, cols] = (dh * u * sig * (1.0 + g * (1.0 - sig))).astype(BF)
        return 0

    lax.fori_loop(0, width // TILE, gates, 0)

    def back(t, _):
        cols = aligned(t, TILE)
        d = dot_nt(dg[...], wg[cols, :]) + dot_nt(du[...], wu[cols, :])
        if first:
            dn_out[:, cols] = d
        else:
            d = d + dn_in[:, cols]
            dn_out[:, cols] = d[:rows]
            dn_send[:, cols] = d[rows:]
        return 0

    lax.fori_loop(0, width // TILE, back, 0)


def ffn_rows(meta, n2m, n2o, cm, co, chains, carried):
    first = carried is None
    arrays, tables = operands(*chains)
    rows, width = 2 * n2m.shape[0], n2m.shape[1]
    low = jax.ShapeDtypeStruct((rows, width), BF)
    return pl.pallas_call(
        functools.partial(ffn_rows_kernel, first, len(arrays), tables),
        in_specs=[SM] + [VM] * 4 + [HB] * len(arrays) + ([] if first else [VM]),
        out_specs=[VM] * (4 if first else 5),
        out_shape=(
            [jax.ShapeDtypeStruct((rows, width), F32)]
            if first
            else [jax.ShapeDtypeStruct((rows // 2, width), F32)] * 2
        )
        + [low, low, low],
        scratch_shapes=[pltpu.VMEM((rows, width), BF)] * 2
        + [pltpu.VMEM((width, width), BF)] * 3
        + [pltpu.SemaphoreType.DMA((3, CHIPS))],
        compiler_params=pltpu.CompilerParams(vmem_limit_bytes=60 * MIB),
        cost_estimate=SMALL,
        name="ffn_rows",
    )(meta, n2m, n2o, cm, co, *arrays, *(() if first else (carried,)))


def ffn_weights_kernel(first, count, table, meta, n2m, n2o, cm, co, hid, dg, du, *refs):
    pieces = refs[:count]
    refs = refs[count:]
    if not first:
        f_in = refs[0]
        refs = refs[1:]
    f_out = refs[0]
    if not first:
        f_send = refs[1]
        refs = refs[1:]
    outs = refs[1:7]
    n2, c, ws, dwg, dwu, dws, in_sem, out_sem = refs[7:]
    chip = meta[0]
    coming = load_blocks(table, pieces, ws, 2, chip, in_sem)
    rows = n2m.shape[0]
    n2[:rows] = n2m[...]
    n2[rows:] = n2o[...]
    c[:rows] = cm[...]
    c[rows:] = co[...]
    width = ws.shape[1]
    leaving = []
    for k, (lhs, rhs, dw) in enumerate(((n2, dg, dwg), (n2, du, dwu), (hid, c, dws))):

        def step(t, _, lhs=lhs, rhs=rhs, dw=dw):
            cols = aligned(t, TILE)
            dw[cols, :] = dot_tn(lhs[:, cols], rhs[...]).astype(BF)
            return 0

        lax.fori_loop(0, width // TILE, step, 0)
        leaving += store_blocks(dw, outs[2 * k : 2 * k + 2], table[0], k, chip, out_sem.at[k])
    finish(coming)

    def down(t, _):
        cols = aligned(t, TILE)
        f = dot(hid[...], ws[:, cols])
        if first:
            f_out[:, cols] = f
        else:
            f = f + f_in[:, cols]
            f_out[:, cols] = f[:rows]
            f_send[:, cols] = f[rows:].astype(BF)
        return 0

    lax.fori_loop(0, width // TILE, down, 0)
    finish(leaving)


def ffn_weights(meta, n2m, n2o, cm, co, hid, dg, du, chain, carried):
    first = carried is None
    arrays, tables = operands(chain)
    rows, width = 2 * n2m.shape[0], n2m.shape[1]
    piece = jax.ShapeDtypeStruct((4 * chain.rows, width), BF)
    return pl.pallas_call(
        functools.partial(ffn_weights_kernel, first, len(arrays), tables[0]),
        in_specs=[SM] + [VM] * 7 + [HB] * len(arrays) + ([] if first else [VM]),
        out_specs=[VM] * (1 if first else 2) + [HB] * 6,
        out_shape=(
            [jax.ShapeDtypeStruct((rows, width), F32)]
            if first
            else [
                jax.ShapeDtypeStruct((rows // 2, width), F32),
                jax.ShapeDtypeStruct((rows // 2, width), BF),
            ]
        )
        + [piece] * 6,
        scratch_shapes=[pltpu.VMEM((rows, width), BF)] * 2
        + [pltpu.VMEM((width, width), BF)] * 4
        + [pltpu.SemaphoreType.DMA((CHIPS,)), pltpu.SemaphoreType.DMA((3, CHIPS))],
        compiler_params=pltpu.CompilerParams(vmem_limit_bytes=60 * MIB),
        cost_estimate=SMALL,
        name="ffn_weights",
    )(meta, n2m, n2o, cm, co, hid, dg, du, *arrays, *(() if first else (carried,)))


OUTPUT_CHAINS = (1, 2)


def load_devices(table, refs, k, side, shard, row, count, target, lo, meta, sem, used):
    chip, core = meta[0], meta[1]
    copies = []
    for j, (index, base) in enumerate(table[1]):
        device = (chip ^ CHAIN_MASKS[k][j]) * 2 + (core if side == 0 else 1 - core)
        start = pl.multiple_of(device * shard + row, 16)
        copy = pltpu.make_async_copy(
            refs[index].at[base : base + count],
            target.at[pl.ds(start, count), lo : lo + target.shape[0]],
            sem.at[used + j],
        )
        copy.start()
        copies.append(copy)
    return copies


def load_joint(tables, refs, target, meta, sem):
    width = target.shape[0]
    shard = width // (2 * CHIPS)
    copies = []
    for k in range(3):
        for side in range(2):
            copies += load_devices(
                tables[3 * side + k], refs, k, side, shard, 0, shard, target, k * width, meta, sem, len(copies)
            )
    return copies


def load_output(tables, refs, target, meta, sem):
    shard = target.shape[0] // (2 * CHIPS)
    half = shard // 2
    copies = []
    for i, k in enumerate(OUTPUT_CHAINS):
        for side in range(2):
            copies += load_devices(
                tables[2 * side + i], refs, k, side, shard, i * half, half, target, 0, meta, sem, len(copies)
            )
    return copies


PAIR_COPIES = 128


def joint_kernel(count, tables, meta, x, *refs):
    pieces = refs[:count]
    first, query, key, value_out, gains, w, gain_rows, sem, gain_sem = refs[count:]
    width = x.shape[1]
    coming = load_joint(tables, pieces, w, meta, sem)
    shard = width // (2 * CHIPS)
    gain_copies = []
    for side in range(2):
        for j, (index, base) in enumerate(tables[3 * side + 2][1]):
            copy = pltpu.make_async_copy(
                pieces[index].at[base + shard : base + shard + 16],
                gain_rows.at[side * CHIPS + j],
                gain_sem.at[side * CHIPS + j],
            )
            copy.start()
            gain_copies.append(copy)
    value = x[...].astype(F32)
    inverse = lax.rsqrt(jnp.mean(value * value, axis=-1, keepdims=True) + NORM_EPS)
    finish(gain_copies)
    whole = jnp.sum(gain_rows[...].astype(F32), axis=0)
    gains[...] = whole[:8]
    first[...] = (value * inverse * whole[0:1]).astype(BF)
    finish(coming)
    tiles = width // TILE
    for part, out in enumerate((query, key, value_out)):

        def step(t, _, part=part, out=out):
            weight = w[:, aligned(t + part * tiles, TILE)]
            out[:, aligned(t, TILE)] = dot(first[...], weight).astype(BF)
            return 0

        lax.fori_loop(0, tiles, step, 0)


def joint_forward(meta, x, chains):
    rows, width = x.shape
    arrays, tables = operands(*chains)
    low = jax.ShapeDtypeStruct((rows, width), BF)
    return pl.pallas_call(
        functools.partial(joint_kernel, len(arrays), tables),
        in_specs=[SM, VM] + [HB] * len(arrays),
        out_specs=[VM] * 5,
        out_shape=[
            low,
            low,
            low,
            low,
            jax.ShapeDtypeStruct((8, width), F32),
        ],
        scratch_shapes=[
            pltpu.VMEM((width, 3 * width), BF),
            pltpu.VMEM((2 * CHIPS, 16, width), BF),
            pltpu.SemaphoreType.DMA((PAIR_COPIES,)),
            pltpu.SemaphoreType.DMA((2 * CHIPS,)),
        ],
        compiler_params=pltpu.CompilerParams(vmem_limit_bytes=60 * MIB),
        cost_estimate=SMALL,
        name="joint_forward",
    )(meta, x, *arrays)


CHUNK = 128


def bias_into(bias, run, upper):
    size = 2 * CHUNK
    row = lax.broadcasted_iota(jnp.int32, (size, size), 0) & (CHUNK - 1)
    column = lax.broadcasted_iota(jnp.int32, (size, size), 1)
    own = column < CHUNK
    column = column & (CHUNK - 1)
    shift = run.bit_length() - 1
    same = (row >> shift) == (column >> shift)
    reach = jnp.where(upper, CHUNK, 0)
    seen = same & ((own & (row >= column)) | (~own & (row < reach)))
    bias[...] = jnp.where(seen, 0.0, -1e30)


def stacked(value, left):
    zero = jnp.zeros_like(value)
    return jnp.concatenate([jnp.where(left, value, zero), jnp.where(left, zero, value)], axis=0)


def probabilities(q_st, k_all, bias, scale):
    scores = dot_nt(q_st, k_all) * scale + bias[...]
    exp_scores = jnp.exp(scores - jnp.max(scores, axis=-1, keepdims=True))
    return exp_scores / jnp.sum(exp_scores, axis=-1, keepdims=True)


def context_kernel(run, head_dim, count, tables, meta, query, k_own, v_own, k_other, v_other, x, live, gains, *refs):
    pieces = refs[:count]
    ctx, h_out, n2, wo, bias, sem = refs[count:]
    rows, width = x.shape
    coming = load_output(tables, pieces, wo, meta, sem)
    bias_into(bias, run, meta[2] == 1)
    scale = head_dim ** (-0.5)
    lanes = 2 * head_dim
    left = lax.broadcasted_iota(jnp.int32, (CHUNK, lanes), 1) < head_dim

    def pair(p, _):
        cols = aligned(p, lanes)
        for chunk in range(rows // CHUNK):
            r = slice(chunk * CHUNK, (chunk + 1) * CHUNK)
            q_st = stacked(query[r, cols], left)
            k_all = jnp.concatenate([k_own[r, cols], k_other[r, cols]], axis=0)
            v_all = jnp.concatenate([v_own[r, cols], v_other[r, cols]], axis=0)
            prob = probabilities(q_st, k_all, bias, scale)
            out = dot(prob.astype(BF), v_all)
            ctx[r, cols] = jnp.where(left, out[:CHUNK], out[CHUNK:]).astype(BF)
        return 0

    lax.fori_loop(0, width // lanes, pair, 0)
    finish(coming)

    def project(t, _):
        cols = aligned(t, TILE)
        h_out[:, cols] = x[:, cols].astype(F32) + live[...] * dot(ctx[...], wo[:, cols])
        return 0

    lax.fori_loop(0, width // TILE, project, 0)
    h = h_out[...]
    inverse = lax.rsqrt(jnp.mean(h * h, axis=-1, keepdims=True) + NORM_EPS)
    n2[...] = (h * inverse * gains[1:2, :]).astype(BF)


def context_forward(
    run, meta, query, k_own, v_own, k_other, v_other, x, live, gains, chains
):
    rows, width = x.shape
    arrays, tables = operands(*chains)
    low = jax.ShapeDtypeStruct((rows, width), BF)
    return pl.pallas_call(
        functools.partial(context_kernel, run, width // HEADS, len(arrays), tables),
        in_specs=[SM] + [VM] * 8 + [HB] * len(arrays),
        out_specs=[VM] * 3,
        out_shape=[low, jax.ShapeDtypeStruct((rows, width), F32), low],
        scratch_shapes=[
            pltpu.VMEM((width, width), BF),
            pltpu.VMEM((2 * CHUNK, 2 * CHUNK), F32),
            pltpu.SemaphoreType.DMA((PAIR_COPIES,)),
        ],
        compiler_params=pltpu.CompilerParams(vmem_limit_bytes=60 * MIB),
        cost_estimate=SMALL,
        name="context_forward",
    )(meta, query, k_own, v_own, k_other, v_other, x, live, gains, *arrays)


def norm_back(value, gain, grad):
    inverse = lax.rsqrt(jnp.mean(value * value, axis=-1, keepdims=True) + NORM_EPS)
    scaled = grad * gain
    mean = jnp.mean(scaled * value, axis=-1, keepdims=True)
    grad_in = inverse * scaled - value * (inverse * inverse * inverse) * mean
    return grad_in, jnp.sum(grad * value * inverse, axis=0, keepdims=True)


def context_back_kernel(
    run, head_dim, count, tables, meta, dn_own, dn_got, h, cot, live, gains, query, *refs
):
    k_own, v_own, k_other, v_other = refs[:4]
    pieces = refs[4 : 4 + count]
    dh, dg2, da, dq, dkv, k_give, v_give, wo, bias, dctx, sem = refs[4 + count :]
    rows, width = h.shape
    coming = load_output(tables, pieces, wo, meta, sem)
    bias_into(bias, run, meta[2] == 1)
    grad_in, dg2[...] = norm_back(h[...], gains[1:2, :], dn_own[...] + dn_got[...])
    grad = cot[...].astype(F32) + grad_in
    dh[...] = grad
    da[...] = (grad * live[...]).astype(BF)
    finish(coming)

    def project(t, _):
        cols = aligned(t, TILE)
        dctx[:, cols] = dot_nt(da[...], wo[cols, :]).astype(BF)
        return 0

    lax.fori_loop(0, width // TILE, project, 0)
    scale = head_dim ** (-0.5)
    lanes = 2 * head_dim
    pairs = width // lanes
    left = lax.broadcasted_iota(jnp.int32, (CHUNK, lanes), 1) < head_dim

    def pair(p, _):
        cols = aligned(p, lanes)
        v_cols = aligned(p + pairs, lanes)
        for chunk in range(rows // CHUNK):
            r = slice(chunk * CHUNK, (chunk + 1) * CHUNK)
            q_st = stacked(query[r, cols], left)
            g_st = stacked(dctx[r, cols], left)
            k_all = jnp.concatenate([k_own[r, cols], k_other[r, cols]], axis=0)
            v_all = jnp.concatenate([v_own[r, cols], v_other[r, cols]], axis=0)
            prob = probabilities(q_st, k_all, bias, scale)
            d_prob = dot_nt(g_st, v_all)
            d_score = prob * (d_prob - jnp.sum(d_prob * prob, axis=-1, keepdims=True))
            d_score = d_score.astype(BF)
            d_query = dot(d_score, k_all) * scale
            d_key = dot_tn(d_score, q_st) * scale
            d_value = dot_tn(prob.astype(BF), g_st)
            dq[r, cols] = jnp.where(left, d_query[:CHUNK], d_query[CHUNK:]).astype(BF)
            dkv[r, cols] = d_key[:CHUNK]
            dkv[r, v_cols] = d_value[:CHUNK]
            k_give[r, cols] = d_key[CHUNK:].astype(BF)
            v_give[r, cols] = d_value[CHUNK:].astype(BF)
        return 0

    lax.fori_loop(0, pairs, pair, 0)


def context_back(
    run, meta, dn_own, dn_got, h, cot, live, gains, query, k_own, v_own, k_other, v_other, chains
):
    rows, width = h.shape
    arrays, tables = operands(*chains)
    low = jax.ShapeDtypeStruct((rows, width), BF)
    return pl.pallas_call(
        functools.partial(context_back_kernel, run, width // HEADS, len(arrays), tables),
        in_specs=[SM] + [VM] * 11 + [HB] * len(arrays),
        out_specs=[VM] * 7,
        out_shape=[
            jax.ShapeDtypeStruct((rows, width), F32),
            jax.ShapeDtypeStruct((1, width), F32),
            low,
            low,
            jax.ShapeDtypeStruct((rows, 2 * width), F32),
            low,
            low,
        ],
        scratch_shapes=[
            pltpu.VMEM((width, width), BF),
            pltpu.VMEM((2 * CHUNK, 2 * CHUNK), F32),
            pltpu.VMEM((rows, width), BF),
            pltpu.SemaphoreType.DMA((PAIR_COPIES,)),
        ],
        compiler_params=pltpu.CompilerParams(vmem_limit_bytes=60 * MIB),
        cost_estimate=SMALL,
        name="context_back",
    )(
        meta,
        dn_own,
        dn_got,
        h,
        cot,
        live,
        gains,
        query,
        k_own,
        v_own,
        k_other,
        v_other,
        *arrays,
    )


def shard_grads(lhs, rhs_cols, dw):
    width = lhs.shape[1]
    for i, rhs in enumerate(rhs_cols):

        def step(t, _, rhs=rhs, i=i):
            cols = aligned(t, TILE)
            dw[i, cols, :] = dot_tn(lhs[:, cols], rhs()).astype(BF)
            return 0

        lax.fori_loop(0, width // TILE, step, 0)


def store_devices(dw, matrix, row, count, k, targets, base, meta, sem, used):
    chip, core = meta[0], meta[1]
    shard = dw.shape[1] // (2 * CHIPS)
    copies = []
    for side, target in enumerate(targets):
        for j in range(CHIPS):
            device = (chip ^ CHAIN_MASKS[k][j]) * 2 + (1 - core if side == 0 else core)
            start = pl.multiple_of(device * shard + row, 16)
            low = base + j * count
            copy = pltpu.make_async_copy(
                dw.at[matrix, pl.ds(start, count), :],
                target.at[low : low + count],
                sem.at[used + len(copies)],
            )
            copy.start()
            copies.append(copy)
    return copies


def output_grad_kernel(meta, context, grad, give, keep, dw, sem):
    shard_grads(context, (lambda: grad[...],), dw)
    half = dw.shape[1] // (4 * CHIPS)
    leaving = []
    for i, k in enumerate(OUTPUT_CHAINS):
        base = i * CHIPS * half
        leaving += store_devices(
            dw, 0, i * half, half, k, (give, keep), base, meta, sem, len(leaving)
        )
    finish(leaving)


def output_grad(meta, context, grad):
    rows, width = context.shape
    part = jax.ShapeDtypeStruct((width // 2, width), BF)
    return pl.pallas_call(
        output_grad_kernel,
        in_specs=[SM, VM, VM],
        out_specs=[HB, HB],
        out_shape=[part, part],
        scratch_shapes=[
            pltpu.VMEM((1, width, width), BF),
            pltpu.SemaphoreType.DMA((PAIR_COPIES,)),
        ],
        compiler_params=pltpu.CompilerParams(vmem_limit_bytes=60 * MIB),
        cost_estimate=SMALL,
        name="output_grad",
    )(meta, context, grad)


def joint_grad_kernel(meta, first, dq, dkv_own, dk_got, dv_got, give, keep, dkv, dw, sem):
    width = first.shape[1]
    for part, got in enumerate((dk_got, dv_got)):
        cols = slice(part * width, (part + 1) * width)
        more = jnp.where(meta[2] == 1, 0.0, got[...].astype(F32))
        dkv[:, cols] = (dkv_own[:, cols] + more).astype(BF)
    rights = (lambda: dq[...], lambda: dkv[:, :width], lambda: dkv[:, width:])
    shard = width // (2 * CHIPS)
    leaving = []
    for k in range(3):

        def step(t, _, k=k):
            cols = aligned(t, TILE)
            dw[k, cols, :] = dot_tn(first[:, cols], rights[k]()).astype(BF)
            return 0

        lax.fori_loop(0, width // TILE, step, 0)
        leaving += store_devices(
            dw, k, 0, shard, k, (give, keep), k * CHIPS * shard, meta, sem, len(leaving)
        )
    finish(leaving)


def joint_grad(meta, first, dq, dkv_own, dk_got, dv_got):
    rows, width = first.shape
    part = jax.ShapeDtypeStruct((3 * width // 2, width), BF)
    return pl.pallas_call(
        joint_grad_kernel,
        in_specs=[SM] + [VM] * 5,
        out_specs=[HB, HB, VM],
        out_shape=[part, part, jax.ShapeDtypeStruct((rows, 2 * width), BF)],
        scratch_shapes=[
            pltpu.VMEM((3, width, width), BF),
            pltpu.SemaphoreType.DMA((PAIR_COPIES,)),
        ],
        compiler_params=pltpu.CompilerParams(vmem_limit_bytes=60 * MIB),
        cost_estimate=SMALL,
        name="joint_grad",
    )(meta, first, dq, dkv_own, dk_got, dv_got)


def input_back_kernel(count, tables, meta, dq, dkv, dh, x, gains, *refs):
    pieces = refs[:count]
    out, dg1, w, dn, sem = refs[count:]
    rows, width = x.shape
    finish(load_joint(tables, pieces, w, meta, sem))

    def step(t, _):
        cols = aligned(t, TILE)
        dn[:, cols] = dot_nt(dq[...], w[cols, :width]) + dot_nt(dkv[...], w[cols, width:])
        return 0

    lax.fori_loop(0, width // TILE, step, 0)
    grad_in, dg1[...] = norm_back(x[...].astype(F32), gains[0:1, :], dn[...])
    out[...] = (dh[...] + grad_in).astype(BF)


def input_back(meta, dq, dkv, dh, x, gains, chains):
    rows, width = x.shape
    arrays, tables = operands(*chains)
    return pl.pallas_call(
        functools.partial(input_back_kernel, len(arrays), tables),
        in_specs=[SM] + [VM] * 5 + [HB] * len(arrays),
        out_specs=[VM, VM],
        out_shape=[
            jax.ShapeDtypeStruct((rows, width), BF),
            jax.ShapeDtypeStruct((1, width), F32),
        ],
        scratch_shapes=[
            pltpu.VMEM((width, 3 * width), BF),
            pltpu.VMEM((rows, width), F32),
            pltpu.SemaphoreType.DMA((PAIR_COPIES,)),
        ],
        compiler_params=pltpu.CompilerParams(vmem_limit_bytes=60 * MIB),
        cost_estimate=SMALL,
        name="input_back",
    )(meta, dq, dkv, dh, x, gains, *arrays)


def adam_expand_kernel(meta, factor, w, m, v, own_a, own_b, got_a, got_b, w_out, m_out, v_out):
    core, group = meta[1], meta[2]
    block = w.shape[1] // (2 * CHIPS)
    k = factor[0]
    turn = (pl.program_id(0) % 2) ^ (1 - group)
    for q in range(2 * CHIPS):
        cols = slice(q * block, (q + 1) * block)
        near = slice((q // 2) * block, (q // 2 + 1) * block)
        own = jnp.where(turn == 0, own_a[:, near], own_b[:, near])
        got = jnp.where(turn == 0, got_a[:, near], got_b[:, near])
        grad = jnp.where(core == q % 2, own, got)
        w_new, m_new, v_new = adam_step(
            w[:, cols], k * grad, m[:, cols], v[:, cols], MATRIX_RATE, MATRIX_DECAY
        )
        w_out[:, cols] = w_new
        m_out[:, cols] = m_new
        v_out[:, cols] = v_new


def adam_expand(meta, factor, w, m, v, own, got):
    rows, width = w.shape
    wide = pl.BlockSpec((rows, width // 4), lambda i: (0, i))
    grad = pl.BlockSpec((rows, width // 8), lambda i: (i // 2, 0))
    return pl.pallas_call(
        adam_expand_kernel,
        grid=(4,),
        in_specs=[SM, SM, wide, wide, wide] + [grad] * 4,
        out_specs=[wide, wide, wide],
        out_shape=[jax.ShapeDtypeStruct(w.shape, F32)] * 3,
        compiler_params=pltpu.CompilerParams(vmem_limit_bytes=60 * MIB),
        name="adam_expand",
    )(meta, factor, w, m, v, *own, *got)


def local_cube(
    count,
    tokens,
    depth_count,
    cotangent,
    joint_weight,
    output_weight,
    expand_weight,
    shrink_weight,
    norm_gains,
    joint_mean,
    joint_square,
    output_mean,
    output_square,
    expand_mean,
    expand_square,
    shrink_mean,
    shrink_square,
    gains_mean,
    gains_square,
):
    cube = Cube(count)
    frames, positions, width = tokens.shape
    run = positions // SETS
    group = cube.bit(cube.top)
    core = cube.bit(0)
    upper = group == 1
    second_core = core == 1
    all_frames = 2 * frames
    rows = all_frames * run
    chip = (cube.index >> 1) & (CHIPS - 1)
    meta = jnp.stack([chip, core, group]).astype(jnp.int32)

    def halves(own, other):
        return jnp.concatenate([jnp.where(upper, other, own), jnp.where(upper, own, other)], axis=0)

    def parted(value):
        first, second = value[:, :run], value[:, run:]
        own, other = jnp.where(upper, second, first), jnp.where(upper, first, second)
        return own.reshape(rows // 2, width), other.reshape(rows // 2, width)

    def from_sets(value):
        value = value.reshape(2, frames, run, width)
        own = jnp.where(upper, value[1], value[0])
        other = cube.swap(jnp.where(upper, value[0], value[1]), cube.top)
        first = jnp.where(upper, other, own)
        second = jnp.where(upper, own, other)
        return jnp.concatenate([first, second], axis=1)

    shard_rows = joint_weight.shape[0]
    lane = norm_gains.shape[1]
    small = jnp.concatenate([norm_gains.astype(BF).reshape(-1), depth_count.astype(BF)])
    small_other = cube.swap(small.reshape(1, -1), cube.top)[0]
    depth_all = halves(small[2 * lane :], small_other[2 * lane :]).astype(jnp.int32)
    gain_pair = halves(small[None, : 2 * lane], small_other[None, : 2 * lane])
    gain_pair = gain_pair.reshape(2, 2, lane).transpose(1, 0, 2)
    spread = jnp.broadcast_to(gain_pair[:, :, None, :], (2, 2, 2 * CHIPS, lane)).reshape(2, width)
    mine = (jnp.arange(width) // lane) % (2 * CHIPS) == (cube.index & (2 * CHIPS - 1))
    gain_rows = jnp.pad(jnp.where(mine[None, :], spread, 0), ((0, 14), (0, 0)))
    shards = list(first_shards(joint_weight))
    shards[2] = lax.dynamic_update_slice(shards[2], gain_rows, (shard_rows, 0))
    joint = [Blocks(shard) for shard in shards]
    x_own, x_give = parted(tokens)
    x_got = cube.swap(x_give, cube.top)
    x_rows = halves(x_own, x_got)

    def begin(name):
        return Round(cube, meta, width, name)

    one = begin("pack_one").gather(joint, 0).run(x_give)
    own_cols, give_cols, shrink_keep, shrink_give, out_a, out_b = split_weights(
        meta, expand_weight, shrink_weight, output_weight
    )
    output = [None, Blocks(out_a), Blocks(out_b)]
    joint_other = [Blocks(rows=blocks.rows) for blocks in joint]
    output_other = [None] + [Blocks(rows=blocks.rows) for blocks in output[1:]]
    two = begin("pack_two").gather(joint, 1).gather(output, 0).run(one.got, give_cols)
    shrink_other = cube.swap(after(shrink_give, two.got, x_got), cube.top)
    got_cols = cube.swap(after(give_cols, two.got, x_got), 0)
    three = begin("pack_three").gather(joint, 2).gather(output, 1)
    three = three.core(joint, joint_other, 0, 4).run(two.got, x_got)
    units = Jobs(width)
    unit_rows = 2 * shard_rows
    for kind in range(2):
        target = units.output(2 * unit_rows)
        for turn_index in range(2):
            unit = turn_index * 2 + kind
            base = turn_index * unit_rows
            low, high = (base, base + shard_rows), (base + shard_rows, base)
            units.copy(own_cols, unit * shard_rows, target, low, shard_rows)
            units.copy(got_cols, unit * shard_rows, target, high, shard_rows)
    target = units.output(2 * unit_rows)
    units.copy(shrink_other, 0, target, 0, unit_rows)
    units.copy(shrink_keep, 0, target, unit_rows, unit_rows)
    units = units.run(meta, "expand_units", three.packed)
    part_a = [Blocks(unit, unit_rows) for unit in units]
    part_b = [Blocks(rows=unit_rows) for unit in units]
    for blocks, unit in zip(part_b, units):
        blocks.arrived(unit, unit_rows, 1)

    cot_own, cot_give = parted(cotangent)
    cot_got = cube.swap(after(cot_give, three.packed, shrink_other), cube.top)
    late = begin("pack_late").core(joint, joint_other, 4, 8).run(three.got, three.core_got, units)
    first_units = after(units, three.got, three.core_got)
    got_four = [cube.swap(unit, 1 + axis) for axis, unit in enumerate(first_units)]
    for k in range(3):
        part_a[k].arrived(got_four[k], 0, 1)
        part_b[k].arrived(got_four[k], unit_rows, 1)

    position = group * run + jnp.arange(run)
    live = (position[None, :] < depth_all[:, None]).astype(F32).reshape(rows, 1)

    first, query, key, value, gains_all = joint_forward(meta, x_rows, joint + joint_other)
    five = begin("pack_five").gather(part_a, 1).gather(part_b, 1).gather(output, 2)
    five = five.run(got_four, key, cot_got)
    key_other = cube.swap(after(key, cot_got), cube.top)
    value_other = cube.swap(after(value, cot_got), cube.top)
    seven = begin("pack_seven").gather(part_a, 2).core(output, output_other, 0, 8)
    seven = seven.run(five.got, key_other, value_other)
    cot_live = (halves(cot_own, after(cot_got, key)).astype(F32) * live).astype(BF)
    cot_other = cube.swap(after(cot_live, five.got, key_other), 0)
    output_chains = output[1:] + output_other[1:]
    context, middle, second = context_forward(
        run,
        meta,
        query,
        key,
        value,
        key_other,
        value_other,
        x_rows,
        live,
        gains_all,
        output_chains,
    )
    eight = begin("pack_eight").gather(part_b, 2).run(
        seven.packed, seven.core_got, cot_other, gate=(seven.got, second)
    )
    second_other = cube.swap(second, 0)
    row_args = (meta, second, second_other, cot_live, cot_other)
    dn_a, *kept_a = ffn_rows(*row_args, part_a, None)
    f_a, *grad_a = ffn_weights(*row_args, *kept_a, part_a[2], None)
    dn_own, dn_send, *kept_b = ffn_rows(*row_args, part_b, after(dn_a, f_a))
    dn_got = cube.swap(dn_send, 0)
    f_own, f_send, *grad_b = ffn_weights(*row_args, *kept_b, part_b[2], f_a)

    outcome = {}

    def expand_final(key, kind):
        def final(jobs, got, keep, count):
            if key not in outcome:
                outcome[key] = (jobs.output(2 * shard_rows, F32), jobs.output(2 * shard_rows, F32))
            own, give = outcome[key]
            half = count // 2
            for target, offset in ((own, (0, half)), (give, (half, 0))):
                got_at = tuple(got[1] + o for o in offset)
                keep_at = tuple(keep[1] + o for o in offset)
                jobs.add(got[0], got_at, keep[0], keep_at, target, kind * shard_rows, half)

        return final

    def plain_final(key):
        def final(jobs, got, keep, count):
            outcome[key] = jobs.output(count, F32)
            jobs.add(got[0], got[1], keep[0], keep[1], outcome[key], 0, count)

        return final

    def ffn_sums(grads, name):
        finals = (expand_final(name, 0), expand_final(name, 1), plain_final(name + "_shrink"))
        block = grads[0].shape[0] // 4
        return [Sums((grads[2 * k], 0), (grads[2 * k + 1], 0), block, finals[k]) for k in range(3)]

    def turn(name, work, *earlier, squares=False, gate=()):
        return reduce_round(cube, meta, width, name, work, *earlier, squares=squares, gate=gate)

    def core_sum(name, give, keep, chains, *earlier):
        got = cube.swap(after(give, *earlier) if earlier else give, 0)
        jobs = Jobs(width)
        row, sums = 0, [None] * 3
        targets = []
        for k, count in chains:
            send, own = jobs.output(4 * count), jobs.output(4 * count)
            jobs.add(got, row + 4 * count, keep, row + 4 * count, send, 0, 4 * count)
            jobs.add(got, row, keep, row, own, 0, 4 * count)
            targets.append((k, count, own, send))
            row += CHIPS * count
        out = jobs.run(meta, name)
        for k, count, own, send in targets:
            sums[k] = Sums((out[own], 0), (out[send], 0), count, plain_final((name, k)))
        return sums

    sums_a = ffn_sums(grad_a, "a")
    sums_b = ffn_sums(grad_b, "b")
    turn_one, _ = turn("turn_one", [(sums_a, 0)], eight.got)
    turn_two, _ = turn("turn_two", [(sums_b, 0)], turn_one)

    grad_middle, grad_gain_two, grad_branch, d_query, dkv_own, k_give, v_give = context_back(
        run,
        meta,
        after(dn_own, f_own, turn_one),
        dn_got,
        middle,
        cot_live,
        live,
        gains_all,
        query,
        key,
        value,
        key_other,
        value_other,
        output_chains,
    )
    turn_three, _ = turn("turn_three", [(sums_a, 1), (sums_b, 1)], turn_two, k_give)
    dk_got = cube.swap(k_give, cube.top)
    dv_got = cube.swap(v_give, cube.top)
    output_give, output_keep = output_grad(meta, context, after(grad_branch, turn_two))
    half_shard = shard_rows // 2
    sums_o = core_sum(
        "output_core", output_give, output_keep, [(k, half_shard) for k in OUTPUT_CHAINS]
    )
    turn_four, packed_four = turn("turn_four", [(sums_a, 2), (sums_b, 2), (sums_o, 0)], turn_three, dk_got, dv_got)
    shrunk_got = cube.swap(after(f_send, turn_three, packed_four), 0)
    shrunk = f_own + shrunk_got.astype(F32)
    result = (middle + live * shrunk).astype(BF)
    joint_give, joint_keep, dkv = joint_grad(
        meta, first, d_query, dkv_own, dk_got, after(dv_got, packed_four)
    )
    sums_j = core_sum("joint_core", joint_give, joint_keep, [(k, shard_rows) for k in range(3)])
    result = from_sets(after(result, packed_four))
    turn_seven, out_seven = turn(
        "turn_seven",
        [(sums_a, 3), (sums_b, 3), (sums_o, 1), (sums_j, 0)],
        turn_four,
        result,
        squares=True,
    )
    expand_own_a, expand_give_a = (out_seven[i] for i in outcome["a"])
    expand_own_b, expand_give_b = (out_seven[i] for i in outcome["b"])
    shrink_first = out_seven[outcome["a_shrink"]]
    shrink_mine = out_seven[outcome["b_shrink"]]

    expand_give = jnp.concatenate([expand_give_a, expand_give_b])
    expand_got = cube.swap(expand_give, 0)
    expand_got_a, expand_got_b = expand_got[: 2 * shard_rows], expand_got[2 * shard_rows :]
    shrink_got = cube.swap(shrink_first.astype(BF), cube.top).astype(F32)
    grad_inputs, grad_gain_one = input_back(
        meta,
        d_query,
        after(dkv, sums_j[0].send[0]),
        grad_middle,
        x_rows,
        gains_all,
        joint + joint_other,
    )
    turn_nine, out_nine = turn(
        "turn_nine", [(sums_o, 2), (sums_j, 1)], turn_seven, shrink_got, expand_got
    )
    gains_term = jnp.concatenate([grad_gain_one, grad_gain_two]).reshape(2, count, -1)
    gains_term = gains_term.transpose(1, 0, 2).reshape(count, -1)
    gains_parts = lax.all_to_all(after(gains_term, out_nine), "fsdp", 0, 0, tiled=True)
    grad_gains = jnp.sum(gains_parts, axis=0).reshape(2, -1)
    grad_inputs = from_sets(after(grad_inputs, turn_seven))
    turn_ten, out_ten = turn(
        "turn_ten", [(sums_o, 3), (sums_j, 2)], turn_nine, grad_inputs, squares=True
    )
    grad_output = jnp.concatenate([out_ten[outcome[("output_core", k)]] for k in OUTPUT_CHAINS])
    _, out_last = turn("turn_last", [(sums_j, 3)], turn_ten, squares=True)
    grad_joint = [out_last[outcome[("joint_core", k)]] for k in range(3)]

    grad_shrink = jnp.stack(
        [jnp.where(upper, shrink_got, shrink_mine), jnp.where(upper, shrink_mine, shrink_got)]
    )
    grad_joint = jnp.concatenate(grad_joint, axis=1)

    local_sq = sum(jnp.sum(out[-1]) for out in (out_seven, out_ten, out_last))
    local_sq = local_sq + jnp.sum(grad_gains * grad_gains)
    squares = lax.all_to_all(jnp.broadcast_to(local_sq, (count, 128)), "fsdp", 0, 0, tiled=True)
    total_sq = jnp.sum(squares[:, 0])
    grad_norm_value = jnp.sqrt(total_sq)
    factor = CLIP_LIMIT / jnp.maximum(grad_norm_value, CLIP_LIMIT)
    joint_new = adam_step(
        joint_weight, factor * grad_joint, joint_mean, joint_square, MATRIX_RATE, MATRIX_DECAY
    )
    output_new = adam_step(
        output_weight, factor * grad_output, output_mean, output_square, MATRIX_RATE, MATRIX_DECAY
    )
    expand_new = adam_expand(
        meta,
        factor.reshape(1),
        expand_weight,
        expand_mean,
        expand_square,
        (expand_own_a, expand_own_b),
        (expand_got_a, expand_got_b),
    )
    shrink_new = adam_step(
        shrink_weight, factor * grad_shrink, shrink_mean, shrink_square, MATRIX_RATE, MATRIX_DECAY
    )
    gains_new = adam_step(norm_gains, factor * grad_gains, gains_mean, gains_square, GAIN_RATE, 0.0)
    return (
        result,
        grad_inputs,
        grad_norm_value,
        *joint_new,
        *output_new,
        *expand_new,
        *shrink_new,
        *gains_new,
    )


def solution(mesh):
    rows = P("fsdp", None)
    cube = P("fsdp", None, None)
    inner = P(None, "fsdp", None)
    gains = P(None, "fsdp")
    count = mesh.shape["fsdp"]

    def body(*args):
        return (local_cube if count == 4 * CHIPS else local_general)(count, *args)

    return jax.shard_map(
        body,
        mesh=mesh,
        in_specs=(cube, P("fsdp"), cube, rows, rows, rows, inner, gains)
        + (rows,) * 6
        + (inner, inner, gains, gains),
        out_specs=(cube, cube, P()) + (rows,) * 9 + (inner,) * 3 + (gains,) * 3,
        check_vma=False,
    )
```

```python
import functools

import jax
import jax.numpy as jnp
from jax import lax
from jax.experimental import pallas as pl
from jax.experimental.pallas import tpu as pltpu
from jax.sharding import PartitionSpec as P

HEADS = 16
SETS = 2
STEP = 10

NORM_EPS = 1e-05
BETA_ONE = 0.9
BETA_TWO = 0.95
ADAM_EPS = 1e-08
MATRIX_RATE = 0.08
GAIN_RATE = 1.0
MATRIX_DECAY = 0.1
CLIP_LIMIT = 1.0

BF = jnp.bfloat16
F32 = jnp.float32


def dot(a, b):
    return lax.dot_general(a, b, (((1,), (0,)), ((), ())), preferred_element_type=F32)


def dot_nt(a, b):
    return lax.dot_general(a, b, (((1,), (1,)), ((), ())), preferred_element_type=F32)


def dot_tn(a, b):
    return lax.dot_general(a, b, (((0,), (0,)), ((), ())), preferred_element_type=F32)


def adam_step(weight, grad_value, mean_old, square_old, learn_rate, weight_decay):
    mean_new = BETA_ONE * mean_old + (1.0 - BETA_ONE) * grad_value
    square_new = BETA_TWO * square_old + (1.0 - BETA_TWO) * grad_value * grad_value
    mean_hat = mean_new / (1.0 - BETA_ONE**STEP)
    square_hat = square_new / (1.0 - BETA_TWO**STEP)
    weight_new = weight - learn_rate * (
        mean_hat / (jnp.sqrt(square_hat) + ADAM_EPS) + weight_decay * weight
    )
    return (weight_new, mean_new, square_new)


class Cube:
    def __init__(self, count):
        self.count = count
        self.bits = count.bit_length() - 1
        self.top = self.bits - 1
        self.index = lax.axis_index("fsdp")
        chip = list(range(1, self.top))
        third = max(1, len(chip) // 3)
        self.orders = [chip[third * k :] + chip[: third * k] for k in range(3)]

    def bit(self, b):
        return (self.index >> b) & 1

    def swap(self, value, b):
        pairs = [(i, i ^ (1 << b)) for i in range(self.count)]
        return lax.ppermute(value, "fsdp", pairs)

    def gather(self, value, bits, lead=0):
        have = []
        for b in bits:
            other = self.swap(value, b)
            mine = self.bit(b) == 1
            axis = lead + sum(1 for h in have if h > b)
            low = jnp.where(mine, other, value)
            high = jnp.where(mine, value, other)
            value = jnp.stack([low, high], axis=axis)
            have.append(b)
        return value

    def reduce(self, value, have, bits, lead=0, last=F32):
        have = list(have)
        for step, b in enumerate(bits):
            axis = lead + sum(1 for h in have if h > b)
            mine = self.bit(b)
            send = lax.dynamic_index_in_dim(value, 1 - mine, axis, keepdims=False).astype(BF)
            keep = lax.dynamic_index_in_dim(value, mine, axis, keepdims=False)
            other = self.swap(send, b)
            value = keep.astype(F32) + other.astype(F32)
            if step < len(bits) - 1:
                value = value.astype(BF)
            have.remove(b)
        return value.astype(last)

    def total(self, value):
        for b in range(self.bits):
            value = value + self.swap(value, b)
        return value


def cuts(width, parts=3, unit=128):
    units = width // unit
    sizes = [units // parts + (1 if k < units % parts else 0) for k in range(parts)]
    edges = [0]
    for size in sizes:
        edges.append(edges[-1] + size * unit)
    return edges


def local_general(
    count,
    tokens,
    depth_count,
    cotangent,
    joint_weight,
    output_weight,
    expand_weight,
    shrink_weight,
    norm_gains,
    joint_mean,
    joint_square,
    output_mean,
    output_square,
    expand_mean,
    expand_square,
    shrink_mean,
    shrink_square,
    gains_mean,
    gains_square,
):
    cube = Cube(count)
    half = count // 2
    own_bits = cube.top
    frames, positions, width = tokens.shape
    run = positions // SETS
    in_set = cube.bit(cube.top)
    upper = in_set == 1
    all_frames = 2 * frames
    rows = all_frames * run
    hidden_width = expand_weight.shape[1] // 2
    head_dim = width // HEADS

    def to_sets(value):
        first, second = value[:, :run], value[:, run:]
        other = cube.swap(jnp.where(upper, first, second), cube.top)
        own = jnp.where(upper, second, first)
        low = jnp.where(upper, other, own)
        high = jnp.where(upper, own, other)
        return jnp.concatenate([low, high], axis=0)

    def from_sets(value):
        value = value.reshape(2, frames, run, value.shape[-1])
        own = jnp.where(upper, value[1], value[0])
        other = cube.swap(jnp.where(upper, value[0], value[1]), cube.top)
        first = jnp.where(upper, other, own)
        second = jnp.where(upper, own, other)
        return jnp.concatenate([first, second], axis=1)

    position_index = jnp.arange(positions)
    live_here = (position_index[None, :] < depth_count[:, None]).astype(F32)[:, :, None]
    masked = (cotangent.astype(F32) * live_here).astype(BF)

    gains_local = norm_gains.astype(BF)
    gains_all = cube.gather(gains_local, range(cube.bits), lead=1)
    gains_all = gains_all.reshape(2, width).astype(F32)

    def gather_matrix(shard, order, lead=0):
        return cube.gather(shard, list(order) + [0], lead=lead)

    joint_low = joint_weight.astype(BF)
    joint_parts = [
        gather_matrix(joint_low[:, k * width : (k + 1) * width], cube.orders[k]).reshape(width, width)
        for k in range(3)
    ]
    x_rows = to_sets(tokens).reshape(rows, width).astype(F32)
    live = to_sets(live_here).reshape(rows, 1)
    cot = to_sets(masked).reshape(rows, width)

    output_low = output_weight.astype(BF)
    expand_low = expand_weight.astype(BF)
    wide = hidden_width // 4
    edge = [0, wide, (wide + hidden_width) // 2, hidden_width]
    expand_shards = []
    for k in range(3):
        gate_cols = expand_low[:, edge[k] : edge[k + 1]]
        up_cols = expand_low[:, hidden_width + edge[k] : hidden_width + edge[k + 1]]
        parts = ([output_low] if k == 0 else []) + [gate_cols, up_cols]
        expand_shards.append(jnp.concatenate(parts, axis=1))
    expand_parts = [
        gather_matrix(expand_shards[k], cube.orders[k]).reshape(width, -1) for k in range(3)
    ]
    output_full = expand_parts[0][:, :width]
    gate_full = [expand_parts[0][:, width : 2 * width]] + [
        expand_parts[k][:, : edge[k + 1] - edge[k]] for k in (1, 2)
    ]
    up_full = [expand_parts[0][:, 2 * width :]] + [
        expand_parts[k][:, edge[k + 1] - edge[k] :] for k in (1, 2)
    ]

    shrink_low = shrink_weight.astype(BF)
    shrink_mine = jnp.where(upper, shrink_low[1], shrink_low[0])
    shrink_send = jnp.where(upper, shrink_low[0], shrink_low[1])
    shrink_other = cube.swap(shrink_send, cube.top)
    shrink_pair = jnp.stack(
        [jnp.where(upper, shrink_other, shrink_mine), jnp.where(upper, shrink_mine, shrink_other)]
    )
    col = cuts(width)
    shrink_parts = [
        gather_matrix(shrink_pair[:, :, col[k] : col[k + 1]], cube.orders[k], lead=1).reshape(
            hidden_width, -1
        )
        for k in range(3)
    ]

    inv_one = lax.rsqrt(jnp.mean(x_rows * x_rows, axis=-1, keepdims=True) + NORM_EPS)
    first = (x_rows * inv_one * gains_all[0]).astype(BF)
    query, key_own, value_own = [dot(first, joint_parts[k]).astype(BF) for k in range(3)]
    key_value = cube.swap(jnp.concatenate([key_own, value_own], axis=1), cube.top)

    def heads(value):
        return value.reshape(all_frames, run, HEADS, head_dim)

    q_h = heads(query)
    k_h = jnp.concatenate([heads(key_value[:, :width]), heads(key_own)], axis=1)
    v_h = jnp.concatenate([heads(key_value[:, width:]), heads(value_own)], axis=1)
    scale = head_dim ** (-0.5)
    scores = jnp.einsum("fphd,fkhd->fhpk", q_h, k_h, preferred_element_type=F32) * scale
    row = jnp.arange(run)[:, None]
    column = jnp.arange(2 * run)[None, :]
    seen = jnp.where(column < run, upper, row >= column - run)
    scores = jnp.where(seen, scores, -1e30)
    exp_scores = jnp.exp(scores - jnp.max(scores, axis=-1, keepdims=True))
    attention = exp_scores / jnp.sum(exp_scores, axis=-1, keepdims=True)
    attention_low = attention.astype(BF)
    context = (
        jnp.einsum("fhpk,fkhd->fphd", attention_low, v_h, preferred_element_type=F32)
        .reshape(rows, width)
        .astype(BF)
    )
    middle = x_rows + live * dot(context, output_full)
    inv_two = lax.rsqrt(jnp.mean(middle * middle, axis=-1, keepdims=True) + NORM_EPS)
    second = (middle * inv_two * gains_all[1]).astype(BF)
    gate = [dot(second, w) for w in gate_full]
    up = [dot(second, w) for w in up_full]
    hidden = jnp.concatenate(
        [(jax.nn.silu(g) * u).astype(BF) for g, u in zip(gate, up)], axis=1
    )
    shrunk = jnp.concatenate([dot(hidden, w) for w in shrink_parts], axis=1)
    result = from_sets((middle + live * shrunk).astype(BF))

    def reduce_matrix(grad, order, lead=0, block=None):
        bits = list(range(own_bits))
        shape = grad.shape
        if lead:
            grad = grad.reshape((2,) + (2,) * own_bits + (shape[0] // 2 // half, shape[1]))
        else:
            grad = grad.reshape((2,) * own_bits + (shape[0] // half, shape[1]))
        return cube.reduce(grad, bits, [0] + list(order), lead=lead)

    grad_shrink_parts = [
        reduce_matrix(dot_tn(hidden, cot[:, col[k] : col[k + 1]]).astype(BF), cube.orders[k], lead=1)
        for k in range(3)
    ]
    grad_shrink_pair = jnp.concatenate(grad_shrink_parts, axis=-1)
    shrink_keep = jnp.where(upper, grad_shrink_pair[1], grad_shrink_pair[0])
    shrink_give = jnp.where(upper, grad_shrink_pair[0], grad_shrink_pair[1]).astype(BF)
    shrink_got = cube.swap(shrink_give, cube.top).astype(F32)
    grad_shrink = jnp.stack(
        [jnp.where(upper, shrink_got, shrink_keep), jnp.where(upper, shrink_keep, shrink_got)]
    )

    grad_hidden = sum(dot_nt(cot[:, col[k] : col[k + 1]], shrink_parts[k]) for k in range(3))
    grad_second = 0.0
    grad_expand_parts = []
    for k in range(3):
        d_hid = grad_hidden[:, edge[k] : edge[k + 1]]
        sig = jax.nn.sigmoid(gate[k])
        d_gate = (d_hid * up[k] * sig * (1.0 + gate[k] * (1.0 - sig))).astype(BF)
        d_up = (d_hid * gate[k] * sig).astype(BF)
        both = jnp.concatenate([d_gate, d_up], axis=1)
        weight_pair = jnp.concatenate([gate_full[k], up_full[k]], axis=1)
        grad_second = grad_second + dot_nt(both, weight_pair)
        grad_expand_parts.append(
            reduce_matrix(dot_tn(second, both).astype(BF), cube.orders[k])
        )
    grad_expand = jnp.concatenate(
        [grad_expand_parts[k][:, : edge[k + 1] - edge[k]] for k in range(3)]
        + [grad_expand_parts[k][:, edge[k + 1] - edge[k] :] for k in range(3)],
        axis=1,
    )

    def normalize_back(values, inverse, gain_row, grad_out):
        scaled = grad_out * gain_row
        grad_in = inverse * scaled - values * inverse * inverse * inverse * jnp.mean(
            scaled * values, axis=-1, keepdims=True
        )
        return (grad_in, jnp.sum(grad_out * values * inverse, axis=0))

    grad_mid_norm, grad_gain_two = normalize_back(middle, inv_two, gains_all[1], grad_second)
    grad_middle = cot.astype(F32) + grad_mid_norm
    grad_branch = (grad_middle * live).astype(BF)
    grad_context = dot_nt(grad_branch, output_full).astype(BF)

    g_h = heads(grad_context)
    grad_attention = jnp.einsum("fphd,fkhd->fhpk", g_h, v_h, preferred_element_type=F32)
    grad_value = jnp.einsum("fhpk,fphd->fkhd", attention_low, g_h, preferred_element_type=F32)
    grad_scores = attention * (
        grad_attention - jnp.sum(grad_attention * attention, axis=-1, keepdims=True)
    )
    grad_scores = grad_scores.astype(BF)
    grad_query = (
        jnp.einsum("fhpk,fkhd->fphd", grad_scores, k_h, preferred_element_type=F32) * scale
    )
    grad_key = jnp.einsum("fhpk,fphd->fkhd", grad_scores, q_h, preferred_element_type=F32) * scale
    give = jnp.concatenate(
        [grad_key[:, :run].reshape(rows, width), grad_value[:, :run].reshape(rows, width)], axis=1
    ).astype(BF)
    got = cube.swap(give, cube.top).astype(F32)
    got = jnp.where(upper, 0.0, got)
    d_query = grad_query.reshape(rows, width).astype(BF)
    d_key = (grad_key[:, run:].reshape(rows, width) + got[:, :width]).astype(BF)
    d_value = (grad_value[:, run:].reshape(rows, width) + got[:, width:]).astype(BF)

    grad_output = reduce_matrix(dot_tn(context, grad_branch).astype(BF), cube.orders[0])
    joint_grads = [
        reduce_matrix(dot_tn(first, d).astype(BF), cube.orders[k])
        for k, d in enumerate((d_query, d_key, d_value))
    ]
    grad_joint = jnp.concatenate(joint_grads, axis=1)
    grad_first = sum(
        dot_nt(d, w) for d, w in zip((d_query, d_key, d_value), joint_parts)
    )
    grad_in_norm, grad_gain_one = normalize_back(x_rows, inv_one, gains_all[0], grad_first)
    grad_inputs = from_sets((grad_middle + grad_in_norm).astype(BF))

    gains_term = jnp.stack([grad_gain_one, grad_gain_two]).reshape((2,) + (2,) * cube.bits + (-1,))
    bits = list(range(cube.bits))
    have = list(bits)
    for b in bits:
        axis = 1 + sum(1 for h in have if h > b)
        mine = cube.bit(b)
        send = lax.dynamic_index_in_dim(gains_term, 1 - mine, axis, keepdims=False)
        keep = lax.dynamic_index_in_dim(gains_term, mine, axis, keepdims=False)
        gains_term = keep + cube.swap(send, b)
        have.remove(b)
    grad_gains = gains_term

    reduced = (grad_joint, grad_output, grad_expand, grad_shrink, grad_gains)
    local_sq = sum(jnp.sum(g * g) for g in reduced)
    total_sq = cube.total(jnp.broadcast_to(local_sq, (8, 128)))[0, 0]
    grad_norm_value = jnp.sqrt(total_sq)
    factor = CLIP_LIMIT / jnp.maximum(grad_norm_value, CLIP_LIMIT)
    joint_new = adam_step(
        joint_weight, factor * reduced[0], joint_mean, joint_square, MATRIX_RATE, MATRIX_DECAY
    )
    output_new = adam_step(
        output_weight, factor * reduced[1], output_mean, output_square, MATRIX_RATE, MATRIX_DECAY
    )
    expand_new = adam_step(
        expand_weight, factor * reduced[2], expand_mean, expand_square, MATRIX_RATE, MATRIX_DECAY
    )
    shrink_new = adam_step(
        shrink_weight, factor * reduced[3], shrink_mean, shrink_square, MATRIX_RATE, MATRIX_DECAY
    )
    gains_new = adam_step(norm_gains, factor * reduced[4], gains_mean, gains_square, GAIN_RATE, 0.0)
    return (
        result,
        grad_inputs,
        grad_norm_value,
        *joint_new,
        *output_new,
        *expand_new,
        *shrink_new,
        *gains_new,
    )


CHIPS = 8
CHAIN_BITS = [[(k + t) % 3 for t in range(3)] for k in range(3)]
CHAIN_MASKS = [
    [sum(((j >> t) & 1) << bits[t] for t in range(3)) for j in range(CHIPS)] for bits in CHAIN_BITS
]
VM = pl.BlockSpec(memory_space=pltpu.VMEM)
HB = pl.BlockSpec(memory_space=pltpu.HBM)
SM = pl.BlockSpec(memory_space=pltpu.SMEM)
MIB = 1 << 20
SMALL = pl.CostEstimate(flops=1, bytes_accessed=1, transcendentals=0)


def aligned(index, size):
    return pl.ds(pl.multiple_of(index * size, size), size)


def after(value, *earlier):
    return lax.optimization_barrier((value, earlier))[0]


def plus(a, b):
    return (a.astype(F32) + b.astype(F32)).astype(BF)


class Jobs:
    def __init__(self, width):
        self.width = width
        self.inputs, self.outputs, self.work = [], [], []

    def source(self, array):
        for i, known in enumerate(self.inputs):
            if known is array:
                return i
        self.inputs.append(array)
        return len(self.inputs) - 1

    def output(self, rows, dtype=BF):
        self.outputs.append(jax.ShapeDtypeStruct((rows, self.width), dtype))
        return len(self.outputs) - 1

    def copy(self, array, row, target, target_row, count):
        self.work.append((self.source(array), row, None, 0, target, target_row, count))

    def add(self, a, a_row, b, b_row, target, target_row, count):
        self.work.append((self.source(a), a_row, self.source(b), b_row, target, target_row, count))

    def run(self, meta, name, *earlier, squares=False, norm=(), waits=()):
        inputs = after(self.inputs, *earlier) if earlier else self.inputs
        adds = [w for w in self.work if w[2] is not None]
        rows = sum(w[6] for w in adds)
        moved = sum(w[6] for w in self.work if w[2] is None)
        scratch = [pltpu.SemaphoreType.DMA((3, len(self.work)))]
        scratch += [pltpu.VMEM((max(moved, 16), self.width), BF)]
        if adds:
            scratch += [pltpu.VMEM((rows, self.width), BF)] * 3
            scratch += [pltpu.VMEM((rows, self.width), F32)]
        shapes = list(self.outputs)
        if squares:
            shape = (norm[0], 128) if norm else (8, self.width)
            shapes.append(jax.ShapeDtypeStruct(shape, F32))
        more = list(norm[1:])
        scratch += [pltpu.VMEM((8, self.width), F32)] if squares else []
        return pl.pallas_call(
            functools.partial(
                jobs_kernel, self.work, len(inputs), self.outputs, squares, len(more), len(waits)
            ),
            in_specs=[SM] + [HB] * len(inputs) + [VM] * len(more) + [HB] * len(waits),
            out_specs=[HB] * len(self.outputs) + ([VM] if squares else []),
            out_shape=shapes,
            scratch_shapes=scratch,
            compiler_params=pltpu.CompilerParams(vmem_limit_bytes=60 * MIB),
            cost_estimate=SMALL,
            name=name,
        )(meta, *inputs, *more, *waits)


def jobs_kernel(work, count, outputs, squares, more, waits, meta, *refs):
    sources, norm = refs[:count], refs[count : count + more]
    refs = refs[count + more + waits :]
    targets = refs[: len(outputs)]
    refs = refs[len(outputs) :]
    if squares:
        square_out, square_ref = refs[0], refs[-1]
        refs = refs[1:-1]
    sem = refs[0]
    core = meta[1]

    def part(ref, row, rows):
        if isinstance(row, tuple):
            start = pl.multiple_of(jnp.where(core == 0, row[0], row[1]), 16)
            return ref.at[pl.ds(start, rows)]
        return ref.at[row : row + rows]

    coming, leaving = [], []
    at, moved = 0, 0
    transit = refs[1]
    refs = refs[:1] + refs[2:]
    for i, (a, a_row, b, b_row, target, target_row, rows) in enumerate(work):
        if b is None:
            spot = slice(moved, moved + rows)
            copy = pltpu.make_async_copy(part(sources[a], a_row, rows), transit.at[spot], sem.at[0, i])
            copy.start()
            coming.append(((copy,), spot))
            moved += rows
            continue
        spot = slice(at, at + rows)
        pair = (
            pltpu.make_async_copy(part(sources[a], a_row, rows), refs[1].at[spot], sem.at[0, i]),
            pltpu.make_async_copy(part(sources[b], b_row, rows), refs[2].at[spot], sem.at[1, i]),
        )
        for copy in pair:
            copy.start()
        coming.append((pair, spot))
        at += rows
    if squares:
        square_ref[...] = jnp.zeros_like(square_ref)
    for i, (a, a_row, b, b_row, target, target_row, rows) in enumerate(work):
        pair, spot = coming[i]
        finish(pair)
        if b is None:
            copy = pltpu.make_async_copy(
                transit.at[spot], part(targets[target], target_row, rows), sem.at[2, i]
            )
            copy.start()
            leaving.append(copy)
            continue
        wide = outputs[target].dtype == F32
        store = refs[4] if wide else refs[3]
        if not wide and not squares:
            store[spot] = plus(refs[1][spot], refs[2][spot])
        else:
            total = refs[1][spot].astype(F32) + refs[2][spot].astype(F32)
            store[spot] = total.astype(store.dtype)
            if wide:
                square = (total * total).reshape(rows // 8, 8, total.shape[1])
                square_ref[...] += jnp.sum(square, axis=0)
        copy = pltpu.make_async_copy(
            store.at[spot], part(targets[target], target_row, rows), sem.at[2, i]
        )
        copy.start()
        leaving.append(copy)
    if squares and not norm:
        square_out[...] = square_ref[...]
    if norm:
        total = jnp.sum(square_ref[...])
        for i, ref in enumerate(norm):
            value = ref[...]
            total = total + jnp.sum(value if i == 0 else value * value)
        square_out[...] = jnp.full(square_out.shape, total, F32)
    finish(leaving)


class Blocks:
    def __init__(self, own=None, rows=None):
        self.rows = own.shape[0] if rows is None else rows
        self.held = [] if own is None else [(own, 0)]

    def arrived(self, array, row, count):
        for j in range(count):
            self.held.append((array, row + j * self.rows))


def place(jobs, held, rows, target, target_row):
    start = 0
    while start < len(held):
        array, row = held[start]
        stop = start + 1
        while stop < len(held) and held[stop][0] is array and held[stop][1] == row + (stop - start) * rows:
            stop += 1
        jobs.copy(array, row, target, target_row + start * rows, (stop - start) * rows)
        start = stop


class Round:
    def __init__(self, cube, meta, width, name):
        self.cube, self.meta, self.name = cube, meta, name
        self.jobs = Jobs(width)
        self.axis_work = []
        self.core_work = []

    def gather(self, chains, level):
        self.axis_work.append((chains, level))
        return self

    def core(self, chains, others, start, stop):
        self.core_work.append((chains, others, start, stop))
        return self

    def run(self, *earlier, gate=()):
        jobs = self.jobs
        filled = []
        for axis in range(3):
            held = []
            for chains, level in self.axis_work:
                blocks = chains[(axis - level) % 3]
                if blocks is not None:
                    held.append((blocks, blocks.held[: 1 << level]))
            filled.append(held)
        core_held = []
        for chains, others, start, stop in self.core_work:
            for blocks, other in zip(chains, others):
                if blocks is not None:
                    core_held.append((blocks, other, blocks.held[start:stop]))
        direct = not core_held and all(len(h) == 1 and len(h[0][1]) == 1 for h in filled)
        if direct:
            payloads = [h[0][1][0][0] for h in filled]
            if earlier:
                payloads = after(payloads, *earlier)
        else:
            for held in filled:
                if held:
                    target = jobs.output(sum(b.rows * len(h) for b, h in held))
                    row = 0
                    for blocks, part in held:
                        place(jobs, part, blocks.rows, target, row)
                        row += blocks.rows * len(part)
            if core_held:
                target = jobs.output(sum(b.rows * len(h) for b, _, h in core_held))
                row = 0
                for blocks, _, part in core_held:
                    place(jobs, part, blocks.rows, target, row)
                    row += blocks.rows * len(part)
            payloads = jobs.run(self.meta, self.name, *earlier)
            self.packed = payloads
            if gate:
                axes = sum(1 for held in filled if held)
                payloads = after(list(payloads[:axes]), *gate) + list(payloads[axes:])
        got = []
        index = 0
        for axis, held in enumerate(filled):
            if not held:
                continue
            array = self.cube.swap(payloads[index], 1 + axis)
            index += 1
            row = 0
            for blocks, part in held:
                blocks.arrived(array, row, len(part))
                row += blocks.rows * len(part)
            got.append(array)
        self.got = got
        self.core_got = None
        if core_held:
            array = self.cube.swap(payloads[index], 0)
            row = 0
            for blocks, other, part in core_held:
                other.arrived(array, row, len(part))
                row += blocks.rows * len(part)
            self.core_got = array
        self.payloads = payloads
        return self


def operands(*chains):
    arrays, tables = [], []
    for blocks in chains:
        table = []
        for array, row in blocks.held:
            found = [i for i, a in enumerate(arrays) if a is array]
            if not found:
                arrays.append(array)
                found = [len(arrays) - 1]
            table.append((found[0], row))
        tables.append((blocks.rows, table))
    return arrays, tables


class Sums:
    def __init__(self, keep, send, rows, final):
        self.keep, self.send, self.rows, self.count, self.final = keep, send, rows, 4, final


def reduce_round(cube, meta, width, name, work, *earlier, squares=False, gate=(), norm=(), waits=()):
    jobs = Jobs(width)
    filled = []
    direct = all(step == 0 for _, step in work) and len(work) == 1
    for axis in range(3):
        parts = []
        for chains, step in work:
            if step < 3:
                chain = chains[(axis - (2 - step)) % 3]
                if chain is not None:
                    parts.append((chain, step))
        filled.append(parts)
    if direct:
        payloads = [parts[0][0].send[0] for parts in filled]
        if earlier:
            payloads = after(payloads, *earlier)
    else:
        layout = []
        for parts in filled:
            if not parts:
                continue
            rows = 0
            target = None
            sizes = []
            for chain, step in parts:
                size = chain.rows * (4 >> step)
                sizes.append((chain, step, rows, size))
                rows += size
            layout.append((jobs.output(rows), sizes))
        kept = {}
        for target, sizes in layout:
            for chain, step, row, size in sizes:
                if step == 0:
                    jobs.copy(chain.send[0], chain.send[1], target, row, size)
                else:
                    got, got_row = chain.got
                    array, keep_row = chain.keep
                    own = jobs.output(size)
                    jobs.add(got, got_row + size, array, keep_row + size, target, row, size)
                    jobs.add(got, got_row, array, keep_row, own, 0, size)
                    kept[own] = chain
        for chains, step in work:
            if step == 3:
                for chain in chains:
                    if chain is not None:
                        chain.final(jobs, chain.got, chain.keep, chain.rows)
        out = jobs.run(meta, name, *earlier, squares=squares, norm=norm, waits=waits)
        for own, chain in kept.items():
            chain.keep = (out[own], 0)
        payloads = [out[target] for target, _ in layout]
        if gate and payloads:
            payloads = after(payloads, *gate)
    got = []
    index = 0
    for axis, parts in enumerate(filled):
        if not parts:
            continue
        array = cube.swap(payloads[index], 1 + axis)
        index += 1
        row = 0
        for chain, step in parts:
            chain.got = (array, row)
            row += chain.rows * (4 >> step)
        got.append(array)
    return (got, out) if not direct else (got, None)


def first_kernel(joint, q, k, v):
    width = q.shape[1]
    q[...] = joint[:, :width].astype(BF)
    k[...] = joint[:, width : 2 * width].astype(BF)
    v[: joint.shape[0]] = joint[:, 2 * width :].astype(BF)


def first_shards(joint):
    rows, width = joint.shape[0], joint.shape[1] // 3
    return pl.pallas_call(
        first_kernel,
        in_specs=[VM],
        out_specs=[VM] * 3,
        out_shape=[jax.ShapeDtypeStruct((r, width), BF) for r in (rows, rows, rows + 16)],
        compiler_params=pltpu.CompilerParams(vmem_limit_bytes=60 * MIB),
        name="first_shards",
    )(joint)


def split_kernel(meta, expand, shrink, output, own, give, shrink_own, shrink_give, out_a, out_b):
    core, group = meta[1], meta[2]
    rows = expand.shape[0]
    block = expand.shape[1] // (2 * 2 * 2 * CHIPS)
    for turn in range(2):
        part = turn ^ (1 - group)
        for kind in range(2):
            for chip in range(CHIPS):
                base = ((kind * 2 + part) * CHIPS + chip) * 2
                cols = slice(chip * block, (chip + 1) * block)
                r = slice((turn * 2 + kind) * rows, (turn * 2 + kind + 1) * rows)
                own[r, cols] = expand[:, aligned(base + core, block)].astype(BF)
                give[r, cols] = expand[:, aligned(base + 1 - core, block)].astype(BF)
    shrink_own[...] = shrink[group].astype(BF)
    shrink_give[...] = shrink[1 - group].astype(BF)
    out_a[...] = output[: rows // 2].astype(BF)
    out_b[...] = output[rows // 2 :].astype(BF)


def split_weights(meta, expand, shrink, output):
    rows, width = output.shape
    four = jax.ShapeDtypeStruct((4 * rows, width), BF)
    two = jax.ShapeDtypeStruct(shrink.shape[1:], BF)
    half = jax.ShapeDtypeStruct((rows // 2, width), BF)
    return pl.pallas_call(
        split_kernel,
        in_specs=[SM, VM, VM, VM],
        out_specs=[VM] * 6,
        out_shape=[four, four, two, two, half, half],
        compiler_params=pltpu.CompilerParams(vmem_limit_bytes=60 * MIB),
        name="split_weights",
    )(meta, expand, shrink, output)


def load_blocks(table, refs, w, k, chip, sem):
    copies = []
    rows, places = table
    for j, (index, row) in enumerate(places):
        target = w.at[aligned(chip ^ CHAIN_MASKS[k][j], rows), :]
        copy = pltpu.make_async_copy(refs[index].at[row : row + rows], target, sem.at[j])
        copy.start()
        copies.append(copy)
    return copies


def store_blocks(w, pieces, rows, k, chip, sem):
    copies = []
    for j in range(CHIPS):
        source = w.at[aligned(chip ^ CHAIN_MASKS[k][j], rows), :]
        row = (j % 4) * rows
        copy = pltpu.make_async_copy(source, pieces[j // 4].at[row : row + rows], sem.at[j])
        copy.start()
        copies.append(copy)
    return copies


def finish(copies):
    for copy in copies:
        copy.wait()


TILE = 256


def ffn_rows_kernel(first, count, tables, meta, n2m, n2o, cm, co, *refs):
    pieces = refs[:count]
    refs = refs[count:]
    if not first:
        dn_in = refs[0]
        refs = refs[1:]
    if first:
        dn_out, hid, dg, du, n2, c, wg, wu, ws, sem = refs
    else:
        dn_out, dn_send, hid, dg, du, n2, c, wg, wu, ws, sem = refs
    chip = meta[0]
    mats = (wg, wu, ws)
    coming = [load_blocks(tables[k], pieces, mats[k], k, chip, sem.at[k]) for k in range(3)]
    rows = n2m.shape[0]
    n2[:rows] = n2m[...]
    n2[rows:] = n2o[...]
    c[:rows] = cm[...]
    c[rows:] = co[...]
    for copies in coming:
        finish(copies)
    width = wg.shape[1]

    def gates(t, _):
        cols = aligned(t, TILE)
        g = dot(n2[...], wg[:, cols])
        u = dot(n2[...], wu[:, cols])
        dh = dot_nt(c[...], ws[cols, :])
        sig = jax.nn.sigmoid(g)
        silu = g * sig
        hid[:, cols] = (silu * u).astype(BF)
        du[:, cols] = (dh * silu).astype(BF)
        dg[:, cols] = (dh * u * sig * (1.0 + g * (1.0 - sig))).astype(BF)
        return 0

    lax.fori_loop(0, width // TILE, gates, 0)

    def back(t, _):
        cols = aligned(t, TILE)
        d = dot_nt(dg[...], wg[cols, :]) + dot_nt(du[...], wu[cols, :])
        if first:
            dn_out[:, cols] = d
        else:
            d = d + dn_in[:, cols]
            dn_out[:, cols] = d[:rows]
            dn_send[:, cols] = d[rows:]
        return 0

    lax.fori_loop(0, width // TILE, back, 0)


def ffn_rows(meta, n2m, n2o, cm, co, chains, carried):
    first = carried is None
    arrays, tables = operands(*chains)
    rows, width = 2 * n2m.shape[0], n2m.shape[1]
    low = jax.ShapeDtypeStruct((rows, width), BF)
    return pl.pallas_call(
        functools.partial(ffn_rows_kernel, first, len(arrays), tables),
        in_specs=[SM] + [VM] * 4 + [HB] * len(arrays) + ([] if first else [VM]),
        out_specs=[VM] * (4 if first else 5),
        out_shape=(
            [jax.ShapeDtypeStruct((rows, width), F32)]
            if first
            else [jax.ShapeDtypeStruct((rows // 2, width), F32)] * 2
        )
        + [low, low, low],
        scratch_shapes=[pltpu.VMEM((rows, width), BF)] * 2
        + [pltpu.VMEM((width, width), BF)] * 3
        + [pltpu.SemaphoreType.DMA((3, CHIPS))],
        compiler_params=pltpu.CompilerParams(vmem_limit_bytes=60 * MIB),
        cost_estimate=SMALL,
        name="ffn_rows",
    )(meta, n2m, n2o, cm, co, *arrays, *(() if first else (carried,)))


def ffn_weights_kernel(first, count, table, meta, n2m, n2o, cm, co, hid, dg, du, *refs):
    pieces = refs[:count]
    refs = refs[count:]
    if not first:
        f_in = refs[0]
        refs = refs[1:]
    f_out = refs[0]
    if not first:
        f_send = refs[1]
        refs = refs[1:]
    outs = refs[1:7]
    n2, c, ws, dwg, dwu, dws, in_sem, out_sem = refs[7:]
    chip = meta[0]
    coming = load_blocks(table, pieces, ws, 2, chip, in_sem)
    rows = n2m.shape[0]
    n2[:rows] = n2m[...]
    n2[rows:] = n2o[...]
    c[:rows] = cm[...]
    c[rows:] = co[...]
    width = ws.shape[1]
    leaving = []
    for k, (lhs, rhs, dw) in enumerate(((n2, dg, dwg), (n2, du, dwu), (hid, c, dws))):

        def step(t, _, lhs=lhs, rhs=rhs, dw=dw):
            cols = aligned(t, TILE)
            dw[cols, :] = dot_tn(lhs[:, cols], rhs[...]).astype(BF)
            return 0

        lax.fori_loop(0, width // TILE, step, 0)
        leaving += store_blocks(dw, outs[2 * k : 2 * k + 2], table[0], k, chip, out_sem.at[k])
    finish(coming)

    def down(t, _):
        cols = aligned(t, TILE)
        f = dot(hid[...], ws[:, cols])
        if first:
            f_out[:, cols] = f
        else:
            f = f + f_in[:, cols]
            f_out[:, cols] = f[:rows]
            f_send[:, cols] = f[rows:].astype(BF)
        return 0

    lax.fori_loop(0, width // TILE, down, 0)
    finish(leaving)


def ffn_weights(meta, n2m, n2o, cm, co, hid, dg, du, chain, carried):
    first = carried is None
    arrays, tables = operands(chain)
    rows, width = 2 * n2m.shape[0], n2m.shape[1]
    piece = jax.ShapeDtypeStruct((4 * chain.rows, width), BF)
    return pl.pallas_call(
        functools.partial(ffn_weights_kernel, first, len(arrays), tables[0]),
        in_specs=[SM] + [VM] * 7 + [HB] * len(arrays) + ([] if first else [VM]),
        out_specs=[VM] * (1 if first else 2) + [HB] * 6,
        out_shape=(
            [jax.ShapeDtypeStruct((rows, width), F32)]
            if first
            else [
                jax.ShapeDtypeStruct((rows // 2, width), F32),
                jax.ShapeDtypeStruct((rows // 2, width), BF),
            ]
        )
        + [piece] * 6,
        scratch_shapes=[pltpu.VMEM((rows, width), BF)] * 2
        + [pltpu.VMEM((width, width), BF)] * 4
        + [pltpu.SemaphoreType.DMA((CHIPS,)), pltpu.SemaphoreType.DMA((3, CHIPS))],
        compiler_params=pltpu.CompilerParams(vmem_limit_bytes=60 * MIB),
        cost_estimate=SMALL,
        name="ffn_weights",
    )(meta, n2m, n2o, cm, co, hid, dg, du, *arrays, *(() if first else (carried,)))


OUTPUT_CHAINS = (1, 2)


def load_devices(table, refs, k, side, shard, row, count, target, lo, meta, sem, used):
    chip, core = meta[0], meta[1]
    copies = []
    for j, (index, base) in enumerate(table[1]):
        device = (chip ^ CHAIN_MASKS[k][j]) * 2 + (core if side == 0 else 1 - core)
        start = pl.multiple_of(device * shard + row, 16)
        copy = pltpu.make_async_copy(
            refs[index].at[base : base + count],
            target.at[pl.ds(start, count), lo : lo + target.shape[0]],
            sem.at[used + j],
        )
        copy.start()
        copies.append(copy)
    return copies


def load_joint(tables, refs, target, meta, sem):
    width = target.shape[0]
    shard = width // (2 * CHIPS)
    copies = []
    for k in range(3):
        for side in range(2):
            copies += load_devices(
                tables[3 * side + k], refs, k, side, shard, 0, shard, target, k * width, meta, sem, len(copies)
            )
    return copies


def load_output(tables, refs, target, meta, sem):
    shard = target.shape[0] // (2 * CHIPS)
    half = shard // 2
    copies = []
    for i, k in enumerate(OUTPUT_CHAINS):
        for side in range(2):
            copies += load_devices(
                tables[2 * side + i], refs, k, side, shard, i * half, half, target, 0, meta, sem, len(copies)
            )
    return copies


PAIR_COPIES = 128
PAD = 16


def joint_kernel(count, tables, meta, x, *refs):
    pieces = refs[:count]
    first, query, pair, gains, w, gain_rows, sem, gain_sem = refs[count:]
    width = x.shape[1]
    coming = load_joint(tables, pieces, w, meta, sem)
    shard = width // (2 * CHIPS)
    gain_copies = []
    for side in range(2):
        for j, (index, base) in enumerate(tables[3 * side + 2][1]):
            copy = pltpu.make_async_copy(
                pieces[index].at[base + shard : base + shard + 16],
                gain_rows.at[side * CHIPS + j],
                gain_sem.at[side * CHIPS + j],
            )
            copy.start()
            gain_copies.append(copy)
    value = x[...].astype(F32)
    inverse = lax.rsqrt(jnp.mean(value * value, axis=-1, keepdims=True) + NORM_EPS)
    finish(gain_copies)
    whole = jnp.sum(gain_rows[...].astype(F32), axis=0)
    gains[...] = whole[:8]
    first[...] = (value * inverse * whole[0:1]).astype(BF)
    finish(coming)
    tiles = width // TILE
    rows = x.shape[0]
    pair[2 * rows :] = jnp.zeros((PAD, width), BF)
    for part, (out, low) in enumerate(((query, 0), (pair, 0), (pair, rows))):

        def step(t, _, part=part, out=out, low=low):
            weight = w[:, aligned(t + part * tiles, TILE)]
            out[low : low + rows, aligned(t, TILE)] = dot(first[...], weight).astype(BF)
            return 0

        lax.fori_loop(0, tiles, step, 0)


def joint_forward(meta, x, chains):
    rows, width = x.shape
    arrays, tables = operands(*chains)
    low = jax.ShapeDtypeStruct((rows, width), BF)
    return pl.pallas_call(
        functools.partial(joint_kernel, len(arrays), tables),
        in_specs=[SM, VM] + [HB] * len(arrays),
        out_specs=[VM] * 4,
        out_shape=[
            low,
            low,
            jax.ShapeDtypeStruct((2 * rows + PAD, width), BF),
            jax.ShapeDtypeStruct((8, width), F32),
        ],
        scratch_shapes=[
            pltpu.VMEM((width, 3 * width), BF),
            pltpu.VMEM((2 * CHIPS, 16, width), BF),
            pltpu.SemaphoreType.DMA((PAIR_COPIES,)),
            pltpu.SemaphoreType.DMA((2 * CHIPS,)),
        ],
        compiler_params=pltpu.CompilerParams(vmem_limit_bytes=60 * MIB),
        cost_estimate=SMALL,
        name="joint_forward",
    )(meta, x, *arrays)


CHUNK = 128


def bias_into(bias, run, upper):
    size = 2 * CHUNK
    row = lax.broadcasted_iota(jnp.int32, (size, size), 0) & (CHUNK - 1)
    column = lax.broadcasted_iota(jnp.int32, (size, size), 1)
    own = column < CHUNK
    column = column & (CHUNK - 1)
    shift = run.bit_length() - 1
    same = (row >> shift) == (column >> shift)
    reach = jnp.where(upper, CHUNK, 0)
    seen = same & ((own & (row >= column)) | (~own & (row < reach)))
    bias[...] = jnp.where(seen, 0.0, -1e30)


def stacked(value, left):
    zero = jnp.zeros_like(value)
    return jnp.concatenate([jnp.where(left, value, zero), jnp.where(left, zero, value)], axis=0)


def probabilities(q_st, k_all, bias, scale):
    scores = dot_nt(q_st, k_all) * scale + bias[...]
    exp_scores = jnp.exp(scores - jnp.max(scores, axis=-1, keepdims=True))
    return exp_scores / jnp.sum(exp_scores, axis=-1, keepdims=True)


def context_kernel(run, head_dim, count, tables, meta, query, own, other, x, live, gains, *refs):
    pieces = refs[:count]
    ctx, h_out, n2, wo, bias, sem = refs[count:]
    rows, width = x.shape
    coming = load_output(tables, pieces, wo, meta, sem)
    bias_into(bias, run, meta[2] == 1)
    scale = head_dim ** (-0.5)
    lanes = 2 * head_dim
    left = lax.broadcasted_iota(jnp.int32, (CHUNK, lanes), 1) < head_dim

    def pair(p, _):
        cols = aligned(p, lanes)
        for chunk in range(rows // CHUNK):
            r = slice(chunk * CHUNK, (chunk + 1) * CHUNK)
            r_v = slice(rows + chunk * CHUNK, rows + (chunk + 1) * CHUNK)
            q_st = stacked(query[r, cols], left)
            k_all = jnp.concatenate([own[r, cols], other[r, cols]], axis=0)
            v_all = jnp.concatenate([own[r_v, cols], other[r_v, cols]], axis=0)
            prob = probabilities(q_st, k_all, bias, scale)
            out = dot(prob.astype(BF), v_all)
            ctx[r, cols] = jnp.where(left, out[:CHUNK], out[CHUNK:]).astype(BF)
        return 0

    lax.fori_loop(0, width // lanes, pair, 0)
    finish(coming)

    def project(t, _):
        cols = aligned(t, TILE)
        h_out[:, cols] = x[:, cols].astype(F32) + live[...] * dot(ctx[...], wo[:, cols])
        return 0

    lax.fori_loop(0, width // TILE, project, 0)
    h = h_out[...]
    inverse = lax.rsqrt(jnp.mean(h * h, axis=-1, keepdims=True) + NORM_EPS)
    n2[...] = (h * inverse * gains[1:2, :]).astype(BF)


def context_forward(
    run, meta, query, own, other, x, live, gains, chains
):
    rows, width = x.shape
    arrays, tables = operands(*chains)
    low = jax.ShapeDtypeStruct((rows, width), BF)
    return pl.pallas_call(
        functools.partial(context_kernel, run, width // HEADS, len(arrays), tables),
        in_specs=[SM] + [VM] * 6 + [HB] * len(arrays),
        out_specs=[VM] * 3,
        out_shape=[low, jax.ShapeDtypeStruct((rows, width), F32), low],
        scratch_shapes=[
            pltpu.VMEM((width, width), BF),
            pltpu.VMEM((2 * CHUNK, 2 * CHUNK), F32),
            pltpu.SemaphoreType.DMA((PAIR_COPIES,)),
        ],
        compiler_params=pltpu.CompilerParams(vmem_limit_bytes=60 * MIB),
        cost_estimate=SMALL,
        name="context_forward",
    )(meta, query, own, other, x, live, gains, *arrays)


def norm_back(value, gain, grad):
    inverse = lax.rsqrt(jnp.mean(value * value, axis=-1, keepdims=True) + NORM_EPS)
    scaled = grad * gain
    mean = jnp.mean(scaled * value, axis=-1, keepdims=True)
    grad_in = inverse * scaled - value * (inverse * inverse * inverse) * mean
    return grad_in, jnp.sum(grad * value * inverse, axis=0, keepdims=True)


def context_back_kernel(
    run, head_dim, count, tables, meta, dn_own, dn_got, h, cot, live, gains, query, *refs
):
    own, other = refs[:2]
    pieces = refs[2 : 2 + count]
    dh, dg2, da, dq, dkv, give, wo, bias, dctx, sem = refs[2 + count :]
    rows, width = h.shape
    coming = load_output(tables, pieces, wo, meta, sem)
    bias_into(bias, run, meta[2] == 1)
    give[2 * rows :] = jnp.zeros((PAD, width), BF)
    grad_in, dg2[...] = norm_back(h[...], gains[1:2, :], dn_own[...] + dn_got[...])
    grad = cot[...].astype(F32) + grad_in
    dh[...] = grad
    da[...] = (grad * live[...]).astype(BF)
    finish(coming)

    def project(t, _):
        cols = aligned(t, TILE)
        dctx[:, cols] = dot_nt(da[...], wo[cols, :]).astype(BF)
        return 0

    lax.fori_loop(0, width // TILE, project, 0)
    scale = head_dim ** (-0.5)
    lanes = 2 * head_dim
    pairs = width // lanes
    left = lax.broadcasted_iota(jnp.int32, (CHUNK, lanes), 1) < head_dim

    def pair(p, _):
        cols = aligned(p, lanes)
        v_cols = aligned(p + pairs, lanes)
        for chunk in range(rows // CHUNK):
            r = slice(chunk * CHUNK, (chunk + 1) * CHUNK)
            r_v = slice(rows + chunk * CHUNK, rows + (chunk + 1) * CHUNK)
            q_st = stacked(query[r, cols], left)
            g_st = stacked(dctx[r, cols], left)
            k_all = jnp.concatenate([own[r, cols], other[r, cols]], axis=0)
            v_all = jnp.concatenate([own[r_v, cols], other[r_v, cols]], axis=0)
            prob = probabilities(q_st, k_all, bias, scale)
            d_prob = dot_nt(g_st, v_all)
            d_score = prob * (d_prob - jnp.sum(d_prob * prob, axis=-1, keepdims=True))
            d_score = d_score.astype(BF)
            d_query = dot(d_score, k_all) * scale
            d_key = dot_tn(d_score, q_st) * scale
            d_value = dot_tn(prob.astype(BF), g_st)
            dq[r, cols] = jnp.where(left, d_query[:CHUNK], d_query[CHUNK:]).astype(BF)
            dkv[r, cols] = d_key[:CHUNK]
            dkv[r, v_cols] = d_value[:CHUNK]
            give[r, cols] = d_key[CHUNK:].astype(BF)
            give[r_v, cols] = d_value[CHUNK:].astype(BF)
        return 0

    lax.fori_loop(0, pairs, pair, 0)


def context_back(
    run, meta, dn_own, dn_got, h, cot, live, gains, query, own, other, chains
):
    rows, width = h.shape
    arrays, tables = operands(*chains)
    low = jax.ShapeDtypeStruct((rows, width), BF)
    return pl.pallas_call(
        functools.partial(context_back_kernel, run, width // HEADS, len(arrays), tables),
        in_specs=[SM] + [VM] * 9 + [HB] * len(arrays),
        out_specs=[VM] * 6,
        out_shape=[
            jax.ShapeDtypeStruct((rows, width), F32),
            jax.ShapeDtypeStruct((1, width), F32),
            low,
            low,
            jax.ShapeDtypeStruct((rows, 2 * width), F32),
            jax.ShapeDtypeStruct((2 * rows + PAD, width), BF),
        ],
        scratch_shapes=[
            pltpu.VMEM((width, width), BF),
            pltpu.VMEM((2 * CHUNK, 2 * CHUNK), F32),
            pltpu.VMEM((rows, width), BF),
            pltpu.SemaphoreType.DMA((PAIR_COPIES,)),
        ],
        compiler_params=pltpu.CompilerParams(vmem_limit_bytes=60 * MIB),
        cost_estimate=SMALL,
        name="context_back",
    )(
        meta,
        dn_own,
        dn_got,
        h,
        cot,
        live,
        gains,
        query,
        own,
        other,
        *arrays,
    )


def shard_grads(lhs, rhs_cols, dw):
    width = lhs.shape[1]
    for i, rhs in enumerate(rhs_cols):

        def step(t, _, rhs=rhs, i=i):
            cols = aligned(t, TILE)
            dw[i, cols, :] = dot_tn(lhs[:, cols], rhs()).astype(BF)
            return 0

        lax.fori_loop(0, width // TILE, step, 0)


def store_devices(dw, matrix, row, count, k, targets, base, meta, sem, used):
    chip, core = meta[0], meta[1]
    shard = dw.shape[1] // (2 * CHIPS)
    copies = []
    for side, target in enumerate(targets):
        for j in range(CHIPS):
            device = (chip ^ CHAIN_MASKS[k][j]) * 2 + (1 - core if side == 0 else core)
            start = pl.multiple_of(device * shard + row, 16)
            low = base + j * count
            copy = pltpu.make_async_copy(
                dw.at[matrix, pl.ds(start, count), :],
                target.at[low : low + count],
                sem.at[used + len(copies)],
            )
            copy.start()
            copies.append(copy)
    return copies


def output_grad_kernel(meta, context, grad, give, keep, dw, sem):
    shard_grads(context, (lambda: grad[...],), dw)
    half = dw.shape[1] // (4 * CHIPS)
    leaving = []
    for i, k in enumerate(OUTPUT_CHAINS):
        base = i * CHIPS * half
        leaving += store_devices(
            dw, 0, i * half, half, k, (give, keep), base, meta, sem, len(leaving)
        )
    finish(leaving)


def output_grad(meta, context, grad):
    rows, width = context.shape
    part = jax.ShapeDtypeStruct((width // 2, width), BF)
    return pl.pallas_call(
        output_grad_kernel,
        in_specs=[SM, VM, VM],
        out_specs=[HB, HB],
        out_shape=[part, part],
        scratch_shapes=[
            pltpu.VMEM((1, width, width), BF),
            pltpu.SemaphoreType.DMA((PAIR_COPIES,)),
        ],
        compiler_params=pltpu.CompilerParams(vmem_limit_bytes=60 * MIB),
        cost_estimate=SMALL,
        name="output_grad",
    )(meta, context, grad)


def joint_grad_kernel(meta, first, dq, dkv_own, dkv_got, give, keep, dkv, dw, sem):
    width = first.shape[1]
    rows = first.shape[0]
    for part in range(2):
        cols = slice(part * width, (part + 1) * width)
        got = dkv_got[part * rows : (part + 1) * rows, :]
        more = jnp.where(meta[2] == 1, 0.0, got.astype(F32))
        dkv[:, cols] = (dkv_own[:, cols] + more).astype(BF)
    rights = (lambda: dq[...], lambda: dkv[:, :width], lambda: dkv[:, width:])
    shard = width // (2 * CHIPS)
    leaving = []
    for k in range(3):

        def step(t, _, k=k):
            cols = aligned(t, TILE)
            dw[k, cols, :] = dot_tn(first[:, cols], rights[k]()).astype(BF)
            return 0

        lax.fori_loop(0, width // TILE, step, 0)
        leaving += store_devices(
            dw, k, 0, shard, k, (give, keep), k * CHIPS * shard, meta, sem, len(leaving)
        )
    finish(leaving)


def joint_grad(meta, first, dq, dkv_own, dkv_got):
    rows, width = first.shape
    part = jax.ShapeDtypeStruct((3 * width // 2, width), BF)
    return pl.pallas_call(
        joint_grad_kernel,
        in_specs=[SM] + [VM] * 4,
        out_specs=[HB, HB, VM],
        out_shape=[part, part, jax.ShapeDtypeStruct((rows, 2 * width), BF)],
        scratch_shapes=[
            pltpu.VMEM((3, width, width), BF),
            pltpu.SemaphoreType.DMA((PAIR_COPIES,)),
        ],
        compiler_params=pltpu.CompilerParams(vmem_limit_bytes=60 * MIB),
        cost_estimate=SMALL,
        name="joint_grad",
    )(meta, first, dq, dkv_own, dkv_got)


def input_back_kernel(count, tables, meta, dq, dkv, dh, x, gains, *refs):
    pieces = refs[:count]
    out, dg1, w, dn, sem = refs[count:]
    rows, width = x.shape
    finish(load_joint(tables, pieces, w, meta, sem))

    def step(t, _):
        cols = aligned(t, TILE)
        dn[:, cols] = dot_nt(dq[...], w[cols, :width]) + dot_nt(dkv[...], w[cols, width:])
        return 0

    lax.fori_loop(0, width // TILE, step, 0)
    grad_in, dg1[...] = norm_back(x[...].astype(F32), gains[0:1, :], dn[...])
    out[...] = (dh[...] + grad_in).astype(BF)


def input_back(meta, dq, dkv, dh, x, gains, chains):
    rows, width = x.shape
    arrays, tables = operands(*chains)
    return pl.pallas_call(
        functools.partial(input_back_kernel, len(arrays), tables),
        in_specs=[SM] + [VM] * 5 + [HB] * len(arrays),
        out_specs=[VM, VM],
        out_shape=[
            jax.ShapeDtypeStruct((rows, width), BF),
            jax.ShapeDtypeStruct((1, width), F32),
        ],
        scratch_shapes=[
            pltpu.VMEM((width, 3 * width), BF),
            pltpu.VMEM((rows, width), F32),
            pltpu.SemaphoreType.DMA((PAIR_COPIES,)),
        ],
        compiler_params=pltpu.CompilerParams(vmem_limit_bytes=60 * MIB),
        cost_estimate=SMALL,
        name="input_back",
    )(meta, dq, dkv, dh, x, gains, *arrays)


def adam_rows(k, w, m, v, grad, outs, where, rate, decay):
    new = adam_step(w[where], k * grad, m[where], v[where], rate, decay)
    for out, value in zip(outs, new):
        out[where] = value


def adam_kernel(meta, squares, *refs):
    (ew, em, ev, own_a, own_b, got_a, got_b, jw, jm, jv, jg, ow, om, ov, og_a, og_b) = refs[:16]
    (sw, sm, sv, sg_mine, sg_got) = refs[16:21]
    e_out, j_out, o_out, s_out = refs[21:24], refs[24:27], refs[27:30], refs[30:33]
    core, group = meta[1], meta[2]
    step = pl.program_id(0)
    total = jnp.sum(squares[...], axis=0, keepdims=True)[0:1, 0:1]
    k = CLIP_LIMIT / jnp.maximum(jnp.sqrt(total), CLIP_LIMIT)
    block = 128
    turn = ((step // 2) % 2) ^ (1 - group)
    for q in range(ew.shape[1] // block):
        cols = (slice(None), slice(q * block, (q + 1) * block))
        near = slice((q // 2) * block, (q // 2 + 1) * block)
        own = jnp.where(turn == 0, own_a[:, near], own_b[:, near])
        got = jnp.where(turn == 0, got_a[:, near], got_b[:, near])
        grad = jnp.where(core == q % 2, own, got)
        adam_rows(k, ew, em, ev, grad, e_out, cols, MATRIX_RATE, MATRIX_DECAY)
    everything = (slice(None), slice(None))

    @pl.when(step < 3)
    def _():
        adam_rows(k, jw, jm, jv, jg[0], j_out, everything, MATRIX_RATE, MATRIX_DECAY)

    @pl.when((step >= 3) & (step < 5))
    def _():
        grad = jnp.where(step == 3, og_a[...], og_b[...])
        adam_rows(k, ow, om, ov, grad, o_out, everything, MATRIX_RATE, MATRIX_DECAY)

    @pl.when(step >= 4)
    def _():
        mine = ((step - 4) // 2) == group
        grad = jnp.where(mine, sg_mine[...], sg_got[...].astype(F32))
        adam_rows(k, sw, sm, sv, grad, s_out, (0,), MATRIX_RATE, MATRIX_DECAY)


def adam_matrices(meta, squares, expand, joint, output, shrink):
    rows, wide = expand[0].shape
    width = wide // 8
    shrink_rows = shrink[0].shape[1] // 2

    def half(i):
        return (i // 4, i % 2)

    e_spec = pl.BlockSpec((rows, width), lambda i: (0, i))
    e_grad = pl.BlockSpec((rows, width // 2), half)
    j_spec = pl.BlockSpec((rows, width), lambda i: (0, jnp.minimum(i, 2)))
    j_grad = pl.BlockSpec((1, rows, width), lambda i: (jnp.minimum(i, 2), 0, 0))
    o_spec = pl.BlockSpec((rows // 2, width), lambda i: (jnp.clip(i - 3, 0, 1), 0))
    o_grad = pl.BlockSpec((rows // 2, width), lambda i: (0, 0))
    s_spec = pl.BlockSpec(
        (1, shrink_rows, width), lambda i: (jnp.maximum(i - 4, 0) // 2, jnp.maximum(i - 4, 0) % 2, 0)
    )
    s_grad = pl.BlockSpec((shrink_rows, width), lambda i: (jnp.maximum(i - 4, 0) % 2, 0))
    whole = pl.BlockSpec(squares.shape, lambda i: (0, 0))
    shapes = [jax.ShapeDtypeStruct(p[0].shape, F32) for p in (expand, joint, output, shrink)]
    return pl.pallas_call(
        adam_kernel,
        grid=(8,),
        in_specs=[SM, whole]
        + [e_spec] * 3
        + [e_grad] * 4
        + [j_spec] * 3
        + [j_grad]
        + [o_spec] * 3
        + [o_grad] * 2
        + [s_spec] * 3
        + [s_grad] * 2,
        out_specs=[e_spec] * 3 + [j_spec] * 3 + [o_spec] * 3 + [s_spec] * 3,
        out_shape=[s for s in shapes for _ in range(3)],
        compiler_params=pltpu.CompilerParams(vmem_limit_bytes=60 * MIB),
        name="adam_matrices",
    )(meta, squares, *expand, *joint, *output, *shrink)


def local_cube(
    count,
    tokens,
    depth_count,
    cotangent,
    joint_weight,
    output_weight,
    expand_weight,
    shrink_weight,
    norm_gains,
    joint_mean,
    joint_square,
    output_mean,
    output_square,
    expand_mean,
    expand_square,
    shrink_mean,
    shrink_square,
    gains_mean,
    gains_square,
):
    cube = Cube(count)
    frames, positions, width = tokens.shape
    run = positions // SETS
    group = cube.bit(cube.top)
    core = cube.bit(0)
    upper = group == 1
    second_core = core == 1
    all_frames = 2 * frames
    rows = all_frames * run
    chip = (cube.index >> 1) & (CHIPS - 1)
    meta = jnp.stack([chip, core, group]).astype(jnp.int32)

    def halves(own, other):
        return jnp.concatenate([jnp.where(upper, other, own), jnp.where(upper, own, other)], axis=0)

    def parted(value):
        first, second = value[:, :run], value[:, run:]
        own, other = jnp.where(upper, second, first), jnp.where(upper, first, second)
        return own.reshape(rows // 2, width), other.reshape(rows // 2, width)

    def from_sets(value):
        value = value.reshape(2, frames, run, width)
        own = jnp.where(upper, value[1], value[0])
        other = cube.swap(jnp.where(upper, value[0], value[1]), cube.top)
        first = jnp.where(upper, other, own)
        second = jnp.where(upper, own, other)
        return jnp.concatenate([first, second], axis=1)

    shard_rows = joint_weight.shape[0]
    lane = norm_gains.shape[1]
    small = jnp.concatenate([norm_gains.astype(BF).reshape(-1), depth_count.astype(BF)])
    small_other = cube.swap(small.reshape(1, -1), cube.top)[0]
    depth_all = halves(small[2 * lane :], small_other[2 * lane :]).astype(jnp.int32)
    gain_pair = halves(small[None, : 2 * lane], small_other[None, : 2 * lane])
    gain_pair = gain_pair.reshape(2, 2, lane).transpose(1, 0, 2)
    spread = jnp.broadcast_to(gain_pair[:, :, None, :], (2, 2, 2 * CHIPS, lane)).reshape(2, width)
    mine = (jnp.arange(width) // lane) % (2 * CHIPS) == (cube.index & (2 * CHIPS - 1))
    gain_rows = jnp.pad(jnp.where(mine[None, :], spread, 0), ((0, 14), (0, 0)))
    shards = list(first_shards(joint_weight))
    shards[2] = lax.dynamic_update_slice(shards[2], gain_rows, (shard_rows, 0))
    joint = [Blocks(shard) for shard in shards]
    x_own, x_give = parted(tokens)
    x_got = cube.swap(x_give, cube.top)
    x_rows = halves(x_own, x_got)

    def begin(name):
        return Round(cube, meta, width, name)

    one = begin("pack_one").gather(joint, 0).run(x_give)
    own_cols, give_cols, shrink_keep, shrink_give, out_a, out_b = split_weights(
        meta, expand_weight, shrink_weight, output_weight
    )
    output = [None, Blocks(out_a), Blocks(out_b)]
    joint_other = [Blocks(rows=blocks.rows) for blocks in joint]
    output_other = [None] + [Blocks(rows=blocks.rows) for blocks in output[1:]]
    two = begin("pack_two").gather(joint, 1).gather(output, 0).run(one.got, give_cols)
    shrink_other = cube.swap(after(shrink_give, two.got, x_got), cube.top)
    got_cols = cube.swap(after(give_cols, two.got, x_got), 0)
    three = begin("pack_three").gather(joint, 2).gather(output, 1)
    three = three.core(joint, joint_other, 0, 4).run(two.got, x_got)
    units = Jobs(width)
    unit_rows = 2 * shard_rows
    for kind in range(2):
        target = units.output(2 * unit_rows)
        for turn_index in range(2):
            unit = turn_index * 2 + kind
            base = turn_index * unit_rows
            low, high = (base, base + shard_rows), (base + shard_rows, base)
            units.copy(own_cols, unit * shard_rows, target, low, shard_rows)
            units.copy(got_cols, unit * shard_rows, target, high, shard_rows)
    target = units.output(2 * unit_rows)
    units.copy(shrink_other, 0, target, 0, unit_rows)
    units.copy(shrink_keep, 0, target, unit_rows, unit_rows)
    units = units.run(meta, "expand_units", three.packed)
    part_a = [Blocks(unit, unit_rows) for unit in units]
    part_b = [Blocks(rows=unit_rows) for unit in units]
    for blocks, unit in zip(part_b, units):
        blocks.arrived(unit, unit_rows, 1)

    cot_own, cot_give = parted(cotangent)
    cot_got = cube.swap(after(cot_give, three.packed, shrink_other), cube.top)
    late = begin("pack_late").core(joint, joint_other, 4, 8)
    late = late.run(three.got, three.core_got, units)
    first_units = after(units, three.got, three.core_got)
    got_four = [cube.swap(unit, 1 + axis) for axis, unit in enumerate(first_units)]
    for k in range(3):
        part_a[k].arrived(got_four[k], 0, 1)
        part_b[k].arrived(got_four[k], unit_rows, 1)

    position = group * run + jnp.arange(run)
    live = (position[None, :] < depth_all[:, None]).astype(F32).reshape(rows, 1)

    first, query, key_value, gains_all = joint_forward(meta, x_rows, joint + joint_other)
    key_value_other = cube.swap(after(key_value, cot_got), cube.top)
    five = begin("pack_five").gather(part_a, 1).gather(part_b, 1).run(got_four, key_value, cot_got)
    last = begin("pack_output").gather(output, 2).run(five.packed)
    seven = begin("pack_seven").gather(part_a, 2).core(output, output_other, 0, 8)
    seven = seven.run(five.got, key_value_other, last.got)
    cot_live = (halves(cot_own, after(cot_got, key_value)).astype(F32) * live).astype(BF)
    cot_other = cube.swap(after(cot_live, five.got, key_value_other), 0)

    output_chains = output[1:] + output_other[1:]
    context, middle, second = context_forward(
        run,
        meta,
        query,
        key_value,
        key_value_other,
        x_rows,
        live,
        gains_all,
        output_chains,
    )
    eight = begin("pack_eight").gather(part_b, 2).run(
        seven.packed, seven.core_got, cot_other, gate=(seven.got, second)
    )
    second_other = cube.swap(second, 0)
    row_args = (meta, second, second_other, cot_live, cot_other)
    dn_a, *kept_a = ffn_rows(*row_args, part_a, None)
    f_a, *grad_a = ffn_weights(*row_args, *kept_a, part_a[2], None)
    dn_own, dn_send, *kept_b = ffn_rows(*row_args, part_b, after(dn_a, f_a))
    dn_got = cube.swap(dn_send, 0)
    f_own, f_send, *grad_b = ffn_weights(*row_args, *kept_b, part_b[2], f_a)

    outcome = {}

    def expand_final(key, kind):
        def final(jobs, got, keep, count):
            if key not in outcome:
                outcome[key] = (jobs.output(2 * shard_rows, F32), jobs.output(2 * shard_rows, F32))
            own, give = outcome[key]
            half = count // 2
            for target, offset in ((own, (0, half)), (give, (half, 0))):
                got_at = tuple(got[1] + o for o in offset)
                keep_at = tuple(keep[1] + o for o in offset)
                jobs.add(got[0], got_at, keep[0], keep_at, target, kind * shard_rows, half)

        return final

    def plain_final(key):
        def final(jobs, got, keep, count):
            outcome[key] = jobs.output(count, F32)
            jobs.add(got[0], got[1], keep[0], keep[1], outcome[key], 0, count)

        return final

    def ffn_sums(grads, name):
        finals = (expand_final(name, 0), expand_final(name, 1), plain_final(name + "_shrink"))
        block = grads[0].shape[0] // 4
        return [Sums((grads[2 * k], 0), (grads[2 * k + 1], 0), block, finals[k]) for k in range(3)]

    def turn(name, work, *earlier, **options):
        return reduce_round(cube, meta, width, name, work, *earlier, **options)

    def core_sums(name, tensors, *waits):
        jobs = Jobs(width)
        result = []
        payload = []
        for k in range(3):
            rows_out = sum(4 * c for *_, chains in tensors for kk, c in chains if kk == k)
            payload.append(jobs.output(rows_out))
        filled_rows = [0, 0, 0]
        for key, got, keep, chains in tensors:
            row, sums = 0, [None] * 3
            for k, c in chains:
                own = jobs.output(4 * c)
                send_row = filled_rows[k]
                jobs.add(got, row + 4 * c, keep, row + 4 * c, payload[k], send_row, 4 * c)
                jobs.add(got, row, keep, row, own, 0, 4 * c)
                filled_rows[k] += 4 * c
                sums[k] = (own, send_row, c)
                row += CHIPS * c
            result.append((key, sums))
        out = jobs.run(meta, name, waits=waits)
        made = []
        for key, sums in result:
            made.append(
                [
                    None
                    if s is None
                    else Sums((out[s[0]], 0), (out[payload[k]], s[1]), s[2], plain_final((key, k)))
                    for k, s in enumerate(sums)
                ]
            )
        return made, [out[p] for p in payload]

    shrunk_got = cube.swap(f_send, 0)
    shrunk = f_own + shrunk_got.astype(F32)
    result_rows = (middle + live * shrunk).astype(BF).reshape(2, frames, run, width)
    result_own = jnp.where(upper, result_rows[1], result_rows[0])
    result_give = jnp.where(upper, result_rows[0], result_rows[1])
    result_got = cube.swap(result_give, cube.top)
    result = jnp.concatenate(
        [jnp.where(upper, result_got, result_own), jnp.where(upper, result_own, result_got)], axis=1
    )
    sums_a = ffn_sums(grad_a, "a")
    sums_b = ffn_sums(grad_b, "b")
    turn_one, _ = turn("turn_one", [(sums_a, 0)], eight.got)
    turn_two, _ = turn("turn_two", [(sums_b, 0)], turn_one)

    grad_middle, grad_gain_two, grad_branch, d_query, dkv_own, dkv_give = context_back(
        run,
        meta,
        after(dn_own, result_give, turn_one),
        dn_got,
        middle,
        cot_live,
        live,
        gains_all,
        query,
        key_value,
        key_value_other,
        output_chains,
    )
    turn_three, packed_three = turn(
        "turn_three", [(sums_a, 1), (sums_b, 1)], turn_two, dkv_give, result_got
    )
    dkv_got = cube.swap(dkv_give, cube.top)
    output_give, output_keep = output_grad(meta, context, after(grad_branch, packed_three))
    joint_give, joint_keep, dkv = joint_grad(
        meta, first, d_query, dkv_own, after(dkv_got, output_give)
    )
    turn_four, packed_four = turn(
        "turn_four", [(sums_a, 2), (sums_b, 2)], turn_three, dkv_got, waits=(joint_give,)
    )
    joint_got = cube.swap(after(joint_give, packed_four), 0)
    output_got = cube.swap(after(output_give, packed_four), 0)
    grad_inputs, grad_gain_one = input_back(
        meta,
        d_query,
        after(dkv, packed_four),
        grad_middle,
        x_rows,
        gains_all,
        joint + joint_other,
    )
    half_shard = shard_rows // 2
    (sums_j, sums_o), sends = core_sums(
        "joint_core",
        [
            ("joint", joint_got, joint_keep, [(k, shard_rows) for k in range(3)]),
            ("output", output_got, output_keep, [(k, half_shard) for k in OUTPUT_CHAINS]),
        ],
        grad_inputs,
    )
    turn_seven = []
    for axis in range(3):
        k = (axis - 2) % 3
        array = cube.swap(sends[k], 1 + axis)
        turn_seven.append(array)
        for sums in (sums_j, sums_o):
            if sums[k] is not None:
                sums[k].got = (array, sums[k].send[1])
    gains_term = jnp.concatenate([grad_gain_one, grad_gain_two]).reshape(2, count, -1)
    gains_term = gains_term.transpose(1, 0, 2).reshape(count, -1)
    gains_parts = lax.all_to_all(after(gains_term, sends[0]), "fsdp", 0, 0, tiled=True)
    grad_gains = jnp.sum(gains_parts, axis=0).reshape(2, -1)
    grad_inputs = from_sets(after(grad_inputs, sends[0]))
    _, out_five = turn(
        "turn_five",
        [(sums_a, 3), (sums_b, 3)],
        turn_four,
        sends[0],
        squares=True,
    )
    expand_own_a, expand_give_a = (out_five[i] for i in outcome["a"])
    expand_own_b, expand_give_b = (out_five[i] for i in outcome["b"])
    shrink_first = out_five[outcome["a_shrink"]]
    shrink_mine = out_five[outcome["b_shrink"]]
    expand_got_a = cube.swap(after(expand_give_a, sends[0]), 0)
    expand_got_b = cube.swap(after(expand_give_b, expand_got_a), 0)
    turn_nine, out_nine = turn(
        "turn_nine",
        [(sums_o, 1), (sums_j, 1)],
        turn_seven,
        grad_inputs,
        waits=(grad_gains, out_five[-1]),
    )
    shrink_got = cube.swap(after(shrink_first.astype(BF), out_nine[0]), cube.top)
    turn_ten, out_ten = turn(
        "turn_ten", [(sums_o, 2), (sums_j, 2)], turn_nine, shrink_got
    )
    _, out_last = turn(
        "turn_last",
        [(sums_o, 3), (sums_j, 3)],
        turn_ten,
        squares=True,
        norm=(count, out_five[-1], grad_gains),
    )
    grad_output = [out_last[outcome[("output", k)]] for k in OUTPUT_CHAINS]
    grad_joint = jnp.stack([out_last[outcome[("joint", k)]] for k in range(3)])

    squares = lax.all_to_all(out_last[-1], "fsdp", 0, 0, tiled=True)
    total_sq = jnp.sum(squares[:, 0])
    grad_norm_value = jnp.sqrt(total_sq)
    factor = CLIP_LIMIT / jnp.maximum(grad_norm_value, CLIP_LIMIT)
    new = adam_matrices(
        meta,
        squares,
        (
            expand_weight,
            expand_mean,
            expand_square,
            expand_own_a,
            expand_own_b,
            expand_got_a,
            expand_got_b,
        ),
        (joint_weight, joint_mean, joint_square, grad_joint),
        (output_weight, output_mean, output_square, *grad_output),
        (shrink_weight, shrink_mean, shrink_square, shrink_mine, shrink_got),
    )
    expand_new, joint_new, output_new, shrink_new = (new[i : i + 3] for i in (0, 3, 6, 9))
    gains_new = adam_step(norm_gains, factor * grad_gains, gains_mean, gains_square, GAIN_RATE, 0.0)
    return (
        result,
        grad_inputs,
        grad_norm_value,
        *joint_new,
        *output_new,
        *expand_new,
        *shrink_new,
        *gains_new,
    )


def solution(mesh):
    rows = P("fsdp", None)
    cube = P("fsdp", None, None)
    inner = P(None, "fsdp", None)
    gains = P(None, "fsdp")
    count = mesh.shape["fsdp"]

    def body(*args):
        return (local_cube if count == 4 * CHIPS else local_general)(count, *args)

    return jax.shard_map(
        body,
        mesh=mesh,
        in_specs=(cube, P("fsdp"), cube, rows, rows, rows, inner, gains)
        + (rows,) * 6
        + (inner, inner, gains, gains),
        out_specs=(cube, cube, P()) + (rows,) * 9 + (inner,) * 3 + (gains,) * 3,
        check_vma=False,
    )
```

```python
import functools

import jax
import jax.numpy as jnp
from jax import lax
from jax.experimental import pallas as pl
from jax.experimental.pallas import tpu as pltpu
from jax.sharding import PartitionSpec as P

HEADS = 16
SETS = 2
STEP = 10

NORM_EPS = 1e-05
BETA_ONE = 0.9
BETA_TWO = 0.95
ADAM_EPS = 1e-08
MATRIX_RATE = 0.08
GAIN_RATE = 1.0
MATRIX_DECAY = 0.1
CLIP_LIMIT = 1.0

BF = jnp.bfloat16
F32 = jnp.float32


def dot(a, b):
    return lax.dot_general(a, b, (((1,), (0,)), ((), ())), preferred_element_type=F32)


def dot_nt(a, b):
    return lax.dot_general(a, b, (((1,), (1,)), ((), ())), preferred_element_type=F32)


def dot_tn(a, b):
    return lax.dot_general(a, b, (((0,), (0,)), ((), ())), preferred_element_type=F32)


def adam_step(weight, grad_value, mean_old, square_old, learn_rate, weight_decay):
    mean_new = BETA_ONE * mean_old + (1.0 - BETA_ONE) * grad_value
    square_new = BETA_TWO * square_old + (1.0 - BETA_TWO) * grad_value * grad_value
    mean_hat = mean_new / (1.0 - BETA_ONE**STEP)
    square_hat = square_new / (1.0 - BETA_TWO**STEP)
    weight_new = weight - learn_rate * (
        mean_hat / (jnp.sqrt(square_hat) + ADAM_EPS) + weight_decay * weight
    )
    return (weight_new, mean_new, square_new)


class Cube:
    def __init__(self, count):
        self.count = count
        self.bits = count.bit_length() - 1
        self.top = self.bits - 1
        self.index = lax.axis_index("fsdp")
        chip = list(range(1, self.top))
        third = max(1, len(chip) // 3)
        self.orders = [chip[third * k :] + chip[: third * k] for k in range(3)]

    def bit(self, b):
        return (self.index >> b) & 1

    def swap(self, value, b):
        pairs = [(i, i ^ (1 << b)) for i in range(self.count)]
        return lax.ppermute(value, "fsdp", pairs)

    def gather(self, value, bits, lead=0):
        have = []
        for b in bits:
            other = self.swap(value, b)
            mine = self.bit(b) == 1
            axis = lead + sum(1 for h in have if h > b)
            low = jnp.where(mine, other, value)
            high = jnp.where(mine, value, other)
            value = jnp.stack([low, high], axis=axis)
            have.append(b)
        return value

    def reduce(self, value, have, bits, lead=0, last=F32):
        have = list(have)
        for step, b in enumerate(bits):
            axis = lead + sum(1 for h in have if h > b)
            mine = self.bit(b)
            send = lax.dynamic_index_in_dim(value, 1 - mine, axis, keepdims=False).astype(BF)
            keep = lax.dynamic_index_in_dim(value, mine, axis, keepdims=False)
            other = self.swap(send, b)
            value = keep.astype(F32) + other.astype(F32)
            if step < len(bits) - 1:
                value = value.astype(BF)
            have.remove(b)
        return value.astype(last)

    def total(self, value):
        for b in range(self.bits):
            value = value + self.swap(value, b)
        return value


def cuts(width, parts=3, unit=128):
    units = width // unit
    sizes = [units // parts + (1 if k < units % parts else 0) for k in range(parts)]
    edges = [0]
    for size in sizes:
        edges.append(edges[-1] + size * unit)
    return edges


def local_general(
    count,
    tokens,
    depth_count,
    cotangent,
    joint_weight,
    output_weight,
    expand_weight,
    shrink_weight,
    norm_gains,
    joint_mean,
    joint_square,
    output_mean,
    output_square,
    expand_mean,
    expand_square,
    shrink_mean,
    shrink_square,
    gains_mean,
    gains_square,
):
    cube = Cube(count)
    half = count // 2
    own_bits = cube.top
    frames, positions, width = tokens.shape
    run = positions // SETS
    in_set = cube.bit(cube.top)
    upper = in_set == 1
    all_frames = 2 * frames
    rows = all_frames * run
    hidden_width = expand_weight.shape[1] // 2
    head_dim = width // HEADS

    def to_sets(value):
        first, second = value[:, :run], value[:, run:]
        other = cube.swap(jnp.where(upper, first, second), cube.top)
        own = jnp.where(upper, second, first)
        low = jnp.where(upper, other, own)
        high = jnp.where(upper, own, other)
        return jnp.concatenate([low, high], axis=0)

    def from_sets(value):
        value = value.reshape(2, frames, run, value.shape[-1])
        own = jnp.where(upper, value[1], value[0])
        other = cube.swap(jnp.where(upper, value[0], value[1]), cube.top)
        first = jnp.where(upper, other, own)
        second = jnp.where(upper, own, other)
        return jnp.concatenate([first, second], axis=1)

    position_index = jnp.arange(positions)
    live_here = (position_index[None, :] < depth_count[:, None]).astype(F32)[:, :, None]
    masked = (cotangent.astype(F32) * live_here).astype(BF)

    gains_local = norm_gains.astype(BF)
    gains_all = cube.gather(gains_local, range(cube.bits), lead=1)
    gains_all = gains_all.reshape(2, width).astype(F32)

    def gather_matrix(shard, order, lead=0):
        return cube.gather(shard, list(order) + [0], lead=lead)

    joint_low = joint_weight.astype(BF)
    joint_parts = [
        gather_matrix(joint_low[:, k * width : (k + 1) * width], cube.orders[k]).reshape(width, width)
        for k in range(3)
    ]
    x_rows = to_sets(tokens).reshape(rows, width).astype(F32)
    live = to_sets(live_here).reshape(rows, 1)
    cot = to_sets(masked).reshape(rows, width)

    output_low = output_weight.astype(BF)
    expand_low = expand_weight.astype(BF)
    wide = hidden_width // 4
    edge = [0, wide, (wide + hidden_width) // 2, hidden_width]
    expand_shards = []
    for k in range(3):
        gate_cols = expand_low[:, edge[k] : edge[k + 1]]
        up_cols = expand_low[:, hidden_width + edge[k] : hidden_width + edge[k + 1]]
        parts = ([output_low] if k == 0 else []) + [gate_cols, up_cols]
        expand_shards.append(jnp.concatenate(parts, axis=1))
    expand_parts = [
        gather_matrix(expand_shards[k], cube.orders[k]).reshape(width, -1) for k in range(3)
    ]
    output_full = expand_parts[0][:, :width]
    gate_full = [expand_parts[0][:, width : 2 * width]] + [
        expand_parts[k][:, : edge[k + 1] - edge[k]] for k in (1, 2)
    ]
    up_full = [expand_parts[0][:, 2 * width :]] + [
        expand_parts[k][:, edge[k + 1] - edge[k] :] for k in (1, 2)
    ]

    shrink_low = shrink_weight.astype(BF)
    shrink_mine = jnp.where(upper, shrink_low[1], shrink_low[0])
    shrink_send = jnp.where(upper, shrink_low[0], shrink_low[1])
    shrink_other = cube.swap(shrink_send, cube.top)
    shrink_pair = jnp.stack(
        [jnp.where(upper, shrink_other, shrink_mine), jnp.where(upper, shrink_mine, shrink_other)]
    )
    col = cuts(width)
    shrink_parts = [
        gather_matrix(shrink_pair[:, :, col[k] : col[k + 1]], cube.orders[k], lead=1).reshape(
            hidden_width, -1
        )
        for k in range(3)
    ]

    inv_one = lax.rsqrt(jnp.mean(x_rows * x_rows, axis=-1, keepdims=True) + NORM_EPS)
    first = (x_rows * inv_one * gains_all[0]).astype(BF)
    query, key_own, value_own = [dot(first, joint_parts[k]).astype(BF) for k in range(3)]
    key_value = cube.swap(jnp.concatenate([key_own, value_own], axis=1), cube.top)

    def heads(value):
        return value.reshape(all_frames, run, HEADS, head_dim)

    q_h = heads(query)
    k_h = jnp.concatenate([heads(key_value[:, :width]), heads(key_own)], axis=1)
    v_h = jnp.concatenate([heads(key_value[:, width:]), heads(value_own)], axis=1)
    scale = head_dim ** (-0.5)
    scores = jnp.einsum("fphd,fkhd->fhpk", q_h, k_h, preferred_element_type=F32) * scale
    row = jnp.arange(run)[:, None]
    column = jnp.arange(2 * run)[None, :]
    seen = jnp.where(column < run, upper, row >= column - run)
    scores = jnp.where(seen, scores, -1e30)
    exp_scores = jnp.exp(scores - jnp.max(scores, axis=-1, keepdims=True))
    attention = exp_scores / jnp.sum(exp_scores, axis=-1, keepdims=True)
    attention_low = attention.astype(BF)
    context = (
        jnp.einsum("fhpk,fkhd->fphd", attention_low, v_h, preferred_element_type=F32)
        .reshape(rows, width)
        .astype(BF)
    )
    middle = x_rows + live * dot(context, output_full)
    inv_two = lax.rsqrt(jnp.mean(middle * middle, axis=-1, keepdims=True) + NORM_EPS)
    second = (middle * inv_two * gains_all[1]).astype(BF)
    gate = [dot(second, w) for w in gate_full]
    up = [dot(second, w) for w in up_full]
    hidden = jnp.concatenate(
        [(jax.nn.silu(g) * u).astype(BF) for g, u in zip(gate, up)], axis=1
    )
    shrunk = jnp.concatenate([dot(hidden, w) for w in shrink_parts], axis=1)
    result = from_sets((middle + live * shrunk).astype(BF))

    def reduce_matrix(grad, order, lead=0, block=None):
        bits = list(range(own_bits))
        shape = grad.shape
        if lead:
            grad = grad.reshape((2,) + (2,) * own_bits + (shape[0] // 2 // half, shape[1]))
        else:
            grad = grad.reshape((2,) * own_bits + (shape[0] // half, shape[1]))
        return cube.reduce(grad, bits, [0] + list(order), lead=lead)

    grad_shrink_parts = [
        reduce_matrix(dot_tn(hidden, cot[:, col[k] : col[k + 1]]).astype(BF), cube.orders[k], lead=1)
        for k in range(3)
    ]
    grad_shrink_pair = jnp.concatenate(grad_shrink_parts, axis=-1)
    shrink_keep = jnp.where(upper, grad_shrink_pair[1], grad_shrink_pair[0])
    shrink_give = jnp.where(upper, grad_shrink_pair[0], grad_shrink_pair[1]).astype(BF)
    shrink_got = cube.swap(shrink_give, cube.top).astype(F32)
    grad_shrink = jnp.stack(
        [jnp.where(upper, shrink_got, shrink_keep), jnp.where(upper, shrink_keep, shrink_got)]
    )

    grad_hidden = sum(dot_nt(cot[:, col[k] : col[k + 1]], shrink_parts[k]) for k in range(3))
    grad_second = 0.0
    grad_expand_parts = []
    for k in range(3):
        d_hid = grad_hidden[:, edge[k] : edge[k + 1]]
        sig = jax.nn.sigmoid(gate[k])
        d_gate = (d_hid * up[k] * sig * (1.0 + gate[k] * (1.0 - sig))).astype(BF)
        d_up = (d_hid * gate[k] * sig).astype(BF)
        both = jnp.concatenate([d_gate, d_up], axis=1)
        weight_pair = jnp.concatenate([gate_full[k], up_full[k]], axis=1)
        grad_second = grad_second + dot_nt(both, weight_pair)
        grad_expand_parts.append(
            reduce_matrix(dot_tn(second, both).astype(BF), cube.orders[k])
        )
    grad_expand = jnp.concatenate(
        [grad_expand_parts[k][:, : edge[k + 1] - edge[k]] for k in range(3)]
        + [grad_expand_parts[k][:, edge[k + 1] - edge[k] :] for k in range(3)],
        axis=1,
    )

    def normalize_back(values, inverse, gain_row, grad_out):
        scaled = grad_out * gain_row
        grad_in = inverse * scaled - values * inverse * inverse * inverse * jnp.mean(
            scaled * values, axis=-1, keepdims=True
        )
        return (grad_in, jnp.sum(grad_out * values * inverse, axis=0))

    grad_mid_norm, grad_gain_two = normalize_back(middle, inv_two, gains_all[1], grad_second)
    grad_middle = cot.astype(F32) + grad_mid_norm
    grad_branch = (grad_middle * live).astype(BF)
    grad_context = dot_nt(grad_branch, output_full).astype(BF)

    g_h = heads(grad_context)
    grad_attention = jnp.einsum("fphd,fkhd->fhpk", g_h, v_h, preferred_element_type=F32)
    grad_value = jnp.einsum("fhpk,fphd->fkhd", attention_low, g_h, preferred_element_type=F32)
    grad_scores = attention * (
        grad_attention - jnp.sum(grad_attention * attention, axis=-1, keepdims=True)
    )
    grad_scores = grad_scores.astype(BF)
    grad_query = (
        jnp.einsum("fhpk,fkhd->fphd", grad_scores, k_h, preferred_element_type=F32) * scale
    )
    grad_key = jnp.einsum("fhpk,fphd->fkhd", grad_scores, q_h, preferred_element_type=F32) * scale
    give = jnp.concatenate(
        [grad_key[:, :run].reshape(rows, width), grad_value[:, :run].reshape(rows, width)], axis=1
    ).astype(BF)
    got = cube.swap(give, cube.top).astype(F32)
    got = jnp.where(upper, 0.0, got)
    d_query = grad_query.reshape(rows, width).astype(BF)
    d_key = (grad_key[:, run:].reshape(rows, width) + got[:, :width]).astype(BF)
    d_value = (grad_value[:, run:].reshape(rows, width) + got[:, width:]).astype(BF)

    grad_output = reduce_matrix(dot_tn(context, grad_branch).astype(BF), cube.orders[0])
    joint_grads = [
        reduce_matrix(dot_tn(first, d).astype(BF), cube.orders[k])
        for k, d in enumerate((d_query, d_key, d_value))
    ]
    grad_joint = jnp.concatenate(joint_grads, axis=1)
    grad_first = sum(
        dot_nt(d, w) for d, w in zip((d_query, d_key, d_value), joint_parts)
    )
    grad_in_norm, grad_gain_one = normalize_back(x_rows, inv_one, gains_all[0], grad_first)
    grad_inputs = from_sets((grad_middle + grad_in_norm).astype(BF))

    gains_term = jnp.stack([grad_gain_one, grad_gain_two]).reshape((2,) + (2,) * cube.bits + (-1,))
    bits = list(range(cube.bits))
    have = list(bits)
    for b in bits:
        axis = 1 + sum(1 for h in have if h > b)
        mine = cube.bit(b)
        send = lax.dynamic_index_in_dim(gains_term, 1 - mine, axis, keepdims=False)
        keep = lax.dynamic_index_in_dim(gains_term, mine, axis, keepdims=False)
        gains_term = keep + cube.swap(send, b)
        have.remove(b)
    grad_gains = gains_term

    reduced = (grad_joint, grad_output, grad_expand, grad_shrink, grad_gains)
    local_sq = sum(jnp.sum(g * g) for g in reduced)
    total_sq = cube.total(jnp.broadcast_to(local_sq, (8, 128)))[0, 0]
    grad_norm_value = jnp.sqrt(total_sq)
    factor = CLIP_LIMIT / jnp.maximum(grad_norm_value, CLIP_LIMIT)
    joint_new = adam_step(
        joint_weight, factor * reduced[0], joint_mean, joint_square, MATRIX_RATE, MATRIX_DECAY
    )
    output_new = adam_step(
        output_weight, factor * reduced[1], output_mean, output_square, MATRIX_RATE, MATRIX_DECAY
    )
    expand_new = adam_step(
        expand_weight, factor * reduced[2], expand_mean, expand_square, MATRIX_RATE, MATRIX_DECAY
    )
    shrink_new = adam_step(
        shrink_weight, factor * reduced[3], shrink_mean, shrink_square, MATRIX_RATE, MATRIX_DECAY
    )
    gains_new = adam_step(norm_gains, factor * reduced[4], gains_mean, gains_square, GAIN_RATE, 0.0)
    return (
        result,
        grad_inputs,
        grad_norm_value,
        *joint_new,
        *output_new,
        *expand_new,
        *shrink_new,
        *gains_new,
    )


CHIPS = 8
CHAIN_BITS = [[(k + t) % 3 for t in range(3)] for k in range(3)]
CHAIN_MASKS = [
    [sum(((j >> t) & 1) << bits[t] for t in range(3)) for j in range(CHIPS)] for bits in CHAIN_BITS
]
VM = pl.BlockSpec(memory_space=pltpu.VMEM)
HB = pl.BlockSpec(memory_space=pltpu.HBM)
SM = pl.BlockSpec(memory_space=pltpu.SMEM)
MIB = 1 << 20
SMALL = pl.CostEstimate(flops=1, bytes_accessed=1, transcendentals=0)


def aligned(index, size):
    return pl.ds(pl.multiple_of(index * size, size), size)


def after(value, *earlier):
    return lax.optimization_barrier((value, earlier))[0]


def plus(a, b):
    return (a.astype(F32) + b.astype(F32)).astype(BF)


class Jobs:
    def __init__(self, width):
        self.width = width
        self.inputs, self.outputs, self.work = [], [], []

    def source(self, array):
        for i, known in enumerate(self.inputs):
            if known is array:
                return i
        self.inputs.append(array)
        return len(self.inputs) - 1

    def output(self, rows, dtype=BF):
        self.outputs.append(jax.ShapeDtypeStruct((rows, self.width), dtype))
        return len(self.outputs) - 1

    def copy(self, array, row, target, target_row, count):
        self.work.append((self.source(array), row, None, 0, target, target_row, count))

    def add(self, a, a_row, b, b_row, target, target_row, count):
        self.work.append((self.source(a), a_row, self.source(b), b_row, target, target_row, count))

    def run(self, meta, name, *earlier, squares=False, norm=(), waits=()):
        inputs = after(self.inputs, *earlier) if earlier else self.inputs
        adds = [w for w in self.work if w[2] is not None]
        rows = sum(w[6] for w in adds)
        moved = sum(w[6] for w in self.work if w[2] is None)
        scratch = [pltpu.SemaphoreType.DMA((3, len(self.work)))]
        scratch += [pltpu.VMEM((max(moved, 16), self.width), BF)]
        if adds:
            scratch += [pltpu.VMEM((rows, self.width), BF)] * 3
            scratch += [pltpu.VMEM((rows, self.width), F32)]
        shapes = list(self.outputs)
        if squares:
            shape = (norm[0], 128 + self.width * (len(norm) - 2)) if norm else (8, self.width)
            shapes.append(jax.ShapeDtypeStruct(shape, F32))
        more = list(norm[1:])
        scratch += [pltpu.VMEM((8, self.width), F32)] if squares else []
        return pl.pallas_call(
            functools.partial(
                jobs_kernel, self.work, len(inputs), self.outputs, squares, len(more), len(waits)
            ),
            in_specs=[SM] + [HB] * len(inputs) + [VM] * len(more) + [HB] * len(waits),
            out_specs=[HB] * len(self.outputs) + ([VM] if squares else []),
            out_shape=shapes,
            scratch_shapes=scratch,
            compiler_params=pltpu.CompilerParams(vmem_limit_bytes=60 * MIB),
            cost_estimate=SMALL,
            name=name,
        )(meta, *inputs, *more, *waits)


def jobs_kernel(work, count, outputs, squares, more, waits, meta, *refs):
    sources, norm = refs[:count], refs[count : count + more]
    refs = refs[count + more + waits :]
    targets = refs[: len(outputs)]
    refs = refs[len(outputs) :]
    if squares:
        square_out, square_ref = refs[0], refs[-1]
        refs = refs[1:-1]
    sem = refs[0]
    core = meta[1]

    def part(ref, row, rows):
        if isinstance(row, tuple):
            start = pl.multiple_of(jnp.where(core == 0, row[0], row[1]), 16)
            return ref.at[pl.ds(start, rows)]
        return ref.at[row : row + rows]

    coming, leaving = [], []
    at, moved = 0, 0
    transit = refs[1]
    refs = refs[:1] + refs[2:]
    for i, (a, a_row, b, b_row, target, target_row, rows) in enumerate(work):
        if b is None:
            spot = slice(moved, moved + rows)
            copy = pltpu.make_async_copy(part(sources[a], a_row, rows), transit.at[spot], sem.at[0, i])
            copy.start()
            coming.append(((copy,), spot))
            moved += rows
            continue
        spot = slice(at, at + rows)
        pair = (
            pltpu.make_async_copy(part(sources[a], a_row, rows), refs[1].at[spot], sem.at[0, i]),
            pltpu.make_async_copy(part(sources[b], b_row, rows), refs[2].at[spot], sem.at[1, i]),
        )
        for copy in pair:
            copy.start()
        coming.append((pair, spot))
        at += rows
    if squares:
        square_ref[...] = jnp.zeros_like(square_ref)
    for i, (a, a_row, b, b_row, target, target_row, rows) in enumerate(work):
        pair, spot = coming[i]
        finish(pair)
        if b is None:
            copy = pltpu.make_async_copy(
                transit.at[spot], part(targets[target], target_row, rows), sem.at[2, i]
            )
            copy.start()
            leaving.append(copy)
            continue
        wide = outputs[target].dtype == F32
        store = refs[4] if wide else refs[3]
        if not wide and not squares:
            store[spot] = plus(refs[1][spot], refs[2][spot])
        else:
            total = refs[1][spot].astype(F32) + refs[2][spot].astype(F32)
            store[spot] = total.astype(store.dtype)
            if wide:
                square = (total * total).reshape(rows // 8, 8, total.shape[1])
                square_ref[...] += jnp.sum(square, axis=0)
        copy = pltpu.make_async_copy(
            store.at[spot], part(targets[target], target_row, rows), sem.at[2, i]
        )
        copy.start()
        leaving.append(copy)
    if squares and not norm:
        square_out[...] = square_ref[...]
    if norm:
        total = jnp.sum(square_ref[...]) + jnp.sum(norm[0][...])
        square_out[:, :128] = jnp.full((square_out.shape[0], 128), total, F32)
        for i, ref in enumerate(norm[1:]):
            width = ref.shape[1]
            spot = slice(128 + i * width, 128 + (i + 1) * width)
            square_out[:, spot] = jnp.broadcast_to(ref[...], (square_out.shape[0], width))
    finish(leaving)


class Blocks:
    def __init__(self, own=None, rows=None):
        self.rows = own.shape[0] if rows is None else rows
        self.held = [] if own is None else [(own, 0)]

    def arrived(self, array, row, count):
        for j in range(count):
            self.held.append((array, row + j * self.rows))


def place(jobs, held, rows, target, target_row):
    start = 0
    while start < len(held):
        array, row = held[start]
        stop = start + 1
        while stop < len(held) and held[stop][0] is array and held[stop][1] == row + (stop - start) * rows:
            stop += 1
        jobs.copy(array, row, target, target_row + start * rows, (stop - start) * rows)
        start = stop


class Round:
    def __init__(self, cube, meta, width, name):
        self.cube, self.meta, self.name = cube, meta, name
        self.jobs = Jobs(width)
        self.axis_work = []
        self.core_work = []

    def gather(self, chains, level):
        self.axis_work.append((chains, level))
        return self

    def core(self, chains, others, start, stop):
        self.core_work.append((chains, others, start, stop))
        return self

    def run(self, *earlier, gate=()):
        jobs = self.jobs
        filled = []
        for axis in range(3):
            held = []
            for chains, level in self.axis_work:
                blocks = chains[(axis - level) % 3]
                if blocks is not None:
                    held.append((blocks, blocks.held[: 1 << level]))
            filled.append(held)
        core_held = []
        for chains, others, start, stop in self.core_work:
            for blocks, other in zip(chains, others):
                if blocks is not None:
                    core_held.append((blocks, other, blocks.held[start:stop]))
        direct = not core_held and all(len(h) == 1 and len(h[0][1]) == 1 for h in filled)
        if direct:
            payloads = [h[0][1][0][0] for h in filled]
            if earlier:
                payloads = after(payloads, *earlier)
        else:
            for held in filled:
                if held:
                    target = jobs.output(sum(b.rows * len(h) for b, h in held))
                    row = 0
                    for blocks, part in held:
                        place(jobs, part, blocks.rows, target, row)
                        row += blocks.rows * len(part)
            if core_held:
                target = jobs.output(sum(b.rows * len(h) for b, _, h in core_held))
                row = 0
                for blocks, _, part in core_held:
                    place(jobs, part, blocks.rows, target, row)
                    row += blocks.rows * len(part)
            payloads = jobs.run(self.meta, self.name, *earlier)
            self.packed = payloads
            if gate:
                axes = sum(1 for held in filled if held)
                payloads = after(list(payloads[:axes]), *gate) + list(payloads[axes:])
        got = []
        index = 0
        for axis, held in enumerate(filled):
            if not held:
                continue
            array = self.cube.swap(payloads[index], 1 + axis)
            index += 1
            row = 0
            for blocks, part in held:
                blocks.arrived(array, row, len(part))
                row += blocks.rows * len(part)
            got.append(array)
        self.got = got
        self.core_got = None
        if core_held:
            array = self.cube.swap(payloads[index], 0)
            row = 0
            for blocks, other, part in core_held:
                other.arrived(array, row, len(part))
                row += blocks.rows * len(part)
            self.core_got = array
        self.payloads = payloads
        return self


def operands(*chains):
    arrays, tables = [], []
    for blocks in chains:
        table = []
        for array, row in blocks.held:
            found = [i for i, a in enumerate(arrays) if a is array]
            if not found:
                arrays.append(array)
                found = [len(arrays) - 1]
            table.append((found[0], row))
        tables.append((blocks.rows, table))
    return arrays, tables


class Sums:
    def __init__(self, keep, send, rows, final):
        self.keep, self.send, self.rows, self.count, self.final = keep, send, rows, 4, final


def reduce_round(cube, meta, width, name, work, *earlier, squares=False, gate=(), norm=(), waits=()):
    jobs = Jobs(width)
    filled = []
    direct = all(step == 0 for _, step in work) and len(work) == 1
    for axis in range(3):
        parts = []
        for chains, step in work:
            if step < 3:
                chain = chains[(axis - (2 - step)) % 3]
                if chain is not None:
                    parts.append((chain, step))
        filled.append(parts)
    if direct:
        payloads = [parts[0][0].send[0] for parts in filled]
        if earlier:
            payloads = after(payloads, *earlier)
    else:
        layout = []
        for parts in filled:
            if not parts:
                continue
            rows = 0
            target = None
            sizes = []
            for chain, step in parts:
                size = chain.rows * (4 >> step)
                sizes.append((chain, step, rows, size))
                rows += size
            layout.append((jobs.output(rows), sizes))
        kept = {}
        for target, sizes in layout:
            for chain, step, row, size in sizes:
                if step == 0:
                    jobs.copy(chain.send[0], chain.send[1], target, row, size)
                else:
                    got, got_row = chain.got
                    array, keep_row = chain.keep
                    own = jobs.output(size)
                    jobs.add(got, got_row + size, array, keep_row + size, target, row, size)
                    jobs.add(got, got_row, array, keep_row, own, 0, size)
                    kept[own] = chain
        for chains, step in work:
            if step == 3:
                for chain in chains:
                    if chain is not None:
                        chain.final(jobs, chain.got, chain.keep, chain.rows)
        out = jobs.run(meta, name, *earlier, squares=squares, norm=norm, waits=waits)
        for own, chain in kept.items():
            chain.keep = (out[own], 0)
        payloads = [out[target] for target, _ in layout]
        if gate and payloads:
            payloads = after(payloads, *gate)
    got = []
    index = 0
    for axis, parts in enumerate(filled):
        if not parts:
            continue
        array = cube.swap(payloads[index], 1 + axis)
        index += 1
        row = 0
        for chain, step in parts:
            chain.got = (array, row)
            row += chain.rows * (4 >> step)
        got.append(array)
    return (got, out) if not direct else (got, None)


def first_kernel(joint, q, k, v):
    width = q.shape[1]
    q[...] = joint[:, :width].astype(BF)
    k[...] = joint[:, width : 2 * width].astype(BF)
    v[: joint.shape[0]] = joint[:, 2 * width :].astype(BF)


def first_shards(joint):
    rows, width = joint.shape[0], joint.shape[1] // 3
    return pl.pallas_call(
        first_kernel,
        in_specs=[VM],
        out_specs=[VM] * 3,
        out_shape=[jax.ShapeDtypeStruct((r, width), BF) for r in (rows, rows, rows + 16)],
        compiler_params=pltpu.CompilerParams(vmem_limit_bytes=60 * MIB),
        name="first_shards",
    )(joint)


def split_kernel(meta, expand, shrink, output, own, give, shrink_own, shrink_give, out_a, out_b):
    core, group = meta[1], meta[2]
    rows = expand.shape[0]
    block = expand.shape[1] // (2 * 2 * 2 * CHIPS)
    for turn in range(2):
        part = turn ^ (1 - group)
        for kind in range(2):
            for chip in range(CHIPS):
                base = ((kind * 2 + part) * CHIPS + chip) * 2
                cols = slice(chip * block, (chip + 1) * block)
                r = slice((turn * 2 + kind) * rows, (turn * 2 + kind + 1) * rows)
                own[r, cols] = expand[:, aligned(base + core, block)].astype(BF)
                give[r, cols] = expand[:, aligned(base + 1 - core, block)].astype(BF)
    shrink_own[...] = shrink[group].astype(BF)
    shrink_give[...] = shrink[1 - group].astype(BF)
    out_a[...] = output[: rows // 2].astype(BF)
    out_b[...] = output[rows // 2 :].astype(BF)


def split_weights(meta, expand, shrink, output):
    rows, width = output.shape
    four = jax.ShapeDtypeStruct((4 * rows, width), BF)
    two = jax.ShapeDtypeStruct(shrink.shape[1:], BF)
    half = jax.ShapeDtypeStruct((rows // 2, width), BF)
    return pl.pallas_call(
        split_kernel,
        in_specs=[SM, VM, VM, VM],
        out_specs=[VM] * 6,
        out_shape=[four, four, two, two, half, half],
        compiler_params=pltpu.CompilerParams(vmem_limit_bytes=60 * MIB),
        name="split_weights",
    )(meta, expand, shrink, output)


def load_blocks(table, refs, w, k, chip, sem):
    copies = []
    rows, places = table
    for j, (index, row) in enumerate(places):
        target = w.at[aligned(chip ^ CHAIN_MASKS[k][j], rows), :]
        copy = pltpu.make_async_copy(refs[index].at[row : row + rows], target, sem.at[j])
        copy.start()
        copies.append(copy)
    return copies


def store_blocks(w, pieces, rows, k, chip, sem):
    copies = []
    for j in range(CHIPS):
        source = w.at[aligned(chip ^ CHAIN_MASKS[k][j], rows), :]
        row = (j % 4) * rows
        copy = pltpu.make_async_copy(source, pieces[j // 4].at[row : row + rows], sem.at[j])
        copy.start()
        copies.append(copy)
    return copies


def finish(copies):
    for copy in copies:
        copy.wait()


TILE = 256


def ffn_rows_kernel(first, count, tables, meta, n2m, n2o, cm, co, *refs):
    pieces = refs[:count]
    refs = refs[count:]
    if not first:
        dn_in = refs[0]
        refs = refs[1:]
    if first:
        dn_out, hid, dg, du, n2, c, wg, wu, ws, sem = refs
    else:
        dn_out, dn_send, hid, dg, du, n2, c, wg, wu, ws, sem = refs
    chip = meta[0]
    mats = (wg, wu, ws)
    coming = [load_blocks(tables[k], pieces, mats[k], k, chip, sem.at[k]) for k in range(3)]
    rows = n2m.shape[0]
    n2[:rows] = n2m[...]
    n2[rows:] = n2o[...]
    c[:rows] = cm[...]
    c[rows:] = co[...]
    for copies in coming:
        finish(copies)
    width = wg.shape[1]

    def gates(t, _):
        cols = aligned(t, TILE)
        g = dot(n2[...], wg[:, cols])
        u = dot(n2[...], wu[:, cols])
        dh = dot_nt(c[...], ws[cols, :])
        sig = jax.nn.sigmoid(g)
        silu = g * sig
        hid[:, cols] = (silu * u).astype(BF)
        du[:, cols] = (dh * silu).astype(BF)
        dg[:, cols] = (dh * u * sig * (1.0 + g * (1.0 - sig))).astype(BF)
        return 0

    lax.fori_loop(0, width // TILE, gates, 0, unroll=True)

    def back(t, _):
        cols = aligned(t, TILE)
        d = dot_nt(dg[...], wg[cols, :]) + dot_nt(du[...], wu[cols, :])
        if first:
            dn_out[:, cols] = d
        else:
            d = d + dn_in[:, cols]
            dn_out[:, cols] = d[:rows]
            dn_send[:, cols] = d[rows:]
        return 0

    lax.fori_loop(0, width // TILE, back, 0, unroll=True)


def ffn_rows(meta, n2m, n2o, cm, co, chains, carried):
    first = carried is None
    arrays, tables = operands(*chains)
    rows, width = 2 * n2m.shape[0], n2m.shape[1]
    low = jax.ShapeDtypeStruct((rows, width), BF)
    return pl.pallas_call(
        functools.partial(ffn_rows_kernel, first, len(arrays), tables),
        in_specs=[SM] + [VM] * 4 + [HB] * len(arrays) + ([] if first else [VM]),
        out_specs=[VM] * (4 if first else 5),
        out_shape=(
            [jax.ShapeDtypeStruct((rows, width), F32)]
            if first
            else [jax.ShapeDtypeStruct((rows // 2, width), F32)] * 2
        )
        + [low, low, low],
        scratch_shapes=[pltpu.VMEM((rows, width), BF)] * 2
        + [pltpu.VMEM((width, width), BF)] * 3
        + [pltpu.SemaphoreType.DMA((3, CHIPS))],
        compiler_params=pltpu.CompilerParams(vmem_limit_bytes=60 * MIB),
        cost_estimate=SMALL,
        name="ffn_rows",
    )(meta, n2m, n2o, cm, co, *arrays, *(() if first else (carried,)))


def ffn_weights_kernel(first, count, table, meta, n2m, n2o, cm, co, hid, dg, du, *refs):
    pieces = refs[:count]
    refs = refs[count:]
    if not first:
        f_in = refs[0]
        refs = refs[1:]
    f_out = refs[0]
    if not first:
        f_send = refs[1]
        refs = refs[1:]
    outs = refs[1:7]
    n2, c, ws, dwg, dwu, dws, in_sem, out_sem = refs[7:]
    chip = meta[0]
    coming = load_blocks(table, pieces, ws, 2, chip, in_sem)
    rows = n2m.shape[0]
    n2[:rows] = n2m[...]
    n2[rows:] = n2o[...]
    c[:rows] = cm[...]
    c[rows:] = co[...]
    width = ws.shape[1]
    leaving = []
    for k, (lhs, rhs, dw) in enumerate(((n2, dg, dwg), (n2, du, dwu), (hid, c, dws))):

        def step(t, _, lhs=lhs, rhs=rhs, dw=dw):
            cols = aligned(t, TILE)
            dw[cols, :] = dot_tn(lhs[:, cols], rhs[...]).astype(BF)
            return 0

        lax.fori_loop(0, width // TILE, step, 0, unroll=True)
        leaving += store_blocks(dw, outs[2 * k : 2 * k + 2], table[0], k, chip, out_sem.at[k])
    finish(coming)

    def down(t, _):
        cols = aligned(t, TILE)
        f = dot(hid[...], ws[:, cols])
        if first:
            f_out[:, cols] = f
        else:
            f = f + f_in[:, cols]
            f_out[:, cols] = f[:rows]
            f_send[:, cols] = f[rows:].astype(BF)
        return 0

    lax.fori_loop(0, width // TILE, down, 0, unroll=True)
    finish(leaving)


def ffn_weights(meta, n2m, n2o, cm, co, hid, dg, du, chain, carried):
    first = carried is None
    arrays, tables = operands(chain)
    rows, width = 2 * n2m.shape[0], n2m.shape[1]
    piece = jax.ShapeDtypeStruct((4 * chain.rows, width), BF)
    return pl.pallas_call(
        functools.partial(ffn_weights_kernel, first, len(arrays), tables[0]),
        in_specs=[SM] + [VM] * 7 + [HB] * len(arrays) + ([] if first else [VM]),
        out_specs=[VM] * (1 if first else 2) + [HB] * 6,
        out_shape=(
            [jax.ShapeDtypeStruct((rows, width), F32)]
            if first
            else [
                jax.ShapeDtypeStruct((rows // 2, width), F32),
                jax.ShapeDtypeStruct((rows // 2, width), BF),
            ]
        )
        + [piece] * 6,
        scratch_shapes=[pltpu.VMEM((rows, width), BF)] * 2
        + [pltpu.VMEM((width, width), BF)] * 4
        + [pltpu.SemaphoreType.DMA((CHIPS,)), pltpu.SemaphoreType.DMA((3, CHIPS))],
        compiler_params=pltpu.CompilerParams(vmem_limit_bytes=60 * MIB),
        cost_estimate=SMALL,
        name="ffn_weights",
    )(meta, n2m, n2o, cm, co, hid, dg, du, *arrays, *(() if first else (carried,)))


OUTPUT_CHAINS = (1, 2)


def load_devices(table, refs, k, side, shard, row, count, target, lo, meta, sem, used):
    chip, core = meta[0], meta[1]
    copies = []
    for j, (index, base) in enumerate(table[1]):
        device = (chip ^ CHAIN_MASKS[k][j]) * 2 + (core if side == 0 else 1 - core)
        start = pl.multiple_of(device * shard + row, 16)
        copy = pltpu.make_async_copy(
            refs[index].at[base : base + count],
            target.at[pl.ds(start, count), lo : lo + target.shape[0]],
            sem.at[used + j],
        )
        copy.start()
        copies.append(copy)
    return copies


def load_joint(tables, refs, target, meta, sem):
    width = target.shape[0]
    shard = width // (2 * CHIPS)
    copies = []
    for k in range(3):
        for side in range(2):
            copies += load_devices(
                tables[3 * side + k], refs, k, side, shard, 0, shard, target, k * width, meta, sem, len(copies)
            )
    return copies


def load_output(tables, refs, target, meta, sem):
    shard = target.shape[0] // (2 * CHIPS)
    half = shard // 2
    copies = []
    for i, k in enumerate(OUTPUT_CHAINS):
        for side in range(2):
            copies += load_devices(
                tables[2 * side + i], refs, k, side, shard, i * half, half, target, 0, meta, sem, len(copies)
            )
    return copies


PAIR_COPIES = 128
PAD = 16


def joint_kernel(count, tables, meta, x, *refs):
    pieces = refs[:count]
    first, query, pair, gains, w, gain_rows, sem, gain_sem = refs[count:]
    width = x.shape[1]
    coming = load_joint(tables, pieces, w, meta, sem)
    shard = width // (2 * CHIPS)
    gain_copies = []
    for side in range(2):
        for j, (index, base) in enumerate(tables[3 * side + 2][1]):
            copy = pltpu.make_async_copy(
                pieces[index].at[base + shard : base + shard + 16],
                gain_rows.at[side * CHIPS + j],
                gain_sem.at[side * CHIPS + j],
            )
            copy.start()
            gain_copies.append(copy)
    value = x[...].astype(F32)
    inverse = lax.rsqrt(jnp.mean(value * value, axis=-1, keepdims=True) + NORM_EPS)
    finish(gain_copies)
    whole = jnp.sum(gain_rows[...].astype(F32), axis=0)
    gains[...] = whole[:8]
    first[...] = (value * inverse * whole[0:1]).astype(BF)
    finish(coming)
    tiles = width // TILE
    rows = x.shape[0]
    pair[2 * rows :] = jnp.zeros((PAD, width), BF)
    for part, (out, low) in enumerate(((query, 0), (pair, 0), (pair, rows))):

        def step(t, _, part=part, out=out, low=low):
            weight = w[:, aligned(t + part * tiles, TILE)]
            out[low : low + rows, aligned(t, TILE)] = dot(first[...], weight).astype(BF)
            return 0

        lax.fori_loop(0, tiles, step, 0, unroll=True)


def joint_forward(meta, x, chains):
    rows, width = x.shape
    arrays, tables = operands(*chains)
    low = jax.ShapeDtypeStruct((rows, width), BF)
    return pl.pallas_call(
        functools.partial(joint_kernel, len(arrays), tables),
        in_specs=[SM, VM] + [HB] * len(arrays),
        out_specs=[VM] * 4,
        out_shape=[
            low,
            low,
            jax.ShapeDtypeStruct((2 * rows + PAD, width), BF),
            jax.ShapeDtypeStruct((8, width), F32),
        ],
        scratch_shapes=[
            pltpu.VMEM((width, 3 * width), BF),
            pltpu.VMEM((2 * CHIPS, 16, width), BF),
            pltpu.SemaphoreType.DMA((PAIR_COPIES,)),
            pltpu.SemaphoreType.DMA((2 * CHIPS,)),
        ],
        compiler_params=pltpu.CompilerParams(vmem_limit_bytes=60 * MIB),
        cost_estimate=SMALL,
        name="joint_forward",
    )(meta, x, *arrays)


CHUNK = 128


def bias_into(bias, run, upper):
    size = 2 * CHUNK
    row = lax.broadcasted_iota(jnp.int32, (size, size), 0) & (CHUNK - 1)
    column = lax.broadcasted_iota(jnp.int32, (size, size), 1)
    own = column < CHUNK
    column = column & (CHUNK - 1)
    shift = run.bit_length() - 1
    same = (row >> shift) == (column >> shift)
    reach = jnp.where(upper, CHUNK, 0)
    seen = same & ((own & (row >= column)) | (~own & (row < reach)))
    bias[...] = jnp.where(seen, 0.0, -1e30)


def stacked(value, left):
    zero = jnp.zeros_like(value)
    return jnp.concatenate([jnp.where(left, value, zero), jnp.where(left, zero, value)], axis=0)


def probabilities(q_st, k_all, bias, scale):
    scores = dot_nt(q_st, k_all) * scale + bias[...]
    exp_scores = jnp.exp(scores - jnp.max(scores, axis=-1, keepdims=True))
    return exp_scores / jnp.sum(exp_scores, axis=-1, keepdims=True)


def context_kernel(run, head_dim, count, tables, meta, query, own, other, x, live, gains, *refs):
    pieces = refs[:count]
    ctx, h_out, n2, wo, bias, sem = refs[count:]
    rows, width = x.shape
    coming = load_output(tables, pieces, wo, meta, sem)
    bias_into(bias, run, meta[2] == 1)
    scale = head_dim ** (-0.5)
    lanes = 2 * head_dim
    left = lax.broadcasted_iota(jnp.int32, (CHUNK, lanes), 1) < head_dim

    def pair(p, _):
        cols = aligned(p, lanes)
        for chunk in range(rows // CHUNK):
            r = slice(chunk * CHUNK, (chunk + 1) * CHUNK)
            r_v = slice(rows + chunk * CHUNK, rows + (chunk + 1) * CHUNK)
            q_st = stacked(query[r, cols], left)
            k_all = jnp.concatenate([own[r, cols], other[r, cols]], axis=0)
            v_all = jnp.concatenate([own[r_v, cols], other[r_v, cols]], axis=0)
            prob = probabilities(q_st, k_all, bias, scale)
            out = dot(prob.astype(BF), v_all)
            ctx[r, cols] = jnp.where(left, out[:CHUNK], out[CHUNK:]).astype(BF)
        return 0

    lax.fori_loop(0, width // lanes, pair, 0)
    finish(coming)

    def project(t, _):
        cols = aligned(t, TILE)
        h_out[:, cols] = x[:, cols].astype(F32) + live[...] * dot(ctx[...], wo[:, cols])
        return 0

    lax.fori_loop(0, width // TILE, project, 0, unroll=True)
    h = h_out[...]
    inverse = lax.rsqrt(jnp.mean(h * h, axis=-1, keepdims=True) + NORM_EPS)
    n2[...] = (h * inverse * gains[1:2, :]).astype(BF)


def context_forward(
    run, meta, query, own, other, x, live, gains, chains
):
    rows, width = x.shape
    arrays, tables = operands(*chains)
    low = jax.ShapeDtypeStruct((rows, width), BF)
    return pl.pallas_call(
        functools.partial(context_kernel, run, width // HEADS, len(arrays), tables),
        in_specs=[SM] + [VM] * 6 + [HB] * len(arrays),
        out_specs=[VM] * 3,
        out_shape=[low, jax.ShapeDtypeStruct((rows, width), F32), low],
        scratch_shapes=[
            pltpu.VMEM((width, width), BF),
            pltpu.VMEM((2 * CHUNK, 2 * CHUNK), F32),
            pltpu.SemaphoreType.DMA((PAIR_COPIES,)),
        ],
        compiler_params=pltpu.CompilerParams(vmem_limit_bytes=60 * MIB),
        cost_estimate=SMALL,
        name="context_forward",
    )(meta, query, own, other, x, live, gains, *arrays)


def norm_back(value, gain, grad):
    inverse = lax.rsqrt(jnp.mean(value * value, axis=-1, keepdims=True) + NORM_EPS)
    scaled = grad * gain
    mean = jnp.mean(scaled * value, axis=-1, keepdims=True)
    grad_in = inverse * scaled - value * (inverse * inverse * inverse) * mean
    return grad_in, jnp.sum(grad * value * inverse, axis=0, keepdims=True)


def context_back_kernel(
    run, head_dim, count, tables, meta, dn_own, dn_got, h, cot, live, gains, query, *refs
):
    own, other = refs[:2]
    pieces = refs[2 : 2 + count]
    dh, dg2, da, dq, dkv, give, wo, bias, dctx, sem = refs[2 + count :]
    rows, width = h.shape
    coming = load_output(tables, pieces, wo, meta, sem)
    bias_into(bias, run, meta[2] == 1)
    give[2 * rows :] = jnp.zeros((PAD, width), BF)
    grad_in, dg2[...] = norm_back(h[...], gains[1:2, :], dn_own[...] + dn_got[...])
    grad = cot[...].astype(F32) + grad_in
    dh[...] = grad
    da[...] = (grad * live[...]).astype(BF)
    finish(coming)

    def project(t, _):
        cols = aligned(t, TILE)
        dctx[:, cols] = dot_nt(da[...], wo[cols, :]).astype(BF)
        return 0

    lax.fori_loop(0, width // TILE, project, 0, unroll=True)
    scale = head_dim ** (-0.5)
    lanes = 2 * head_dim
    pairs = width // lanes
    left = lax.broadcasted_iota(jnp.int32, (CHUNK, lanes), 1) < head_dim

    def pair(p, _):
        cols = aligned(p, lanes)
        v_cols = aligned(p + pairs, lanes)
        for chunk in range(rows // CHUNK):
            r = slice(chunk * CHUNK, (chunk + 1) * CHUNK)
            r_v = slice(rows + chunk * CHUNK, rows + (chunk + 1) * CHUNK)
            q_st = stacked(query[r, cols], left)
            g_st = stacked(dctx[r, cols], left)
            k_all = jnp.concatenate([own[r, cols], other[r, cols]], axis=0)
            v_all = jnp.concatenate([own[r_v, cols], other[r_v, cols]], axis=0)
            prob = probabilities(q_st, k_all, bias, scale)
            d_prob = dot_nt(g_st, v_all)
            d_score = prob * (d_prob - jnp.sum(d_prob * prob, axis=-1, keepdims=True))
            d_score = d_score.astype(BF)
            d_query = dot(d_score, k_all) * scale
            d_key = dot_tn(d_score, q_st) * scale
            d_value = dot_tn(prob.astype(BF), g_st)
            dq[r, cols] = jnp.where(left, d_query[:CHUNK], d_query[CHUNK:]).astype(BF)
            dkv[r, cols] = d_key[:CHUNK]
            dkv[r, v_cols] = d_value[:CHUNK]
            give[r, cols] = d_key[CHUNK:].astype(BF)
            give[r_v, cols] = d_value[CHUNK:].astype(BF)
        return 0

    lax.fori_loop(0, pairs, pair, 0)


def context_back(
    run, meta, dn_own, dn_got, h, cot, live, gains, query, own, other, chains
):
    rows, width = h.shape
    arrays, tables = operands(*chains)
    low = jax.ShapeDtypeStruct((rows, width), BF)
    return pl.pallas_call(
        functools.partial(context_back_kernel, run, width // HEADS, len(arrays), tables),
        in_specs=[SM] + [VM] * 9 + [HB] * len(arrays),
        out_specs=[VM] * 6,
        out_shape=[
            jax.ShapeDtypeStruct((rows, width), F32),
            jax.ShapeDtypeStruct((1, width), F32),
            low,
            low,
            jax.ShapeDtypeStruct((rows, 2 * width), F32),
            jax.ShapeDtypeStruct((2 * rows + PAD, width), BF),
        ],
        scratch_shapes=[
            pltpu.VMEM((width, width), BF),
            pltpu.VMEM((2 * CHUNK, 2 * CHUNK), F32),
            pltpu.VMEM((rows, width), BF),
            pltpu.SemaphoreType.DMA((PAIR_COPIES,)),
        ],
        compiler_params=pltpu.CompilerParams(vmem_limit_bytes=60 * MIB),
        cost_estimate=SMALL,
        name="context_back",
    )(
        meta,
        dn_own,
        dn_got,
        h,
        cot,
        live,
        gains,
        query,
        own,
        other,
        *arrays,
    )


def shard_grads(lhs, rhs_cols, dw):
    width = lhs.shape[1]
    for i, rhs in enumerate(rhs_cols):

        def step(t, _, rhs=rhs, i=i):
            cols = aligned(t, TILE)
            dw[i, cols, :] = dot_tn(lhs[:, cols], rhs()).astype(BF)
            return 0

        lax.fori_loop(0, width // TILE, step, 0, unroll=True)


def store_devices(dw, matrix, row, count, k, targets, base, meta, sem, used):
    chip, core = meta[0], meta[1]
    shard = dw.shape[1] // (2 * CHIPS)
    copies = []
    for side, target in enumerate(targets):
        for j in range(CHIPS):
            device = (chip ^ CHAIN_MASKS[k][j]) * 2 + (1 - core if side == 0 else core)
            start = pl.multiple_of(device * shard + row, 16)
            low = base + j * count
            copy = pltpu.make_async_copy(
                dw.at[matrix, pl.ds(start, count), :],
                target.at[low : low + count],
                sem.at[used + len(copies)],
            )
            copy.start()
            copies.append(copy)
    return copies


def output_grad_kernel(meta, context, grad, give, keep, dw, sem):
    shard_grads(context, (lambda: grad[...],), dw)
    half = dw.shape[1] // (4 * CHIPS)
    leaving = []
    for i, k in enumerate(OUTPUT_CHAINS):
        base = i * CHIPS * half
        leaving += store_devices(
            dw, 0, i * half, half, k, (give, keep), base, meta, sem, len(leaving)
        )
    finish(leaving)


def output_grad(meta, context, grad):
    rows, width = context.shape
    part = jax.ShapeDtypeStruct((width // 2, width), BF)
    return pl.pallas_call(
        output_grad_kernel,
        in_specs=[SM, VM, VM],
        out_specs=[HB, HB],
        out_shape=[part, part],
        scratch_shapes=[
            pltpu.VMEM((1, width, width), BF),
            pltpu.SemaphoreType.DMA((PAIR_COPIES,)),
        ],
        compiler_params=pltpu.CompilerParams(vmem_limit_bytes=60 * MIB),
        cost_estimate=SMALL,
        name="output_grad",
    )(meta, context, grad)


def joint_grad_kernel(meta, first, dq, dkv_own, dkv_got, give, keep, dkv):
    width = first.shape[1]
    rows = first.shape[0]
    chip, core = meta[0], meta[1]
    for part in range(2):
        cols = slice(part * width, (part + 1) * width)
        got = dkv_got[part * rows : (part + 1) * rows, :]
        more = jnp.where(meta[2] == 1, 0.0, got.astype(F32))
        dkv[:, cols] = (dkv_own[:, cols] + more).astype(BF)
    rights = (lambda: dq[...], lambda: dkv[:, :width], lambda: dkv[:, width:])
    shard = width // (2 * CHIPS)
    for k in range(3):
        for j in range(CHIPS):
            grad = dot_tn(first[:, aligned(chip ^ CHAIN_MASKS[k][j], 2 * shard)], rights[k]())
            low, high = grad[:shard].astype(BF), grad[shard:].astype(BF)
            at = slice((k * CHIPS + j) * shard, (k * CHIPS + j + 1) * shard)
            give[at] = jnp.where(core == 0, high, low)
            keep[at] = jnp.where(core == 0, low, high)


def joint_grad(meta, first, dq, dkv_own, dkv_got):
    rows, width = first.shape
    part = jax.ShapeDtypeStruct((3 * width // 2, width), BF)
    return pl.pallas_call(
        joint_grad_kernel,
        in_specs=[SM] + [VM] * 4,
        out_specs=[VM] * 3,
        out_shape=[part, part, jax.ShapeDtypeStruct((rows, 2 * width), BF)],
        compiler_params=pltpu.CompilerParams(vmem_limit_bytes=60 * MIB),
        cost_estimate=SMALL,
        name="joint_grad",
    )(meta, first, dq, dkv_own, dkv_got)


def input_back_kernel(count, tables, meta, dq, dkv, dh, x, gains, *refs):
    pieces = refs[:count]
    out, dg1, w, dn, sem = refs[count:]
    rows, width = x.shape
    finish(load_joint(tables, pieces, w, meta, sem))

    def step(t, _):
        cols = aligned(t, TILE)
        dn[:, cols] = dot_nt(dq[...], w[cols, :width]) + dot_nt(dkv[...], w[cols, width:])
        return 0

    lax.fori_loop(0, width // TILE, step, 0, unroll=True)
    grad_in, dg1[...] = norm_back(x[...].astype(F32), gains[0:1, :], dn[...])
    out[...] = (dh[...] + grad_in).astype(BF)


def input_back(meta, dq, dkv, dh, x, gains, chains):
    rows, width = x.shape
    arrays, tables = operands(*chains)
    return pl.pallas_call(
        functools.partial(input_back_kernel, len(arrays), tables),
        in_specs=[SM] + [VM] * 5 + [HB] * len(arrays),
        out_specs=[VM, VM],
        out_shape=[
            jax.ShapeDtypeStruct((rows, width), BF),
            jax.ShapeDtypeStruct((1, width), F32),
        ],
        scratch_shapes=[
            pltpu.VMEM((width, 3 * width), BF),
            pltpu.VMEM((rows, width), F32),
            pltpu.SemaphoreType.DMA((PAIR_COPIES,)),
        ],
        compiler_params=pltpu.CompilerParams(vmem_limit_bytes=60 * MIB),
        cost_estimate=SMALL,
        name="input_back",
    )(meta, dq, dkv, dh, x, gains, *arrays)


def adam_in_place(k, w, m, v, grad, where, rate, decay):
    grad = k * grad
    mean = BETA_ONE * m[where] + (1.0 - BETA_ONE) * grad
    square = BETA_TWO * v[where] + (1.0 - BETA_TWO) * grad * grad
    root = jnp.sqrt(square * (1.0 / (1.0 - BETA_TWO**STEP))) + ADAM_EPS
    old = w[where]
    move = mean * (rate / (1.0 - BETA_ONE**STEP)) / root
    w[where] = old - (move + (rate * decay) * old)
    m[where] = mean
    v[where] = square


def adam_kernel(meta, squares, *refs):
    sources, targets, held = refs[:21], refs[21:33], refs[33:54]
    in_sem, out_sem = refs[54:]
    core, group = meta[1], meta[2]
    (ew, em, ev, own_a, own_b, got_a, got_b, jw, jm, jv, jg, ow, om, ov, og_a, og_b) = held[:16]
    (sw, sm, sv, sg_mine, sg_got) = held[16:]
    width = own_a.shape[1]
    rows = ew.shape[0]
    started = []

    def load(index, where):
        copy = pltpu.make_async_copy(
            sources[index].at[where], held[index].at[where], in_sem.at[len(started)]
        )
        copy.start()
        started.append(copy)
        return copy

    def whole(ref):
        return (slice(None),) * len(ref.shape)

    pieces = []
    gradients = [load(i, whole(held[i])) for i in (3, 4, 5, 6)]
    for c in range(ew.shape[1] // width):
        where = (slice(None), slice(c * width, (c + 1) * width))
        pieces.append(("expand", c, where, [load(i, where) for i in (0, 1, 2)]))
    for c in range(jw.shape[1] // width):
        where = (slice(None), slice(c * width, (c + 1) * width))
        copies = [load(10, (c,))] + [load(i, where) for i in (7, 8, 9)]
        pieces.append(("joint", c, where, copies))
    copies = [load(i, whole(held[i])) for i in (14, 15, 11, 12, 13)]
    pieces.append(("output", 0, None, copies))
    more = [load(i, whole(held[i])) for i in (19, 20)]
    for c in range(sw.shape[0]):
        pieces.append(("shrink", c, (c,), (more if c == 0 else []) + [load(i, (c,)) for i in (16, 17, 18)]))

    sums = jnp.sum(squares[...], axis=0, keepdims=True)
    total = sums[:, 0:1] + jnp.sum(sums[:, 128:] * sums[:, 128:], axis=1, keepdims=True)
    k = CLIP_LIMIT / jnp.maximum(jnp.sqrt(total), CLIP_LIMIT)
    finish(gradients)
    leaving = []

    def store(target, index, where):
        copy = pltpu.make_async_copy(
            held[index].at[where], targets[target].at[where], out_sem.at[len(leaving)]
        )
        copy.start()
        leaving.append(copy)

    block = width // CHIPS
    for kind, c, where, copies in pieces:
        finish(copies)
        if kind == "expand":
            turn = ((c // 2) % 2) ^ (1 - group)
            r = slice((c // 4) * rows, (c // 4 + 1) * rows)
            for q in range(CHIPS):
                near = (c % 2) * (CHIPS // 2) + q // 2
                near = (r, slice(near * block, (near + 1) * block))
                own = jnp.where(turn == 0, own_a[near], own_b[near])
                got = jnp.where(turn == 0, got_a[near], got_b[near])
                grad = jnp.where(core == q % 2, own, got)
                cols = (slice(None), slice(c * width + q * block, c * width + (q + 1) * block))
                adam_in_place(k, ew, em, ev, grad, cols, MATRIX_RATE, MATRIX_DECAY)
            for i in range(3):
                store(i, i, where)
        elif kind == "joint":
            adam_in_place(k, jw, jm, jv, jg[c], where, MATRIX_RATE, MATRIX_DECAY)
            for i in range(3):
                store(3 + i, 7 + i, where)
        elif kind == "output":
            half = og_a.shape[0]
            for part, grad in enumerate((og_a, og_b)):
                at = (slice(part * half, (part + 1) * half),)
                adam_in_place(k, ow, om, ov, grad[...], at, MATRIX_RATE, MATRIX_DECAY)
            for i in range(3):
                store(6 + i, 11 + i, whole(ow))
        else:
            grad = jnp.where(group == c, sg_mine[...], sg_got[...].astype(F32))
            adam_in_place(k, sw, sm, sv, grad, where, MATRIX_RATE, MATRIX_DECAY)
            for i in range(3):
                store(9 + i, 16 + i, where)
    finish(leaving)


def adam_matrices(meta, squares, expand, joint, output, shrink):
    arrays = (*expand, *joint, *output, *shrink)
    shapes = [jax.ShapeDtypeStruct(p[0].shape, F32) for p in (expand, joint, output, shrink)]
    return pl.pallas_call(
        adam_kernel,
        in_specs=[SM, VM] + [HB] * len(arrays),
        out_specs=[HB] * 12,
        out_shape=[s for s in shapes for _ in range(3)],
        scratch_shapes=[pltpu.VMEM(a.shape, a.dtype) for a in arrays]
        + [pltpu.SemaphoreType.DMA((64,)), pltpu.SemaphoreType.DMA((64,))],
        compiler_params=pltpu.CompilerParams(vmem_limit_bytes=60 * MIB),
        cost_estimate=SMALL,
        name="adam_matrices",
    )(meta, squares, *arrays)


def local_cube(
    count,
    tokens,
    depth_count,
    cotangent,
    joint_weight,
    output_weight,
    expand_weight,
    shrink_weight,
    norm_gains,
    joint_mean,
    joint_square,
    output_mean,
    output_square,
    expand_mean,
    expand_square,
    shrink_mean,
    shrink_square,
    gains_mean,
    gains_square,
):
    cube = Cube(count)
    frames, positions, width = tokens.shape
    run = positions // SETS
    group = cube.bit(cube.top)
    core = cube.bit(0)
    upper = group == 1
    second_core = core == 1
    all_frames = 2 * frames
    rows = all_frames * run
    chip = (cube.index >> 1) & (CHIPS - 1)
    meta = jnp.stack([chip, core, group]).astype(jnp.int32)

    def halves(own, other):
        return jnp.concatenate([jnp.where(upper, other, own), jnp.where(upper, own, other)], axis=0)

    def parted(value):
        first, second = value[:, :run], value[:, run:]
        own, other = jnp.where(upper, second, first), jnp.where(upper, first, second)
        return own.reshape(rows // 2, width), other.reshape(rows // 2, width)

    def from_sets(value):
        value = value.reshape(2, frames, run, width)
        own = jnp.where(upper, value[1], value[0])
        other = cube.swap(jnp.where(upper, value[0], value[1]), cube.top)
        first = jnp.where(upper, other, own)
        second = jnp.where(upper, own, other)
        return jnp.concatenate([first, second], axis=1)

    shard_rows = joint_weight.shape[0]
    lane = norm_gains.shape[1]
    small = jnp.concatenate([norm_gains.astype(BF).reshape(-1), depth_count.astype(BF)])
    small_other = cube.swap(small.reshape(1, -1), cube.top)[0]
    depth_all = halves(small[2 * lane :], small_other[2 * lane :]).astype(jnp.int32)
    gain_pair = halves(small[None, : 2 * lane], small_other[None, : 2 * lane])
    gain_pair = gain_pair.reshape(2, 2, lane).transpose(1, 0, 2)
    spread = jnp.broadcast_to(gain_pair[:, :, None, :], (2, 2, 2 * CHIPS, lane)).reshape(2, width)
    mine = (jnp.arange(width) // lane) % (2 * CHIPS) == (cube.index & (2 * CHIPS - 1))
    gain_rows = jnp.pad(jnp.where(mine[None, :], spread, 0), ((0, 14), (0, 0)))
    shards = list(first_shards(joint_weight))
    shards[2] = lax.dynamic_update_slice(shards[2], gain_rows, (shard_rows, 0))
    joint = [Blocks(shard) for shard in shards]
    x_own, x_give = parted(tokens)
    x_got = cube.swap(x_give, cube.top)
    x_rows = halves(x_own, x_got)

    def begin(name):
        return Round(cube, meta, width, name)

    one = begin("pack_one").gather(joint, 0).run(x_give)
    own_cols, give_cols, shrink_keep, shrink_give, out_a, out_b = split_weights(
        meta, expand_weight, shrink_weight, output_weight
    )
    output = [None, Blocks(out_a), Blocks(out_b)]
    joint_other = [Blocks(rows=blocks.rows) for blocks in joint]
    output_other = [None] + [Blocks(rows=blocks.rows) for blocks in output[1:]]
    two = begin("pack_two").gather(joint, 1).gather(output, 0).run(one.got, give_cols)
    shrink_other = cube.swap(after(shrink_give, two.got, x_got), cube.top)
    got_cols = cube.swap(after(give_cols, two.got, x_got), 0)
    three = begin("pack_three").gather(joint, 2).gather(output, 1)
    three = three.core(joint, joint_other, 0, 4).run(two.got, x_got)
    units = Jobs(width)
    unit_rows = 2 * shard_rows
    for kind in range(2):
        target = units.output(2 * unit_rows)
        for turn_index in range(2):
            unit = turn_index * 2 + kind
            base = turn_index * unit_rows
            low, high = (base, base + shard_rows), (base + shard_rows, base)
            units.copy(own_cols, unit * shard_rows, target, low, shard_rows)
            units.copy(got_cols, unit * shard_rows, target, high, shard_rows)
    target = units.output(2 * unit_rows)
    units.copy(shrink_other, 0, target, 0, unit_rows)
    units.copy(shrink_keep, 0, target, unit_rows, unit_rows)
    units = units.run(meta, "expand_units", three.packed)
    part_a = [Blocks(unit, unit_rows) for unit in units]
    part_b = [Blocks(rows=unit_rows) for unit in units]
    for blocks, unit in zip(part_b, units):
        blocks.arrived(unit, unit_rows, 1)

    cot_own, cot_give = parted(cotangent)
    cot_got = cube.swap(after(cot_give, three.packed, shrink_other), cube.top)
    late = begin("pack_late").core(joint, joint_other, 4, 8)
    late = late.run(three.got, three.core_got, units, x_rows)
    first_units = after(units, three.got, three.core_got)
    got_four = [cube.swap(unit, 1 + axis) for axis, unit in enumerate(first_units)]
    for k in range(3):
        part_a[k].arrived(got_four[k], 0, 1)
        part_b[k].arrived(got_four[k], unit_rows, 1)

    position = group * run + jnp.arange(run)
    live = (position[None, :] < depth_all[:, None]).astype(F32).reshape(rows, 1)

    first, query, key_value, gains_all = joint_forward(meta, x_rows, joint + joint_other)
    key_value_other = cube.swap(key_value, cube.top)
    five = begin("pack_five").gather(part_a, 1).gather(part_b, 1).run(got_four, key_value, cot_got)
    last = begin("pack_output").gather(output, 2).run(five.packed)
    output_core = begin("pack_core").core(output, output_other, 0, 8).run(last.got)
    seven = begin("pack_seven").gather(part_a, 2)
    seven = seven.run(five.got, key_value_other, output_core.packed)
    cot_live = (halves(cot_own, after(cot_got, key_value)).astype(F32) * live).astype(BF)
    cot_other = cube.swap(after(cot_live, five.got, key_value_other), 0)

    output_chains = output[1:] + output_other[1:]
    context, middle, second = context_forward(
        run,
        meta,
        query,
        key_value,
        key_value_other,
        x_rows,
        live,
        gains_all,
        output_chains,
    )
    eight = begin("pack_eight").gather(part_b, 2).run(
        seven.packed, cot_other, gate=(seven.got, second)
    )
    second_other = cube.swap(second, 0)
    row_args = (meta, second, second_other, cot_live, cot_other)
    dn_a, *kept_a = ffn_rows(*row_args, part_a, None)
    f_a, *grad_a = ffn_weights(*row_args, *kept_a, part_a[2], None)
    dn_own, dn_send, *kept_b = ffn_rows(*row_args, part_b, after(dn_a, f_a))
    dn_got = cube.swap(dn_send, 0)
    f_own, f_send, *grad_b = ffn_weights(*row_args, *kept_b, part_b[2], f_a)

    outcome = {}

    def expand_final(key, kind):
        def final(jobs, got, keep, count):
            if key not in outcome:
                outcome[key] = (jobs.output(2 * shard_rows, F32), jobs.output(2 * shard_rows, F32))
            own, give = outcome[key]
            half = count // 2
            for target, offset in ((own, (0, half)), (give, (half, 0))):
                got_at = tuple(got[1] + o for o in offset)
                keep_at = tuple(keep[1] + o for o in offset)
                jobs.add(got[0], got_at, keep[0], keep_at, target, kind * shard_rows, half)

        return final

    def plain_final(key):
        def final(jobs, got, keep, count):
            outcome[key] = jobs.output(count, F32)
            jobs.add(got[0], got[1], keep[0], keep[1], outcome[key], 0, count)

        return final

    def ffn_sums(grads, name):
        finals = (expand_final(name, 0), expand_final(name, 1), plain_final(name + "_shrink"))
        block = grads[0].shape[0] // 4
        return [Sums((grads[2 * k], 0), (grads[2 * k + 1], 0), block, finals[k]) for k in range(3)]

    def turn(name, work, *earlier, **options):
        return reduce_round(cube, meta, width, name, work, *earlier, **options)

    def core_sums(name, tensors, *waits):
        jobs = Jobs(width)
        result = []
        payload = []
        for k in range(3):
            rows_out = sum(4 * c for *_, chains in tensors for kk, c in chains if kk == k)
            payload.append(jobs.output(rows_out))
        filled_rows = [0, 0, 0]
        for key, got, keep, chains in tensors:
            row, sums = 0, [None] * 3
            for k, c in chains:
                own = jobs.output(4 * c)
                send_row = filled_rows[k]
                jobs.add(got, row + 4 * c, keep, row + 4 * c, payload[k], send_row, 4 * c)
                jobs.add(got, row, keep, row, own, 0, 4 * c)
                filled_rows[k] += 4 * c
                sums[k] = (own, send_row, c)
                row += CHIPS * c
            result.append((key, sums))
        out = jobs.run(meta, name, waits=waits)
        made = []
        for key, sums in result:
            made.append(
                [
                    None
                    if s is None
                    else Sums((out[s[0]], 0), (out[payload[k]], s[1]), s[2], plain_final((key, k)))
                    for k, s in enumerate(sums)
                ]
            )
        return made, [out[p] for p in payload]

    shrunk_got = cube.swap(f_send, 0)
    shrunk = f_own + shrunk_got.astype(F32)
    result_rows = (middle + live * shrunk).astype(BF).reshape(2, frames, run, width)
    result_own = jnp.where(upper, result_rows[1], result_rows[0])
    result_give = jnp.where(upper, result_rows[0], result_rows[1])
    result_got = cube.swap(result_give, cube.top)
    result = jnp.concatenate(
        [jnp.where(upper, result_got, result_own), jnp.where(upper, result_own, result_got)], axis=1
    )
    sums_a = ffn_sums(grad_a, "a")
    sums_b = ffn_sums(grad_b, "b")
    turn_one, _ = turn("turn_one", [(sums_a, 0)], eight.got)
    turn_two, _ = turn("turn_two", [(sums_b, 0)], turn_one)

    grad_middle, grad_gain_two, grad_branch, d_query, dkv_own, dkv_give = context_back(
        run,
        meta,
        after(dn_own, result_give, turn_one),
        dn_got,
        middle,
        cot_live,
        live,
        gains_all,
        query,
        key_value,
        key_value_other,
        output_chains,
    )
    turn_three, packed_three = turn(
        "turn_three", [(sums_a, 1), (sums_b, 1)], turn_two, dkv_give, result_got
    )
    dkv_got = cube.swap(dkv_give, cube.top)
    output_give, output_keep = output_grad(meta, context, after(grad_branch, packed_three))
    joint_give, joint_keep, dkv = joint_grad(
        meta, first, d_query, dkv_own, after(dkv_got, output_give)
    )
    turn_four, packed_four = turn(
        "turn_four", [(sums_a, 2), (sums_b, 2)], turn_three, dkv_got, waits=(joint_give,)
    )
    joint_got = cube.swap(after(joint_give, packed_four), 0)
    output_got = cube.swap(after(output_give, packed_four), 0)
    grad_inputs, grad_gain_one = input_back(
        meta,
        d_query,
        after(dkv, packed_four),
        grad_middle,
        x_rows,
        gains_all,
        joint + joint_other,
    )
    half_shard = shard_rows // 2
    (sums_j, sums_o), sends = core_sums(
        "joint_core",
        [
            ("joint", joint_got, joint_keep, [(k, shard_rows) for k in range(3)]),
            ("output", output_got, output_keep, [(k, half_shard) for k in OUTPUT_CHAINS]),
        ],
        grad_inputs,
    )
    turn_seven = []
    for axis in range(3):
        k = (axis - 2) % 3
        array = cube.swap(sends[k], 1 + axis)
        turn_seven.append(array)
        for sums in (sums_j, sums_o):
            if sums[k] is not None:
                sums[k].got = (array, sums[k].send[1])
    grad_inputs = from_sets(after(grad_inputs, sends[0]))
    _, out_five = turn(
        "turn_five",
        [(sums_a, 3), (sums_b, 3)],
        turn_four,
        sends[0],
        squares=True,
    )
    expand_own_a, expand_give_a = (out_five[i] for i in outcome["a"])
    expand_own_b, expand_give_b = (out_five[i] for i in outcome["b"])
    shrink_first = out_five[outcome["a_shrink"]]
    shrink_mine = out_five[outcome["b_shrink"]]
    expand_got_a = cube.swap(after(expand_give_a, sends[0]), 0)
    expand_got_b = cube.swap(after(expand_give_b, expand_got_a), 0)
    turn_nine, out_nine = turn(
        "turn_nine",
        [(sums_o, 1), (sums_j, 1)],
        turn_seven,
        grad_inputs,
        waits=(out_five[-1],),
    )
    shrink_got = cube.swap(after(shrink_first.astype(BF), out_nine[0]), cube.top)
    turn_ten, out_ten = turn(
        "turn_ten", [(sums_o, 2), (sums_j, 2)], turn_nine, shrink_got
    )
    _, out_last = turn(
        "turn_last",
        [(sums_o, 3), (sums_j, 3)],
        turn_ten,
        squares=True,
        norm=(count, out_five[-1], grad_gain_one, grad_gain_two),
    )
    grad_output = [out_last[outcome[("output", k)]] for k in OUTPUT_CHAINS]
    grad_joint = jnp.stack([out_last[outcome[("joint", k)]] for k in range(3)])

    squares = lax.all_to_all(out_last[-1], "fsdp", 0, 0, tiled=True)
    gains_sum = jnp.sum(squares[:, 128:], axis=0)
    total_sq = jnp.sum(squares[:, 0]) + jnp.sum(gains_sum * gains_sum)
    grad_gains = lax.dynamic_index_in_dim(
        gains_sum.reshape(2, count, lane), cube.index, 1, keepdims=False
    )
    grad_norm_value = jnp.sqrt(total_sq)
    factor = CLIP_LIMIT / jnp.maximum(grad_norm_value, CLIP_LIMIT)
    new = adam_matrices(
        meta,
        squares,
        (
            expand_weight,
            expand_mean,
            expand_square,
            expand_own_a,
            expand_own_b,
            expand_got_a,
            expand_got_b,
        ),
        (joint_weight, joint_mean, joint_square, grad_joint),
        (output_weight, output_mean, output_square, *grad_output),
        (shrink_weight, shrink_mean, shrink_square, shrink_mine, shrink_got),
    )
    expand_new, joint_new, output_new, shrink_new = (new[i : i + 3] for i in (0, 3, 6, 9))
    gains_new = adam_step(norm_gains, factor * grad_gains, gains_mean, gains_square, GAIN_RATE, 0.0)
    return (
        result,
        grad_inputs,
        grad_norm_value,
        *joint_new,
        *output_new,
        *expand_new,
        *shrink_new,
        *gains_new,
    )


def solution(mesh):
    rows = P("fsdp", None)
    cube = P("fsdp", None, None)
    inner = P(None, "fsdp", None)
    gains = P(None, "fsdp")
    count = mesh.shape["fsdp"]

    def body(*args):
        return (local_cube if count == 4 * CHIPS else local_general)(count, *args)

    return jax.shard_map(
        body,
        mesh=mesh,
        in_specs=(cube, P("fsdp"), cube, rows, rows, rows, inner, gains)
        + (rows,) * 6
        + (inner, inner, gains, gains),
        out_specs=(cube, cube, P()) + (rows,) * 9 + (inner,) * 3 + (gains,) * 3,
        check_vma=False,
    )
```

```python
import functools

import jax
import jax.numpy as jnp
from jax import lax
from jax.experimental import pallas as pl
from jax.experimental.pallas import tpu as pltpu
from jax.sharding import PartitionSpec as P

HEADS = 16
SETS = 2
STEP = 10

NORM_EPS = 1e-05
BETA_ONE = 0.9
BETA_TWO = 0.95
ADAM_EPS = 1e-08
MATRIX_RATE = 0.08
GAIN_RATE = 1.0
MATRIX_DECAY = 0.1
CLIP_LIMIT = 1.0

BF = jnp.bfloat16
F32 = jnp.float32


def dot(a, b):
    return lax.dot_general(a, b, (((1,), (0,)), ((), ())), preferred_element_type=F32)


def dot_nt(a, b):
    return lax.dot_general(a, b, (((1,), (1,)), ((), ())), preferred_element_type=F32)


def dot_tn(a, b):
    return lax.dot_general(a, b, (((0,), (0,)), ((), ())), preferred_element_type=F32)


def adam_step(weight, grad_value, mean_old, square_old, learn_rate, weight_decay):
    mean_new = BETA_ONE * mean_old + (1.0 - BETA_ONE) * grad_value
    square_new = BETA_TWO * square_old + (1.0 - BETA_TWO) * grad_value * grad_value
    mean_hat = mean_new / (1.0 - BETA_ONE**STEP)
    square_hat = square_new / (1.0 - BETA_TWO**STEP)
    weight_new = weight - learn_rate * (
        mean_hat / (jnp.sqrt(square_hat) + ADAM_EPS) + weight_decay * weight
    )
    return (weight_new, mean_new, square_new)


class Cube:
    def __init__(self, count):
        self.count = count
        self.bits = count.bit_length() - 1
        self.top = self.bits - 1
        self.index = lax.axis_index("fsdp")
        chip = list(range(1, self.top))
        third = max(1, len(chip) // 3)
        self.orders = [chip[third * k :] + chip[: third * k] for k in range(3)]

    def bit(self, b):
        return (self.index >> b) & 1

    def swap(self, value, b):
        pairs = [(i, i ^ (1 << b)) for i in range(self.count)]
        return lax.ppermute(value, "fsdp", pairs)

    def gather(self, value, bits, lead=0):
        have = []
        for b in bits:
            other = self.swap(value, b)
            mine = self.bit(b) == 1
            axis = lead + sum(1 for h in have if h > b)
            low = jnp.where(mine, other, value)
            high = jnp.where(mine, value, other)
            value = jnp.stack([low, high], axis=axis)
            have.append(b)
        return value

    def reduce(self, value, have, bits, lead=0, last=F32):
        have = list(have)
        for step, b in enumerate(bits):
            axis = lead + sum(1 for h in have if h > b)
            mine = self.bit(b)
            send = lax.dynamic_index_in_dim(value, 1 - mine, axis, keepdims=False).astype(BF)
            keep = lax.dynamic_index_in_dim(value, mine, axis, keepdims=False)
            other = self.swap(send, b)
            value = keep.astype(F32) + other.astype(F32)
            if step < len(bits) - 1:
                value = value.astype(BF)
            have.remove(b)
        return value.astype(last)

    def total(self, value):
        for b in range(self.bits):
            value = value + self.swap(value, b)
        return value


def cuts(width, parts=3, unit=128):
    units = width // unit
    sizes = [units // parts + (1 if k < units % parts else 0) for k in range(parts)]
    edges = [0]
    for size in sizes:
        edges.append(edges[-1] + size * unit)
    return edges


def local_general(
    count,
    tokens,
    depth_count,
    cotangent,
    joint_weight,
    output_weight,
    expand_weight,
    shrink_weight,
    norm_gains,
    joint_mean,
    joint_square,
    output_mean,
    output_square,
    expand_mean,
    expand_square,
    shrink_mean,
    shrink_square,
    gains_mean,
    gains_square,
):
    cube = Cube(count)
    half = count // 2
    own_bits = cube.top
    frames, positions, width = tokens.shape
    run = positions // SETS
    in_set = cube.bit(cube.top)
    upper = in_set == 1
    all_frames = 2 * frames
    rows = all_frames * run
    hidden_width = expand_weight.shape[1] // 2
    head_dim = width // HEADS

    def to_sets(value):
        first, second = value[:, :run], value[:, run:]
        other = cube.swap(jnp.where(upper, first, second), cube.top)
        own = jnp.where(upper, second, first)
        low = jnp.where(upper, other, own)
        high = jnp.where(upper, own, other)
        return jnp.concatenate([low, high], axis=0)

    def from_sets(value):
        value = value.reshape(2, frames, run, value.shape[-1])
        own = jnp.where(upper, value[1], value[0])
        other = cube.swap(jnp.where(upper, value[0], value[1]), cube.top)
        first = jnp.where(upper, other, own)
        second = jnp.where(upper, own, other)
        return jnp.concatenate([first, second], axis=1)

    position_index = jnp.arange(positions)
    live_here = (position_index[None, :] < depth_count[:, None]).astype(F32)[:, :, None]
    masked = (cotangent.astype(F32) * live_here).astype(BF)

    gains_local = norm_gains.astype(BF)
    gains_all = cube.gather(gains_local, range(cube.bits), lead=1)
    gains_all = gains_all.reshape(2, width).astype(F32)

    def gather_matrix(shard, order, lead=0):
        return cube.gather(shard, list(order) + [0], lead=lead)

    joint_low = joint_weight.astype(BF)
    joint_parts = [
        gather_matrix(joint_low[:, k * width : (k + 1) * width], cube.orders[k]).reshape(width, width)
        for k in range(3)
    ]
    x_rows = to_sets(tokens).reshape(rows, width).astype(F32)
    live = to_sets(live_here).reshape(rows, 1)
    cot = to_sets(masked).reshape(rows, width)

    output_low = output_weight.astype(BF)
    expand_low = expand_weight.astype(BF)
    wide = hidden_width // 4
    edge = [0, wide, (wide + hidden_width) // 2, hidden_width]
    expand_shards = []
    for k in range(3):
        gate_cols = expand_low[:, edge[k] : edge[k + 1]]
        up_cols = expand_low[:, hidden_width + edge[k] : hidden_width + edge[k + 1]]
        parts = ([output_low] if k == 0 else []) + [gate_cols, up_cols]
        expand_shards.append(jnp.concatenate(parts, axis=1))
    expand_parts = [
        gather_matrix(expand_shards[k], cube.orders[k]).reshape(width, -1) for k in range(3)
    ]
    output_full = expand_parts[0][:, :width]
    gate_full = [expand_parts[0][:, width : 2 * width]] + [
        expand_parts[k][:, : edge[k + 1] - edge[k]] for k in (1, 2)
    ]
    up_full = [expand_parts[0][:, 2 * width :]] + [
        expand_parts[k][:, edge[k + 1] - edge[k] :] for k in (1, 2)
    ]

    shrink_low = shrink_weight.astype(BF)
    shrink_mine = jnp.where(upper, shrink_low[1], shrink_low[0])
    shrink_send = jnp.where(upper, shrink_low[0], shrink_low[1])
    shrink_other = cube.swap(shrink_send, cube.top)
    shrink_pair = jnp.stack(
        [jnp.where(upper, shrink_other, shrink_mine), jnp.where(upper, shrink_mine, shrink_other)]
    )
    col = cuts(width)
    shrink_parts = [
        gather_matrix(shrink_pair[:, :, col[k] : col[k + 1]], cube.orders[k], lead=1).reshape(
            hidden_width, -1
        )
        for k in range(3)
    ]

    inv_one = lax.rsqrt(jnp.mean(x_rows * x_rows, axis=-1, keepdims=True) + NORM_EPS)
    first = (x_rows * inv_one * gains_all[0]).astype(BF)
    query, key_own, value_own = [dot(first, joint_parts[k]).astype(BF) for k in range(3)]
    key_value = cube.swap(jnp.concatenate([key_own, value_own], axis=1), cube.top)

    def heads(value):
        return value.reshape(all_frames, run, HEADS, head_dim)

    q_h = heads(query)
    k_h = jnp.concatenate([heads(key_value[:, :width]), heads(key_own)], axis=1)
    v_h = jnp.concatenate([heads(key_value[:, width:]), heads(value_own)], axis=1)
    scale = head_dim ** (-0.5)
    scores = jnp.einsum("fphd,fkhd->fhpk", q_h, k_h, preferred_element_type=F32) * scale
    row = jnp.arange(run)[:, None]
    column = jnp.arange(2 * run)[None, :]
    seen = jnp.where(column < run, upper, row >= column - run)
    scores = jnp.where(seen, scores, -1e30)
    exp_scores = jnp.exp(scores - jnp.max(scores, axis=-1, keepdims=True))
    attention = exp_scores / jnp.sum(exp_scores, axis=-1, keepdims=True)
    attention_low = attention.astype(BF)
    context = (
        jnp.einsum("fhpk,fkhd->fphd", attention_low, v_h, preferred_element_type=F32)
        .reshape(rows, width)
        .astype(BF)
    )
    middle = x_rows + live * dot(context, output_full)
    inv_two = lax.rsqrt(jnp.mean(middle * middle, axis=-1, keepdims=True) + NORM_EPS)
    second = (middle * inv_two * gains_all[1]).astype(BF)
    gate = [dot(second, w) for w in gate_full]
    up = [dot(second, w) for w in up_full]
    hidden = jnp.concatenate(
        [(jax.nn.silu(g) * u).astype(BF) for g, u in zip(gate, up)], axis=1
    )
    shrunk = jnp.concatenate([dot(hidden, w) for w in shrink_parts], axis=1)
    result = from_sets((middle + live * shrunk).astype(BF))

    def reduce_matrix(grad, order, lead=0, block=None):
        bits = list(range(own_bits))
        shape = grad.shape
        if lead:
            grad = grad.reshape((2,) + (2,) * own_bits + (shape[0] // 2 // half, shape[1]))
        else:
            grad = grad.reshape((2,) * own_bits + (shape[0] // half, shape[1]))
        return cube.reduce(grad, bits, [0] + list(order), lead=lead)

    grad_shrink_parts = [
        reduce_matrix(dot_tn(hidden, cot[:, col[k] : col[k + 1]]).astype(BF), cube.orders[k], lead=1)
        for k in range(3)
    ]
    grad_shrink_pair = jnp.concatenate(grad_shrink_parts, axis=-1)
    shrink_keep = jnp.where(upper, grad_shrink_pair[1], grad_shrink_pair[0])
    shrink_give = jnp.where(upper, grad_shrink_pair[0], grad_shrink_pair[1]).astype(BF)
    shrink_got = cube.swap(shrink_give, cube.top).astype(F32)
    grad_shrink = jnp.stack(
        [jnp.where(upper, shrink_got, shrink_keep), jnp.where(upper, shrink_keep, shrink_got)]
    )

    grad_hidden = sum(dot_nt(cot[:, col[k] : col[k + 1]], shrink_parts[k]) for k in range(3))
    grad_second = 0.0
    grad_expand_parts = []
    for k in range(3):
        d_hid = grad_hidden[:, edge[k] : edge[k + 1]]
        sig = jax.nn.sigmoid(gate[k])
        d_gate = (d_hid * up[k] * sig * (1.0 + gate[k] * (1.0 - sig))).astype(BF)
        d_up = (d_hid * gate[k] * sig).astype(BF)
        both = jnp.concatenate([d_gate, d_up], axis=1)
        weight_pair = jnp.concatenate([gate_full[k], up_full[k]], axis=1)
        grad_second = grad_second + dot_nt(both, weight_pair)
        grad_expand_parts.append(
            reduce_matrix(dot_tn(second, both).astype(BF), cube.orders[k])
        )
    grad_expand = jnp.concatenate(
        [grad_expand_parts[k][:, : edge[k + 1] - edge[k]] for k in range(3)]
        + [grad_expand_parts[k][:, edge[k + 1] - edge[k] :] for k in range(3)],
        axis=1,
    )

    def normalize_back(values, inverse, gain_row, grad_out):
        scaled = grad_out * gain_row
        grad_in = inverse * scaled - values * inverse * inverse * inverse * jnp.mean(
            scaled * values, axis=-1, keepdims=True
        )
        return (grad_in, jnp.sum(grad_out * values * inverse, axis=0))

    grad_mid_norm, grad_gain_two = normalize_back(middle, inv_two, gains_all[1], grad_second)
    grad_middle = cot.astype(F32) + grad_mid_norm
    grad_branch = (grad_middle * live).astype(BF)
    grad_context = dot_nt(grad_branch, output_full).astype(BF)

    g_h = heads(grad_context)
    grad_attention = jnp.einsum("fphd,fkhd->fhpk", g_h, v_h, preferred_element_type=F32)
    grad_value = jnp.einsum("fhpk,fphd->fkhd", attention_low, g_h, preferred_element_type=F32)
    grad_scores = attention * (
        grad_attention - jnp.sum(grad_attention * attention, axis=-1, keepdims=True)
    )
    grad_scores = grad_scores.astype(BF)
    grad_query = (
        jnp.einsum("fhpk,fkhd->fphd", grad_scores, k_h, preferred_element_type=F32) * scale
    )
    grad_key = jnp.einsum("fhpk,fphd->fkhd", grad_scores, q_h, preferred_element_type=F32) * scale
    give = jnp.concatenate(
        [grad_key[:, :run].reshape(rows, width), grad_value[:, :run].reshape(rows, width)], axis=1
    ).astype(BF)
    got = cube.swap(give, cube.top).astype(F32)
    got = jnp.where(upper, 0.0, got)
    d_query = grad_query.reshape(rows, width).astype(BF)
    d_key = (grad_key[:, run:].reshape(rows, width) + got[:, :width]).astype(BF)
    d_value = (grad_value[:, run:].reshape(rows, width) + got[:, width:]).astype(BF)

    grad_output = reduce_matrix(dot_tn(context, grad_branch).astype(BF), cube.orders[0])
    joint_grads = [
        reduce_matrix(dot_tn(first, d).astype(BF), cube.orders[k])
        for k, d in enumerate((d_query, d_key, d_value))
    ]
    grad_joint = jnp.concatenate(joint_grads, axis=1)
    grad_first = sum(
        dot_nt(d, w) for d, w in zip((d_query, d_key, d_value), joint_parts)
    )
    grad_in_norm, grad_gain_one = normalize_back(x_rows, inv_one, gains_all[0], grad_first)
    grad_inputs = from_sets((grad_middle + grad_in_norm).astype(BF))

    gains_term = jnp.stack([grad_gain_one, grad_gain_two]).reshape((2,) + (2,) * cube.bits + (-1,))
    bits = list(range(cube.bits))
    have = list(bits)
    for b in bits:
        axis = 1 + sum(1 for h in have if h > b)
        mine = cube.bit(b)
        send = lax.dynamic_index_in_dim(gains_term, 1 - mine, axis, keepdims=False)
        keep = lax.dynamic_index_in_dim(gains_term, mine, axis, keepdims=False)
        gains_term = keep + cube.swap(send, b)
        have.remove(b)
    grad_gains = gains_term

    reduced = (grad_joint, grad_output, grad_expand, grad_shrink, grad_gains)
    local_sq = sum(jnp.sum(g * g) for g in reduced)
    total_sq = cube.total(jnp.broadcast_to(local_sq, (8, 128)))[0, 0]
    grad_norm_value = jnp.sqrt(total_sq)
    factor = CLIP_LIMIT / jnp.maximum(grad_norm_value, CLIP_LIMIT)
    joint_new = adam_step(
        joint_weight, factor * reduced[0], joint_mean, joint_square, MATRIX_RATE, MATRIX_DECAY
    )
    output_new = adam_step(
        output_weight, factor * reduced[1], output_mean, output_square, MATRIX_RATE, MATRIX_DECAY
    )
    expand_new = adam_step(
        expand_weight, factor * reduced[2], expand_mean, expand_square, MATRIX_RATE, MATRIX_DECAY
    )
    shrink_new = adam_step(
        shrink_weight, factor * reduced[3], shrink_mean, shrink_square, MATRIX_RATE, MATRIX_DECAY
    )
    gains_new = adam_step(norm_gains, factor * reduced[4], gains_mean, gains_square, GAIN_RATE, 0.0)
    return (
        result,
        grad_inputs,
        grad_norm_value,
        *joint_new,
        *output_new,
        *expand_new,
        *shrink_new,
        *gains_new,
    )


CHIPS = 8
CHAIN_BITS = [[(k + t) % 3 for t in range(3)] for k in range(3)]
CHAIN_MASKS = [
    [sum(((j >> t) & 1) << bits[t] for t in range(3)) for j in range(CHIPS)] for bits in CHAIN_BITS
]
VM = pl.BlockSpec(memory_space=pltpu.VMEM)
HB = pl.BlockSpec(memory_space=pltpu.HBM)
SM = pl.BlockSpec(memory_space=pltpu.SMEM)
MIB = 1 << 20
SMALL = pl.CostEstimate(flops=1, bytes_accessed=1, transcendentals=0)


def aligned(index, size):
    return pl.ds(pl.multiple_of(index * size, size), size)


def after(value, *earlier):
    return lax.optimization_barrier((value, earlier))[0]


def plus(a, b):
    return (a.astype(F32) + b.astype(F32)).astype(BF)


class Jobs:
    def __init__(self, width):
        self.width = width
        self.inputs, self.outputs, self.work = [], [], []

    def source(self, array):
        for i, known in enumerate(self.inputs):
            if known is array:
                return i
        self.inputs.append(array)
        return len(self.inputs) - 1

    def output(self, rows, dtype=BF):
        self.outputs.append(jax.ShapeDtypeStruct((rows, self.width), dtype))
        return len(self.outputs) - 1

    def copy(self, array, row, target, target_row, count):
        self.work.append((self.source(array), row, None, 0, target, target_row, count))

    def add(self, a, a_row, b, b_row, target, target_row, count):
        self.work.append((self.source(a), a_row, self.source(b), b_row, target, target_row, count))

    def run(self, meta, name, *earlier, squares=False, norm=(), waits=()):
        inputs = after(self.inputs, *earlier) if earlier else self.inputs
        adds = [w for w in self.work if w[2] is not None]
        rows = sum(w[6] for w in adds)
        moved = sum(w[6] for w in self.work if w[2] is None)
        scratch = [pltpu.SemaphoreType.DMA((3, len(self.work)))]
        scratch += [pltpu.VMEM((max(moved, 16), self.width), BF)]
        if adds:
            scratch += [pltpu.VMEM((rows, self.width), BF)] * 3
            scratch += [pltpu.VMEM((rows, self.width), F32)]
        shapes = list(self.outputs)
        if squares:
            shape = (norm[0], 128 + self.width * (len(norm) - 2)) if norm else (8, self.width)
            shapes.append(jax.ShapeDtypeStruct(shape, F32))
        more = list(norm[1:])
        scratch += [pltpu.VMEM((8, self.width), F32)] if squares else []
        return pl.pallas_call(
            functools.partial(
                jobs_kernel, self.work, len(inputs), self.outputs, squares, len(more), len(waits)
            ),
            in_specs=[SM] + [HB] * len(inputs) + [VM] * len(more) + [HB] * len(waits),
            out_specs=[HB] * len(self.outputs) + ([VM] if squares else []),
            out_shape=shapes,
            scratch_shapes=scratch,
            compiler_params=pltpu.CompilerParams(vmem_limit_bytes=60 * MIB),
            cost_estimate=SMALL,
            name=name,
        )(meta, *inputs, *more, *waits)


def jobs_kernel(work, count, outputs, squares, more, waits, meta, *refs):
    sources, norm = refs[:count], refs[count : count + more]
    refs = refs[count + more + waits :]
    targets = refs[: len(outputs)]
    refs = refs[len(outputs) :]
    if squares:
        square_out, square_ref = refs[0], refs[-1]
        refs = refs[1:-1]
    sem = refs[0]
    core = meta[1]

    def part(ref, row, rows):
        if isinstance(row, tuple):
            start = pl.multiple_of(jnp.where(core == 0, row[0], row[1]), 16)
            return ref.at[pl.ds(start, rows)]
        return ref.at[row : row + rows]

    coming, leaving = [], []
    at, moved = 0, 0
    transit = refs[1]
    refs = refs[:1] + refs[2:]
    for i, (a, a_row, b, b_row, target, target_row, rows) in enumerate(work):
        if b is None:
            spot = slice(moved, moved + rows)
            copy = pltpu.make_async_copy(part(sources[a], a_row, rows), transit.at[spot], sem.at[0, i])
            copy.start()
            coming.append(((copy,), spot))
            moved += rows
            continue
        spot = slice(at, at + rows)
        pair = (
            pltpu.make_async_copy(part(sources[a], a_row, rows), refs[1].at[spot], sem.at[0, i]),
            pltpu.make_async_copy(part(sources[b], b_row, rows), refs[2].at[spot], sem.at[1, i]),
        )
        for copy in pair:
            copy.start()
        coming.append((pair, spot))
        at += rows
    if squares:
        square_ref[...] = jnp.zeros_like(square_ref)
    for i, (a, a_row, b, b_row, target, target_row, rows) in enumerate(work):
        pair, spot = coming[i]
        finish(pair)
        if b is None:
            copy = pltpu.make_async_copy(
                transit.at[spot], part(targets[target], target_row, rows), sem.at[2, i]
            )
            copy.start()
            leaving.append(copy)
            continue
        wide = outputs[target].dtype == F32
        store = refs[4] if wide else refs[3]
        if not wide and not squares:
            store[spot] = plus(refs[1][spot], refs[2][spot])
        else:
            total = refs[1][spot].astype(F32) + refs[2][spot].astype(F32)
            store[spot] = total.astype(store.dtype)
            if wide:
                square = (total * total).reshape(rows // 8, 8, total.shape[1])
                square_ref[...] += jnp.sum(square, axis=0)
        copy = pltpu.make_async_copy(
            store.at[spot], part(targets[target], target_row, rows), sem.at[2, i]
        )
        copy.start()
        leaving.append(copy)
    if squares and not norm:
        square_out[...] = square_ref[...]
    if norm:
        total = jnp.sum(square_ref[...]) + jnp.sum(norm[0][...])
        square_out[:, :128] = jnp.full((square_out.shape[0], 128), total, F32)
        for i, ref in enumerate(norm[1:]):
            width = ref.shape[1]
            spot = slice(128 + i * width, 128 + (i + 1) * width)
            square_out[:, spot] = jnp.broadcast_to(ref[...], (square_out.shape[0], width))
    finish(leaving)


class Blocks:
    def __init__(self, own=None, rows=None):
        self.rows = own.shape[0] if rows is None else rows
        self.held = [] if own is None else [(own, 0)]

    def arrived(self, array, row, count):
        for j in range(count):
            self.held.append((array, row + j * self.rows))


def place(jobs, held, rows, target, target_row):
    start = 0
    while start < len(held):
        array, row = held[start]
        stop = start + 1
        while stop < len(held) and held[stop][0] is array and held[stop][1] == row + (stop - start) * rows:
            stop += 1
        jobs.copy(array, row, target, target_row + start * rows, (stop - start) * rows)
        start = stop


class Round:
    def __init__(self, cube, meta, width, name):
        self.cube, self.meta, self.name = cube, meta, name
        self.jobs = Jobs(width)
        self.axis_work = []
        self.core_work = []

    def gather(self, chains, level):
        self.axis_work.append((chains, level))
        return self

    def core(self, chains, others, start, stop):
        self.core_work.append((chains, others, start, stop))
        return self

    def run(self, *earlier, gate=()):
        jobs = self.jobs
        filled = []
        for axis in range(3):
            held = []
            for chains, level in self.axis_work:
                blocks = chains[(axis - level) % 3]
                if blocks is not None:
                    held.append((blocks, blocks.held[: 1 << level]))
            filled.append(held)
        core_held = []
        for chains, others, start, stop in self.core_work:
            for blocks, other in zip(chains, others):
                if blocks is not None:
                    core_held.append((blocks, other, blocks.held[start:stop]))
        direct = not core_held and all(len(h) == 1 and len(h[0][1]) == 1 for h in filled)
        if direct:
            payloads = [h[0][1][0][0] for h in filled]
            if earlier:
                payloads = after(payloads, *earlier)
        else:
            for held in filled:
                if held:
                    target = jobs.output(sum(b.rows * len(h) for b, h in held))
                    row = 0
                    for blocks, part in held:
                        place(jobs, part, blocks.rows, target, row)
                        row += blocks.rows * len(part)
            if core_held:
                target = jobs.output(sum(b.rows * len(h) for b, _, h in core_held))
                row = 0
                for blocks, _, part in core_held:
                    place(jobs, part, blocks.rows, target, row)
                    row += blocks.rows * len(part)
            payloads = jobs.run(self.meta, self.name, *earlier)
            self.packed = payloads
            if gate:
                axes = sum(1 for held in filled if held)
                payloads = after(list(payloads[:axes]), *gate) + list(payloads[axes:])
        got = []
        index = 0
        for axis, held in enumerate(filled):
            if not held:
                continue
            array = self.cube.swap(payloads[index], 1 + axis)
            index += 1
            row = 0
            for blocks, part in held:
                blocks.arrived(array, row, len(part))
                row += blocks.rows * len(part)
            got.append(array)
        self.got = got
        self.core_got = None
        if core_held:
            array = self.cube.swap(payloads[index], 0)
            row = 0
            for blocks, other, part in core_held:
                other.arrived(array, row, len(part))
                row += blocks.rows * len(part)
            self.core_got = array
        self.payloads = payloads
        return self


def operands(*chains):
    arrays, tables = [], []
    for blocks in chains:
        table = []
        for array, row in blocks.held:
            found = [i for i, a in enumerate(arrays) if a is array]
            if not found:
                arrays.append(array)
                found = [len(arrays) - 1]
            table.append((found[0], row))
        tables.append((blocks.rows, table))
    return arrays, tables


class Sums:
    def __init__(self, keep, send, rows, final):
        self.keep, self.send, self.rows, self.count, self.final = keep, send, rows, 4, final


def reduce_round(cube, meta, width, name, work, *earlier, squares=False, gate=(), norm=(), waits=()):
    jobs = Jobs(width)
    filled = []
    direct = all(step == 0 for _, step in work) and len(work) == 1
    for axis in range(3):
        parts = []
        for chains, step in work:
            if step < 3:
                chain = chains[(axis - (2 - step)) % 3]
                if chain is not None:
                    parts.append((chain, step))
        filled.append(parts)
    if direct:
        payloads = [parts[0][0].send[0] for parts in filled]
        if earlier:
            payloads = after(payloads, *earlier)
    else:
        layout = []
        for parts in filled:
            if not parts:
                continue
            rows = 0
            target = None
            sizes = []
            for chain, step in parts:
                size = chain.rows * (4 >> step)
                sizes.append((chain, step, rows, size))
                rows += size
            layout.append((jobs.output(rows), sizes))
        kept = {}
        for target, sizes in layout:
            for chain, step, row, size in sizes:
                if step == 0:
                    jobs.copy(chain.send[0], chain.send[1], target, row, size)
                else:
                    got, got_row = chain.got
                    array, keep_row = chain.keep
                    own = jobs.output(size)
                    jobs.add(got, got_row + size, array, keep_row + size, target, row, size)
                    jobs.add(got, got_row, array, keep_row, own, 0, size)
                    kept[own] = chain
        for chains, step in work:
            if step == 3:
                for chain in chains:
                    if chain is not None:
                        chain.final(jobs, chain.got, chain.keep, chain.rows)
        out = jobs.run(meta, name, *earlier, squares=squares, norm=norm, waits=waits)
        for own, chain in kept.items():
            chain.keep = (out[own], 0)
        payloads = [out[target] for target, _ in layout]
        if gate and payloads:
            payloads = after(payloads, *gate)
    got = []
    index = 0
    for axis, parts in enumerate(filled):
        if not parts:
            continue
        array = cube.swap(payloads[index], 1 + axis)
        index += 1
        row = 0
        for chain, step in parts:
            chain.got = (array, row)
            row += chain.rows * (4 >> step)
        got.append(array)
    return (got, out) if not direct else (got, None)


def first_kernel(joint, q, k, v):
    width = q.shape[1]
    q[...] = joint[:, :width].astype(BF)
    k[...] = joint[:, width : 2 * width].astype(BF)
    v[: joint.shape[0]] = joint[:, 2 * width :].astype(BF)


def first_shards(joint):
    rows, width = joint.shape[0], joint.shape[1] // 3
    return pl.pallas_call(
        first_kernel,
        in_specs=[VM],
        out_specs=[VM] * 3,
        out_shape=[jax.ShapeDtypeStruct((r, width), BF) for r in (rows, rows, rows + 16)],
        compiler_params=pltpu.CompilerParams(vmem_limit_bytes=60 * MIB),
        name="first_shards",
    )(joint)


def split_kernel(meta, expand, shrink, output, own, give, shrink_own, shrink_give, out_a, out_b):
    core, group = meta[1], meta[2]
    rows = expand.shape[0]
    block = expand.shape[1] // (2 * 2 * 2 * CHIPS)
    for turn in range(2):
        part = turn ^ (1 - group)
        for kind in range(2):
            for chip in range(CHIPS):
                base = ((kind * 2 + part) * CHIPS + chip) * 2
                cols = slice(chip * block, (chip + 1) * block)
                r = slice((turn * 2 + kind) * rows, (turn * 2 + kind + 1) * rows)
                own[r, cols] = expand[:, aligned(base + core, block)].astype(BF)
                give[r, cols] = expand[:, aligned(base + 1 - core, block)].astype(BF)
    shrink_own[...] = shrink[group].astype(BF)
    shrink_give[...] = shrink[1 - group].astype(BF)
    out_a[...] = output[: rows // 2].astype(BF)
    out_b[...] = output[rows // 2 :].astype(BF)


def split_weights(meta, expand, shrink, output):
    rows, width = output.shape
    four = jax.ShapeDtypeStruct((4 * rows, width), BF)
    two = jax.ShapeDtypeStruct(shrink.shape[1:], BF)
    half = jax.ShapeDtypeStruct((rows // 2, width), BF)
    return pl.pallas_call(
        split_kernel,
        in_specs=[SM, VM, VM, VM],
        out_specs=[VM] * 6,
        out_shape=[four, four, two, two, half, half],
        compiler_params=pltpu.CompilerParams(vmem_limit_bytes=60 * MIB),
        name="split_weights",
    )(meta, expand, shrink, output)


def load_blocks(table, refs, w, k, chip, sem):
    copies = []
    rows, places = table
    for j, (index, row) in enumerate(places):
        target = w.at[aligned(chip ^ CHAIN_MASKS[k][j], rows), :]
        copy = pltpu.make_async_copy(refs[index].at[row : row + rows], target, sem.at[j])
        copy.start()
        copies.append(copy)
    return copies


def store_blocks(w, pieces, rows, k, chip, sem):
    copies = []
    for j in range(CHIPS):
        source = w.at[aligned(chip ^ CHAIN_MASKS[k][j], rows), :]
        row = (j % 4) * rows
        copy = pltpu.make_async_copy(source, pieces[j // 4].at[row : row + rows], sem.at[j])
        copy.start()
        copies.append(copy)
    return copies


def finish(copies):
    for copy in copies:
        copy.wait()


TILE = 256


def ffn_rows_kernel(first, count, tables, meta, n2m, n2o, cm, co, *refs):
    pieces = refs[:count]
    refs = refs[count:]
    if not first:
        dn_in = refs[0]
        refs = refs[1:]
    if first:
        dn_out, hid, dg, du, n2, c, wg, wu, ws, sem = refs
    else:
        dn_out, dn_send, hid, dg, du, n2, c, wg, wu, ws, sem = refs
    chip = meta[0]
    mats = (wg, wu, ws)
    coming = [load_blocks(tables[k], pieces, mats[k], k, chip, sem.at[k]) for k in range(3)]
    rows = n2m.shape[0]
    n2[:rows] = n2m[...]
    n2[rows:] = n2o[...]
    c[:rows] = cm[...]
    c[rows:] = co[...]
    for copies in coming:
        finish(copies)
    width = wg.shape[1]

    def gates(t, _):
        cols = aligned(t, TILE)
        g = dot(n2[...], wg[:, cols])
        u = dot(n2[...], wu[:, cols])
        dh = dot_nt(c[...], ws[cols, :])
        sig = jax.nn.sigmoid(g)
        silu = g * sig
        hid[:, cols] = (silu * u).astype(BF)
        du[:, cols] = (dh * silu).astype(BF)
        dg[:, cols] = (dh * u * sig * (1.0 + g * (1.0 - sig))).astype(BF)
        return 0

    lax.fori_loop(0, width // TILE, gates, 0, unroll=True)

    def back(t, _):
        cols = aligned(t, TILE)
        d = dot_nt(dg[...], wg[cols, :]) + dot_nt(du[...], wu[cols, :])
        if first:
            dn_out[:, cols] = d
        else:
            d = d + dn_in[:, cols]
            dn_out[:, cols] = d[:rows]
            dn_send[:, cols] = d[rows:]
        return 0

    lax.fori_loop(0, width // TILE, back, 0, unroll=True)


def ffn_rows(meta, n2m, n2o, cm, co, chains, carried):
    first = carried is None
    arrays, tables = operands(*chains)
    rows, width = 2 * n2m.shape[0], n2m.shape[1]
    low = jax.ShapeDtypeStruct((rows, width), BF)
    return pl.pallas_call(
        functools.partial(ffn_rows_kernel, first, len(arrays), tables),
        in_specs=[SM] + [VM] * 4 + [HB] * len(arrays) + ([] if first else [VM]),
        out_specs=[VM] * (4 if first else 5),
        out_shape=(
            [jax.ShapeDtypeStruct((rows, width), F32)]
            if first
            else [jax.ShapeDtypeStruct((rows // 2, width), F32)] * 2
        )
        + [low, low, low],
        scratch_shapes=[pltpu.VMEM((rows, width), BF)] * 2
        + [pltpu.VMEM((width, width), BF)] * 3
        + [pltpu.SemaphoreType.DMA((3, CHIPS))],
        compiler_params=pltpu.CompilerParams(vmem_limit_bytes=60 * MIB),
        cost_estimate=SMALL,
        name="ffn_rows",
    )(meta, n2m, n2o, cm, co, *arrays, *(() if first else (carried,)))


def ffn_weights_kernel(first, count, table, meta, n2m, n2o, cm, co, hid, dg, du, *refs):
    pieces = refs[:count]
    refs = refs[count:]
    if not first:
        f_in = refs[0]
        refs = refs[1:]
    f_out = refs[0]
    if not first:
        f_send = refs[1]
        refs = refs[1:]
    outs = refs[1:7]
    n2, c, ws, dwg, dwu, dws, in_sem, out_sem = refs[7:]
    chip = meta[0]
    coming = load_blocks(table, pieces, ws, 2, chip, in_sem)
    rows = n2m.shape[0]
    n2[:rows] = n2m[...]
    n2[rows:] = n2o[...]
    c[:rows] = cm[...]
    c[rows:] = co[...]
    width = ws.shape[1]
    leaving = []
    for k, (lhs, rhs, dw) in enumerate(((n2, dg, dwg), (n2, du, dwu), (hid, c, dws))):

        def step(t, _, lhs=lhs, rhs=rhs, dw=dw):
            cols = aligned(t, TILE)
            dw[cols, :] = dot_tn(lhs[:, cols], rhs[...]).astype(BF)
            return 0

        lax.fori_loop(0, width // TILE, step, 0, unroll=True)
        leaving += store_blocks(dw, outs[2 * k : 2 * k + 2], table[0], k, chip, out_sem.at[k])
    finish(coming)

    def down(t, _):
        cols = aligned(t, TILE)
        f = dot(hid[...], ws[:, cols])
        if first:
            f_out[:, cols] = f
        else:
            f = f + f_in[:, cols]
            f_out[:, cols] = f[:rows]
            f_send[:, cols] = f[rows:].astype(BF)
        return 0

    lax.fori_loop(0, width // TILE, down, 0, unroll=True)
    finish(leaving)


def ffn_weights(meta, n2m, n2o, cm, co, hid, dg, du, chain, carried):
    first = carried is None
    arrays, tables = operands(chain)
    rows, width = 2 * n2m.shape[0], n2m.shape[1]
    piece = jax.ShapeDtypeStruct((4 * chain.rows, width), BF)
    return pl.pallas_call(
        functools.partial(ffn_weights_kernel, first, len(arrays), tables[0]),
        in_specs=[SM] + [VM] * 7 + [HB] * len(arrays) + ([] if first else [VM]),
        out_specs=[VM] * (1 if first else 2) + [HB] * 6,
        out_shape=(
            [jax.ShapeDtypeStruct((rows, width), F32)]
            if first
            else [
                jax.ShapeDtypeStruct((rows // 2, width), F32),
                jax.ShapeDtypeStruct((rows // 2, width), BF),
            ]
        )
        + [piece] * 6,
        scratch_shapes=[pltpu.VMEM((rows, width), BF)] * 2
        + [pltpu.VMEM((width, width), BF)] * 4
        + [pltpu.SemaphoreType.DMA((CHIPS,)), pltpu.SemaphoreType.DMA((3, CHIPS))],
        compiler_params=pltpu.CompilerParams(vmem_limit_bytes=60 * MIB),
        cost_estimate=SMALL,
        name="ffn_weights",
    )(meta, n2m, n2o, cm, co, hid, dg, du, *arrays, *(() if first else (carried,)))


OUTPUT_CHAINS = (1, 2)


def load_devices(table, refs, k, side, shard, row, count, target, lo, meta, sem, used):
    chip, core = meta[0], meta[1]
    copies = []
    for j, (index, base) in enumerate(table[1]):
        device = (chip ^ CHAIN_MASKS[k][j]) * 2 + (core if side == 0 else 1 - core)
        start = pl.multiple_of(device * shard + row, 16)
        copy = pltpu.make_async_copy(
            refs[index].at[base : base + count],
            target.at[pl.ds(start, count), lo : lo + target.shape[0]],
            sem.at[used + j],
        )
        copy.start()
        copies.append(copy)
    return copies


def load_joint(tables, refs, target, meta, sem):
    width = target.shape[0]
    shard = width // (2 * CHIPS)
    copies = []
    for k in range(3):
        for side in range(2):
            copies += load_devices(
                tables[3 * side + k], refs, k, side, shard, 0, shard, target, k * width, meta, sem, len(copies)
            )
    return copies


def load_output(tables, refs, target, meta, sem):
    shard = target.shape[0] // (2 * CHIPS)
    half = shard // 2
    copies = []
    for i, k in enumerate(OUTPUT_CHAINS):
        for side in range(2):
            copies += load_devices(
                tables[2 * side + i], refs, k, side, shard, i * half, half, target, 0, meta, sem, len(copies)
            )
    return copies


PAIR_COPIES = 128
PAD = 16


def joint_kernel(count, tables, meta, x, *refs):
    pieces = refs[:count]
    first, query, pair, gains, w, gain_rows, sem, gain_sem = refs[count:]
    width = x.shape[1]
    coming = load_joint(tables, pieces, w, meta, sem)
    shard = width // (2 * CHIPS)
    gain_copies = []
    for side in range(2):
        for j, (index, base) in enumerate(tables[3 * side + 2][1]):
            copy = pltpu.make_async_copy(
                pieces[index].at[base + shard : base + shard + 16],
                gain_rows.at[side * CHIPS + j],
                gain_sem.at[side * CHIPS + j],
            )
            copy.start()
            gain_copies.append(copy)
    value = x[...].astype(F32)
    inverse = lax.rsqrt(jnp.mean(value * value, axis=-1, keepdims=True) + NORM_EPS)
    finish(gain_copies)
    whole = jnp.sum(gain_rows[...].astype(F32), axis=0)
    gains[...] = whole[:8]
    first[...] = (value * inverse * whole[0:1]).astype(BF)
    finish(coming)
    tiles = width // TILE
    rows = x.shape[0]
    pair[2 * rows :] = jnp.zeros((PAD, width), BF)
    for part, (out, low) in enumerate(((query, 0), (pair, 0), (pair, rows))):

        def step(t, _, part=part, out=out, low=low):
            weight = w[:, aligned(t + part * tiles, TILE)]
            out[low : low + rows, aligned(t, TILE)] = dot(first[...], weight).astype(BF)
            return 0

        lax.fori_loop(0, tiles, step, 0, unroll=True)


def joint_forward(meta, x, chains):
    rows, width = x.shape
    arrays, tables = operands(*chains)
    low = jax.ShapeDtypeStruct((rows, width), BF)
    return pl.pallas_call(
        functools.partial(joint_kernel, len(arrays), tables),
        in_specs=[SM, VM] + [HB] * len(arrays),
        out_specs=[VM] * 4,
        out_shape=[
            low,
            low,
            jax.ShapeDtypeStruct((2 * rows + PAD, width), BF),
            jax.ShapeDtypeStruct((8, width), F32),
        ],
        scratch_shapes=[
            pltpu.VMEM((width, 3 * width), BF),
            pltpu.VMEM((2 * CHIPS, 16, width), BF),
            pltpu.SemaphoreType.DMA((PAIR_COPIES,)),
            pltpu.SemaphoreType.DMA((2 * CHIPS,)),
        ],
        compiler_params=pltpu.CompilerParams(vmem_limit_bytes=60 * MIB),
        cost_estimate=SMALL,
        name="joint_forward",
    )(meta, x, *arrays)


CHUNK = 128


def bias_into(bias, run, upper):
    size = 2 * CHUNK
    row = lax.broadcasted_iota(jnp.int32, (size, size), 0) & (CHUNK - 1)
    column = lax.broadcasted_iota(jnp.int32, (size, size), 1)
    own = column < CHUNK
    column = column & (CHUNK - 1)
    shift = run.bit_length() - 1
    same = (row >> shift) == (column >> shift)
    reach = jnp.where(upper, CHUNK, 0)
    seen = same & ((own & (row >= column)) | (~own & (row < reach)))
    bias[...] = jnp.where(seen, 0.0, -1e30)


def stacked(value, left):
    zero = jnp.zeros_like(value)
    return jnp.concatenate([jnp.where(left, value, zero), jnp.where(left, zero, value)], axis=0)


def probabilities(q_st, k_all, bias, scale):
    scores = dot_nt(q_st, k_all) * scale + bias[...]
    exp_scores = jnp.exp(scores - jnp.max(scores, axis=-1, keepdims=True))
    return exp_scores / jnp.sum(exp_scores, axis=-1, keepdims=True)


def context_kernel(run, head_dim, count, tables, meta, query, own, other, x, live, gains, *refs):
    pieces = refs[:count]
    ctx, h_out, n2, wo, bias, sem = refs[count:]
    rows, width = x.shape
    coming = load_output(tables, pieces, wo, meta, sem)
    bias_into(bias, run, meta[2] == 1)
    scale = head_dim ** (-0.5)
    lanes = 2 * head_dim
    left = lax.broadcasted_iota(jnp.int32, (CHUNK, lanes), 1) < head_dim

    def pair(p, _):
        cols = aligned(p, lanes)
        for chunk in range(rows // CHUNK):
            r = slice(chunk * CHUNK, (chunk + 1) * CHUNK)
            r_v = slice(rows + chunk * CHUNK, rows + (chunk + 1) * CHUNK)
            q_st = stacked(query[r, cols], left)
            k_all = jnp.concatenate([own[r, cols], other[r, cols]], axis=0)
            v_all = jnp.concatenate([own[r_v, cols], other[r_v, cols]], axis=0)
            prob = probabilities(q_st, k_all, bias, scale)
            out = dot(prob.astype(BF), v_all)
            ctx[r, cols] = jnp.where(left, out[:CHUNK], out[CHUNK:]).astype(BF)
        return 0

    lax.fori_loop(0, width // lanes, pair, 0)
    finish(coming)

    def project(t, _):
        cols = aligned(t, TILE)
        h_out[:, cols] = x[:, cols].astype(F32) + live[...] * dot(ctx[...], wo[:, cols])
        return 0

    lax.fori_loop(0, width // TILE, project, 0, unroll=True)
    h = h_out[...]
    inverse = lax.rsqrt(jnp.mean(h * h, axis=-1, keepdims=True) + NORM_EPS)
    n2[...] = (h * inverse * gains[1:2, :]).astype(BF)


def context_forward(
    run, meta, query, own, other, x, live, gains, chains
):
    rows, width = x.shape
    arrays, tables = operands(*chains)
    low = jax.ShapeDtypeStruct((rows, width), BF)
    return pl.pallas_call(
        functools.partial(context_kernel, run, width // HEADS, len(arrays), tables),
        in_specs=[SM] + [VM] * 6 + [HB] * len(arrays),
        out_specs=[VM] * 3,
        out_shape=[low, jax.ShapeDtypeStruct((rows, width), F32), low],
        scratch_shapes=[
            pltpu.VMEM((width, width), BF),
            pltpu.VMEM((2 * CHUNK, 2 * CHUNK), F32),
            pltpu.SemaphoreType.DMA((PAIR_COPIES,)),
        ],
        compiler_params=pltpu.CompilerParams(vmem_limit_bytes=60 * MIB),
        cost_estimate=SMALL,
        name="context_forward",
    )(meta, query, own, other, x, live, gains, *arrays)


def norm_back(value, gain, grad):
    inverse = lax.rsqrt(jnp.mean(value * value, axis=-1, keepdims=True) + NORM_EPS)
    scaled = grad * gain
    mean = jnp.mean(scaled * value, axis=-1, keepdims=True)
    grad_in = inverse * scaled - value * (inverse * inverse * inverse) * mean
    return grad_in, jnp.sum(grad * value * inverse, axis=0, keepdims=True)


def context_back_kernel(
    run, head_dim, count, tables, meta, dn_own, dn_got, h, cot, live, gains, query, *refs
):
    own, other = refs[:2]
    pieces = refs[2 : 2 + count]
    dh, dg2, da, dq, dkv, give, wo, bias, dctx, sem = refs[2 + count :]
    rows, width = h.shape
    coming = load_output(tables, pieces, wo, meta, sem)
    bias_into(bias, run, meta[2] == 1)
    give[2 * rows :] = jnp.zeros((PAD, width), BF)
    grad_in, dg2[...] = norm_back(h[...], gains[1:2, :], dn_own[...] + dn_got[...])
    grad = cot[...].astype(F32) + grad_in
    dh[...] = grad
    da[...] = (grad * live[...]).astype(BF)
    finish(coming)

    def project(t, _):
        cols = aligned(t, TILE)
        dctx[:, cols] = dot_nt(da[...], wo[cols, :]).astype(BF)
        return 0

    lax.fori_loop(0, width // TILE, project, 0, unroll=True)
    scale = head_dim ** (-0.5)
    lanes = 2 * head_dim
    pairs = width // lanes
    left = lax.broadcasted_iota(jnp.int32, (CHUNK, lanes), 1) < head_dim

    def pair(p, _):
        cols = aligned(p, lanes)
        v_cols = aligned(p + pairs, lanes)
        for chunk in range(rows // CHUNK):
            r = slice(chunk * CHUNK, (chunk + 1) * CHUNK)
            r_v = slice(rows + chunk * CHUNK, rows + (chunk + 1) * CHUNK)
            q_st = stacked(query[r, cols], left)
            g_st = stacked(dctx[r, cols], left)
            k_all = jnp.concatenate([own[r, cols], other[r, cols]], axis=0)
            v_all = jnp.concatenate([own[r_v, cols], other[r_v, cols]], axis=0)
            prob = probabilities(q_st, k_all, bias, scale)
            d_prob = dot_nt(g_st, v_all)
            d_score = prob * (d_prob - jnp.sum(d_prob * prob, axis=-1, keepdims=True))
            d_score = d_score.astype(BF)
            d_query = dot(d_score, k_all) * scale
            d_key = dot_tn(d_score, q_st) * scale
            d_value = dot_tn(prob.astype(BF), g_st)
            dq[r, cols] = jnp.where(left, d_query[:CHUNK], d_query[CHUNK:]).astype(BF)
            dkv[r, cols] = d_key[:CHUNK]
            dkv[r, v_cols] = d_value[:CHUNK]
            give[r, cols] = d_key[CHUNK:].astype(BF)
            give[r_v, cols] = d_value[CHUNK:].astype(BF)
        return 0

    lax.fori_loop(0, pairs, pair, 0)


def context_back(
    run, meta, dn_own, dn_got, h, cot, live, gains, query, own, other, chains
):
    rows, width = h.shape
    arrays, tables = operands(*chains)
    low = jax.ShapeDtypeStruct((rows, width), BF)
    return pl.pallas_call(
        functools.partial(context_back_kernel, run, width // HEADS, len(arrays), tables),
        in_specs=[SM] + [VM] * 9 + [HB] * len(arrays),
        out_specs=[VM] * 6,
        out_shape=[
            jax.ShapeDtypeStruct((rows, width), F32),
            jax.ShapeDtypeStruct((1, width), F32),
            low,
            low,
            jax.ShapeDtypeStruct((rows, 2 * width), F32),
            jax.ShapeDtypeStruct((2 * rows + PAD, width), BF),
        ],
        scratch_shapes=[
            pltpu.VMEM((width, width), BF),
            pltpu.VMEM((2 * CHUNK, 2 * CHUNK), F32),
            pltpu.VMEM((rows, width), BF),
            pltpu.SemaphoreType.DMA((PAIR_COPIES,)),
        ],
        compiler_params=pltpu.CompilerParams(vmem_limit_bytes=60 * MIB),
        cost_estimate=SMALL,
        name="context_back",
    )(
        meta,
        dn_own,
        dn_got,
        h,
        cot,
        live,
        gains,
        query,
        own,
        other,
        *arrays,
    )


def shard_grads(lhs, rhs_cols, dw):
    width = lhs.shape[1]
    for i, rhs in enumerate(rhs_cols):

        def step(t, _, rhs=rhs, i=i):
            cols = aligned(t, TILE)
            dw[i, cols, :] = dot_tn(lhs[:, cols], rhs()).astype(BF)
            return 0

        lax.fori_loop(0, width // TILE, step, 0, unroll=True)


def store_devices(dw, matrix, row, count, k, targets, base, meta, sem, used):
    chip, core = meta[0], meta[1]
    shard = dw.shape[1] // (2 * CHIPS)
    copies = []
    for side, target in enumerate(targets):
        for j in range(CHIPS):
            device = (chip ^ CHAIN_MASKS[k][j]) * 2 + (1 - core if side == 0 else core)
            start = pl.multiple_of(device * shard + row, 16)
            low = base + j * count
            copy = pltpu.make_async_copy(
                dw.at[matrix, pl.ds(start, count), :],
                target.at[low : low + count],
                sem.at[used + len(copies)],
            )
            copy.start()
            copies.append(copy)
    return copies


def output_grad_kernel(meta, context, grad, give, keep, dw, sem):
    shard_grads(context, (lambda: grad[...],), dw)
    half = dw.shape[1] // (4 * CHIPS)
    leaving = []
    for i, k in enumerate(OUTPUT_CHAINS):
        base = i * CHIPS * half
        leaving += store_devices(
            dw, 0, i * half, half, k, (give, keep), base, meta, sem, len(leaving)
        )
    finish(leaving)


def output_grad(meta, context, grad):
    rows, width = context.shape
    part = jax.ShapeDtypeStruct((width // 2, width), BF)
    return pl.pallas_call(
        output_grad_kernel,
        in_specs=[SM, VM, VM],
        out_specs=[HB, HB],
        out_shape=[part, part],
        scratch_shapes=[
            pltpu.VMEM((1, width, width), BF),
            pltpu.SemaphoreType.DMA((PAIR_COPIES,)),
        ],
        compiler_params=pltpu.CompilerParams(vmem_limit_bytes=60 * MIB),
        cost_estimate=SMALL,
        name="output_grad",
    )(meta, context, grad)


def joint_grad_kernel(meta, first, dq, dkv_own, dkv_got, give, keep, dkv):
    width = first.shape[1]
    rows = first.shape[0]
    chip, core = meta[0], meta[1]
    for part in range(2):
        cols = slice(part * width, (part + 1) * width)
        got = dkv_got[part * rows : (part + 1) * rows, :]
        more = jnp.where(meta[2] == 1, 0.0, got.astype(F32))
        dkv[:, cols] = (dkv_own[:, cols] + more).astype(BF)
    rights = (lambda: dq[...], lambda: dkv[:, :width], lambda: dkv[:, width:])
    shard = width // (2 * CHIPS)
    for k in range(3):
        for j in range(CHIPS):
            grad = dot_tn(first[:, aligned(chip ^ CHAIN_MASKS[k][j], 2 * shard)], rights[k]())
            low, high = grad[:shard].astype(BF), grad[shard:].astype(BF)
            at = slice((k * CHIPS + j) * shard, (k * CHIPS + j + 1) * shard)
            give[at] = jnp.where(core == 0, high, low)
            keep[at] = jnp.where(core == 0, low, high)


def joint_grad(meta, first, dq, dkv_own, dkv_got):
    rows, width = first.shape
    part = jax.ShapeDtypeStruct((3 * width // 2, width), BF)
    return pl.pallas_call(
        joint_grad_kernel,
        in_specs=[SM] + [VM] * 4,
        out_specs=[VM] * 3,
        out_shape=[part, part, jax.ShapeDtypeStruct((rows, 2 * width), BF)],
        compiler_params=pltpu.CompilerParams(vmem_limit_bytes=60 * MIB),
        cost_estimate=SMALL,
        name="joint_grad",
    )(meta, first, dq, dkv_own, dkv_got)


def input_back_kernel(count, tables, meta, dq, dkv, dh, x, gains, *refs):
    pieces = refs[:count]
    out, dg1, w, dn, sem = refs[count:]
    rows, width = x.shape
    finish(load_joint(tables, pieces, w, meta, sem))

    def step(t, _):
        cols = aligned(t, TILE)
        dn[:, cols] = dot_nt(dq[...], w[cols, :width]) + dot_nt(dkv[...], w[cols, width:])
        return 0

    lax.fori_loop(0, width // TILE, step, 0, unroll=True)
    grad_in, dg1[...] = norm_back(x[...].astype(F32), gains[0:1, :], dn[...])
    out[...] = (dh[...] + grad_in).astype(BF)


def input_back(meta, dq, dkv, dh, x, gains, chains):
    rows, width = x.shape
    arrays, tables = operands(*chains)
    return pl.pallas_call(
        functools.partial(input_back_kernel, len(arrays), tables),
        in_specs=[SM] + [VM] * 5 + [HB] * len(arrays),
        out_specs=[VM, VM],
        out_shape=[
            jax.ShapeDtypeStruct((rows, width), BF),
            jax.ShapeDtypeStruct((1, width), F32),
        ],
        scratch_shapes=[
            pltpu.VMEM((width, 3 * width), BF),
            pltpu.VMEM((rows, width), F32),
            pltpu.SemaphoreType.DMA((PAIR_COPIES,)),
        ],
        compiler_params=pltpu.CompilerParams(vmem_limit_bytes=60 * MIB),
        cost_estimate=SMALL,
        name="input_back",
    )(meta, dq, dkv, dh, x, gains, *arrays)


def adam_in_place(k, w, m, v, grad, where, rate, decay):
    grad = k * grad
    mean = BETA_ONE * m[where] + (1.0 - BETA_ONE) * grad
    square = BETA_TWO * v[where] + (1.0 - BETA_TWO) * grad * grad
    root = jnp.sqrt(square * (1.0 / (1.0 - BETA_TWO**STEP))) + ADAM_EPS
    old = w[where]
    move = mean * (rate / (1.0 - BETA_ONE**STEP)) / root
    w[where] = old - (move + (rate * decay) * old)
    m[where] = mean
    v[where] = square


def adam_kernel(meta, squares, *refs):
    sources, targets, held = refs[:21], refs[21:33], refs[33:54]
    in_sem, out_sem = refs[54:]
    core, group = meta[1], meta[2]
    (ew, em, ev, own_a, own_b, got_a, got_b, jw, jm, jv, jg, ow, om, ov, og_a, og_b) = held[:16]
    (sw, sm, sv, sg_mine, sg_got) = held[16:]
    width = own_a.shape[1]
    rows = ew.shape[0]
    started = []

    def load(index, where):
        copy = pltpu.make_async_copy(
            sources[index].at[where], held[index].at[where], in_sem.at[len(started)]
        )
        copy.start()
        started.append(copy)
        return copy

    def whole(ref):
        return (slice(None),) * len(ref.shape)

    pieces = []
    gradients = [load(i, whole(held[i])) for i in (3, 4, 5, 6)]
    for c in range(4):
        where = (slice(None), slice(2 * c * width, 2 * (c + 1) * width))
        pieces.append(("expand", c, where, [load(i, where) for i in (0, 1, 2)]))
    copies = [load(i, whole(held[i])) for i in (10, 7, 8, 9)]
    pieces.append(("joint", 0, whole(jw), copies))
    copies = [load(i, whole(held[i])) for i in (14, 15, 11, 12, 13)]
    pieces.append(("output", 0, None, copies))
    more = [load(i, whole(held[i])) for i in (19, 20)]
    for c in range(sw.shape[0]):
        pieces.append(("shrink", c, (c,), (more if c == 0 else []) + [load(i, (c,)) for i in (16, 17, 18)]))

    sums = jnp.sum(squares[...], axis=0, keepdims=True)
    total = sums[:, 0:1] + jnp.sum(sums[:, 128:] * sums[:, 128:], axis=1, keepdims=True)
    k = CLIP_LIMIT / jnp.maximum(jnp.sqrt(total), CLIP_LIMIT)
    finish(gradients)
    leaving = []

    def store(target, index, where):
        copy = pltpu.make_async_copy(
            held[index].at[where], targets[target].at[where], out_sem.at[len(leaving)]
        )
        copy.start()
        leaving.append(copy)

    block = width // CHIPS
    for kind, c, where, copies in pieces:
        finish(copies)
        if kind == "expand":
            turn = (c % 2) ^ (1 - group)
            r = slice((c // 2) * rows, (c // 2 + 1) * rows)
            for q in range(2 * CHIPS):
                near = (r, slice((q // 2) * block, (q // 2 + 1) * block))
                own = jnp.where(turn == 0, own_a[near], own_b[near])
                got = jnp.where(turn == 0, got_a[near], got_b[near])
                grad = jnp.where(core == q % 2, own, got)
                low = 2 * c * width + q * block
                cols = (slice(None), slice(low, low + block))
                adam_in_place(k, ew, em, ev, grad, cols, MATRIX_RATE, MATRIX_DECAY)
            for i in range(3):
                store(i, i, where)
        elif kind == "joint":
            for part in range(jg.shape[0]):
                cols = (slice(None), slice(part * width, (part + 1) * width))
                adam_in_place(k, jw, jm, jv, jg[part], cols, MATRIX_RATE, MATRIX_DECAY)
            for i in range(3):
                store(3 + i, 7 + i, where)
        elif kind == "output":
            half = og_a.shape[0]
            for part, grad in enumerate((og_a, og_b)):
                at = (slice(part * half, (part + 1) * half),)
                adam_in_place(k, ow, om, ov, grad[...], at, MATRIX_RATE, MATRIX_DECAY)
            for i in range(3):
                store(6 + i, 11 + i, whole(ow))
        else:
            grad = jnp.where(group == c, sg_mine[...], sg_got[...].astype(F32))
            adam_in_place(k, sw, sm, sv, grad, where, MATRIX_RATE, MATRIX_DECAY)
            for i in range(3):
                store(9 + i, 16 + i, where)
    finish(leaving)


def adam_matrices(meta, squares, expand, joint, output, shrink):
    arrays = (*expand, *joint, *output, *shrink)
    shapes = [jax.ShapeDtypeStruct(p[0].shape, F32) for p in (expand, joint, output, shrink)]
    return pl.pallas_call(
        adam_kernel,
        in_specs=[SM, VM] + [HB] * len(arrays),
        out_specs=[HB] * 12,
        out_shape=[s for s in shapes for _ in range(3)],
        scratch_shapes=[pltpu.VMEM(a.shape, a.dtype) for a in arrays]
        + [pltpu.SemaphoreType.DMA((64,)), pltpu.SemaphoreType.DMA((64,))],
        compiler_params=pltpu.CompilerParams(vmem_limit_bytes=60 * MIB),
        cost_estimate=SMALL,
        name="adam_matrices",
    )(meta, squares, *arrays)


def local_cube(
    count,
    tokens,
    depth_count,
    cotangent,
    joint_weight,
    output_weight,
    expand_weight,
    shrink_weight,
    norm_gains,
    joint_mean,
    joint_square,
    output_mean,
    output_square,
    expand_mean,
    expand_square,
    shrink_mean,
    shrink_square,
    gains_mean,
    gains_square,
):
    cube = Cube(count)
    frames, positions, width = tokens.shape
    run = positions // SETS
    group = cube.bit(cube.top)
    core = cube.bit(0)
    upper = group == 1
    second_core = core == 1
    all_frames = 2 * frames
    rows = all_frames * run
    chip = (cube.index >> 1) & (CHIPS - 1)
    meta = jnp.stack([chip, core, group]).astype(jnp.int32)

    def halves(own, other):
        return jnp.concatenate([jnp.where(upper, other, own), jnp.where(upper, own, other)], axis=0)

    def parted(value):
        first, second = value[:, :run], value[:, run:]
        own, other = jnp.where(upper, second, first), jnp.where(upper, first, second)
        return own.reshape(rows // 2, width), other.reshape(rows // 2, width)

    def from_sets(value):
        value = value.reshape(2, frames, run, width)
        own = jnp.where(upper, value[1], value[0])
        other = cube.swap(jnp.where(upper, value[0], value[1]), cube.top)
        first = jnp.where(upper, other, own)
        second = jnp.where(upper, own, other)
        return jnp.concatenate([first, second], axis=1)

    shard_rows = joint_weight.shape[0]
    lane = norm_gains.shape[1]
    small = jnp.concatenate([norm_gains.astype(BF).reshape(-1), depth_count.astype(BF)])
    small_other = cube.swap(small.reshape(1, -1), cube.top)[0]
    depth_all = halves(small[2 * lane :], small_other[2 * lane :]).astype(jnp.int32)
    gain_pair = halves(small[None, : 2 * lane], small_other[None, : 2 * lane])
    gain_pair = gain_pair.reshape(2, 2, lane).transpose(1, 0, 2)
    spread = jnp.broadcast_to(gain_pair[:, :, None, :], (2, 2, 2 * CHIPS, lane)).reshape(2, width)
    mine = (jnp.arange(width) // lane) % (2 * CHIPS) == (cube.index & (2 * CHIPS - 1))
    gain_rows = jnp.pad(jnp.where(mine[None, :], spread, 0), ((0, 14), (0, 0)))
    shards = list(first_shards(joint_weight))
    shards[2] = lax.dynamic_update_slice(shards[2], gain_rows, (shard_rows, 0))
    joint = [Blocks(shard) for shard in shards]
    x_own, x_give = parted(tokens)
    x_got = cube.swap(x_give, cube.top)
    x_rows = halves(x_own, x_got)

    def begin(name):
        return Round(cube, meta, width, name)

    one = begin("pack_one").gather(joint, 0).run(x_give)
    own_cols, give_cols, shrink_keep, shrink_give, out_a, out_b = split_weights(
        meta, expand_weight, shrink_weight, output_weight
    )
    output = [None, Blocks(out_a), Blocks(out_b)]
    joint_other = [Blocks(rows=blocks.rows) for blocks in joint]
    output_other = [None] + [Blocks(rows=blocks.rows) for blocks in output[1:]]
    two = begin("pack_two").gather(joint, 1).gather(output, 0).run(one.got, give_cols)
    shrink_other = cube.swap(after(shrink_give, two.got, x_got), cube.top)
    got_cols = cube.swap(after(give_cols, two.got, x_got), 0)
    three = begin("pack_three").gather(joint, 2).gather(output, 1)
    three = three.core(joint, joint_other, 0, 4).run(two.got, x_got)
    units = Jobs(width)
    unit_rows = 2 * shard_rows
    for kind in range(2):
        target = units.output(2 * unit_rows)
        for turn_index in range(2):
            unit = turn_index * 2 + kind
            base = turn_index * unit_rows
            low, high = (base, base + shard_rows), (base + shard_rows, base)
            units.copy(own_cols, unit * shard_rows, target, low, shard_rows)
            units.copy(got_cols, unit * shard_rows, target, high, shard_rows)
    target = units.output(2 * unit_rows)
    units.copy(shrink_other, 0, target, 0, unit_rows)
    units.copy(shrink_keep, 0, target, unit_rows, unit_rows)
    units = units.run(meta, "expand_units", three.packed)
    part_a = [Blocks(unit, unit_rows) for unit in units]
    part_b = [Blocks(rows=unit_rows) for unit in units]
    for blocks, unit in zip(part_b, units):
        blocks.arrived(unit, unit_rows, 1)

    cot_own, cot_give = parted(cotangent)
    cot_got = cube.swap(after(cot_give, three.packed, shrink_other), cube.top)
    late = begin("pack_late").core(joint, joint_other, 4, 8)
    late = late.run(three.got, three.core_got, units, x_rows)
    first_units = after(units, three.got, three.core_got)
    got_four = [cube.swap(unit, 1 + axis) for axis, unit in enumerate(first_units)]
    for k in range(3):
        part_a[k].arrived(got_four[k], 0, 1)
        part_b[k].arrived(got_four[k], unit_rows, 1)

    position = group * run + jnp.arange(run)
    live = (position[None, :] < depth_all[:, None]).astype(F32).reshape(rows, 1)

    first, query, key_value, gains_all = joint_forward(meta, x_rows, joint + joint_other)
    key_value_other = cube.swap(key_value, cube.top)
    five = begin("pack_five").gather(part_a, 1).gather(part_b, 1).run(got_four, key_value, cot_got)
    last = begin("pack_output").gather(output, 2).run(five.packed)
    output_core = begin("pack_core").core(output, output_other, 0, 8).run(last.got)
    seven = begin("pack_seven").gather(part_a, 2)
    seven = seven.run(five.got, key_value_other, output_core.packed)
    cot_live = (halves(cot_own, after(cot_got, key_value)).astype(F32) * live).astype(BF)
    cot_other = cube.swap(after(cot_live, five.got, key_value_other), 0)

    output_chains = output[1:] + output_other[1:]
    context, middle, second = context_forward(
        run,
        meta,
        query,
        key_value,
        key_value_other,
        x_rows,
        live,
        gains_all,
        output_chains,
    )
    second_other = cube.swap(second, 0)
    eight = begin("pack_eight").gather(part_b, 2).run(
        seven.packed, cot_other, gate=(seven.got, second_other)
    )
    row_args = (meta, second, second_other, cot_live, cot_other)
    dn_a, *kept_a = ffn_rows(*row_args, part_a, None)
    f_a, *grad_a = ffn_weights(*row_args, *kept_a, part_a[2], None)
    dn_own, dn_send, *kept_b = ffn_rows(*row_args, part_b, after(dn_a, f_a))
    dn_got = cube.swap(dn_send, 0)
    f_own, f_send, *grad_b = ffn_weights(*row_args, *kept_b, part_b[2], f_a)

    outcome = {}

    def expand_final(key, kind):
        def final(jobs, got, keep, count):
            if key not in outcome:
                outcome[key] = (jobs.output(2 * shard_rows, F32), jobs.output(2 * shard_rows, F32))
            own, give = outcome[key]
            half = count // 2
            for target, offset in ((own, (0, half)), (give, (half, 0))):
                got_at = tuple(got[1] + o for o in offset)
                keep_at = tuple(keep[1] + o for o in offset)
                jobs.add(got[0], got_at, keep[0], keep_at, target, kind * shard_rows, half)

        return final

    def plain_final(key):
        def final(jobs, got, keep, count):
            outcome[key] = jobs.output(count, F32)
            jobs.add(got[0], got[1], keep[0], keep[1], outcome[key], 0, count)

        return final

    def ffn_sums(grads, name):
        finals = (expand_final(name, 0), expand_final(name, 1), plain_final(name + "_shrink"))
        block = grads[0].shape[0] // 4
        return [Sums((grads[2 * k], 0), (grads[2 * k + 1], 0), block, finals[k]) for k in range(3)]

    def turn(name, work, *earlier, **options):
        return reduce_round(cube, meta, width, name, work, *earlier, **options)

    def core_sums(name, tensors, *waits):
        jobs = Jobs(width)
        result = []
        payload = []
        for k in range(3):
            rows_out = sum(4 * c for *_, chains in tensors for kk, c in chains if kk == k)
            payload.append(jobs.output(rows_out))
        filled_rows = [0, 0, 0]
        for key, got, keep, chains in tensors:
            row, sums = 0, [None] * 3
            for k, c in chains:
                own = jobs.output(4 * c)
                send_row = filled_rows[k]
                jobs.add(got, row + 4 * c, keep, row + 4 * c, payload[k], send_row, 4 * c)
                jobs.add(got, row, keep, row, own, 0, 4 * c)
                filled_rows[k] += 4 * c
                sums[k] = (own, send_row, c)
                row += CHIPS * c
            result.append((key, sums))
        out = jobs.run(meta, name, waits=waits)
        made = []
        for key, sums in result:
            made.append(
                [
                    None
                    if s is None
                    else Sums((out[s[0]], 0), (out[payload[k]], s[1]), s[2], plain_final((key, k)))
                    for k, s in enumerate(sums)
                ]
            )
        return made, [out[p] for p in payload]

    shrunk_got = cube.swap(f_send, 0)
    shrunk = f_own + shrunk_got.astype(F32)
    result_rows = (middle + live * shrunk).astype(BF).reshape(2, frames, run, width)
    result_own = jnp.where(upper, result_rows[1], result_rows[0])
    result_give = jnp.where(upper, result_rows[0], result_rows[1])
    result_got = cube.swap(result_give, cube.top)
    result = jnp.concatenate(
        [jnp.where(upper, result_got, result_own), jnp.where(upper, result_own, result_got)], axis=1
    )
    sums_a = ffn_sums(grad_a, "a")
    sums_b = ffn_sums(grad_b, "b")
    turn_one, _ = turn("turn_one", [(sums_a, 0)], eight.got)
    turn_two, _ = turn("turn_two", [(sums_b, 0)], turn_one)

    grad_middle, grad_gain_two, grad_branch, d_query, dkv_own, dkv_give = context_back(
        run,
        meta,
        after(dn_own, result_give, turn_one),
        dn_got,
        middle,
        cot_live,
        live,
        gains_all,
        query,
        key_value,
        key_value_other,
        output_chains,
    )
    turn_three, packed_three = turn(
        "turn_three", [(sums_a, 1), (sums_b, 1)], turn_two, dkv_give, result_got
    )
    dkv_got = cube.swap(dkv_give, cube.top)
    output_give, output_keep = output_grad(meta, context, after(grad_branch, packed_three))
    joint_give, joint_keep, dkv = joint_grad(
        meta, first, d_query, dkv_own, after(dkv_got, output_give)
    )
    turn_four, packed_four = turn(
        "turn_four", [(sums_a, 2), (sums_b, 2)], turn_three, dkv_got, waits=(joint_give,)
    )
    joint_got = cube.swap(after(joint_give, packed_four), 0)
    output_got = cube.swap(after(output_give, packed_four), 0)
    grad_inputs, grad_gain_one = input_back(
        meta,
        d_query,
        after(dkv, packed_four),
        grad_middle,
        x_rows,
        gains_all,
        joint + joint_other,
    )
    half_shard = shard_rows // 2
    (sums_j, sums_o), sends = core_sums(
        "joint_core",
        [
            ("joint", joint_got, joint_keep, [(k, shard_rows) for k in range(3)]),
            ("output", output_got, output_keep, [(k, half_shard) for k in OUTPUT_CHAINS]),
        ],
        grad_inputs,
    )
    turn_seven = []
    for axis in range(3):
        k = (axis - 2) % 3
        array = cube.swap(sends[k], 1 + axis)
        turn_seven.append(array)
        for sums in (sums_j, sums_o):
            if sums[k] is not None:
                sums[k].got = (array, sums[k].send[1])
    grad_inputs = from_sets(after(grad_inputs, sends[0]))
    _, out_five = turn(
        "turn_five",
        [(sums_a, 3), (sums_b, 3)],
        turn_four,
        sends[0],
        squares=True,
    )
    expand_own_a, expand_give_a = (out_five[i] for i in outcome["a"])
    expand_own_b, expand_give_b = (out_five[i] for i in outcome["b"])
    shrink_first = out_five[outcome["a_shrink"]]
    shrink_mine = out_five[outcome["b_shrink"]]
    expand_got_a = cube.swap(after(expand_give_a, sends[0]), 0)
    expand_got_b = cube.swap(after(expand_give_b, expand_got_a), 0)
    turn_nine, out_nine = turn(
        "turn_nine",
        [(sums_o, 1), (sums_j, 1)],
        turn_seven,
        grad_inputs,
        waits=(out_five[-1],),
    )
    shrink_got = cube.swap(after(shrink_first.astype(BF), out_nine[0]), cube.top)
    turn_ten, out_ten = turn(
        "turn_ten", [(sums_o, 2), (sums_j, 2)], turn_nine, shrink_got
    )
    _, out_last = turn(
        "turn_last",
        [(sums_o, 3), (sums_j, 3)],
        turn_ten,
        squares=True,
        norm=(count, out_five[-1], grad_gain_one, grad_gain_two),
    )
    grad_output = [out_last[outcome[("output", k)]] for k in OUTPUT_CHAINS]
    grad_joint = jnp.stack([out_last[outcome[("joint", k)]] for k in range(3)])

    squares = lax.all_to_all(out_last[-1], "fsdp", 0, 0, tiled=True)
    gains_sum = jnp.sum(squares[:, 128:], axis=0)
    total_sq = jnp.sum(squares[:, 0]) + jnp.sum(gains_sum * gains_sum)
    grad_gains = lax.dynamic_index_in_dim(
        gains_sum.reshape(2, count, lane), cube.index, 1, keepdims=False
    )
    grad_norm_value = jnp.sqrt(total_sq)
    factor = CLIP_LIMIT / jnp.maximum(grad_norm_value, CLIP_LIMIT)
    new = adam_matrices(
        meta,
        squares,
        (
            expand_weight,
            expand_mean,
            expand_square,
            expand_own_a,
            expand_own_b,
            expand_got_a,
            expand_got_b,
        ),
        (joint_weight, joint_mean, joint_square, grad_joint),
        (output_weight, output_mean, output_square, *grad_output),
        (shrink_weight, shrink_mean, shrink_square, shrink_mine, shrink_got),
    )
    expand_new, joint_new, output_new, shrink_new = (new[i : i + 3] for i in (0, 3, 6, 9))
    gains_new = adam_step(norm_gains, factor * grad_gains, gains_mean, gains_square, GAIN_RATE, 0.0)
    return (
        result,
        grad_inputs,
        grad_norm_value,
        *joint_new,
        *output_new,
        *expand_new,
        *shrink_new,
        *gains_new,
    )


def solution(mesh):
    rows = P("fsdp", None)
    cube = P("fsdp", None, None)
    inner = P(None, "fsdp", None)
    gains = P(None, "fsdp")
    count = mesh.shape["fsdp"]

    def body(*args):
        return (local_cube if count == 4 * CHIPS else local_general)(count, *args)

    return jax.shard_map(
        body,
        mesh=mesh,
        in_specs=(cube, P("fsdp"), cube, rows, rows, rows, inner, gains)
        + (rows,) * 6
        + (inner, inner, gains, gains),
        out_specs=(cube, cube, P()) + (rows,) * 9 + (inner,) * 3 + (gains,) * 3,
        check_vma=False,
    )
```

```python
import functools

import jax
import jax.numpy as jnp
from jax import lax
from jax.experimental import pallas as pl
from jax.experimental.pallas import tpu as pltpu
from jax.sharding import PartitionSpec as P

HEADS = 16
SETS = 2
STEP = 10

NORM_EPS = 1e-05
BETA_ONE = 0.9
BETA_TWO = 0.95
ADAM_EPS = 1e-08
MATRIX_RATE = 0.08
GAIN_RATE = 1.0
MATRIX_DECAY = 0.1
CLIP_LIMIT = 1.0

BF = jnp.bfloat16
F32 = jnp.float32


def dot(a, b):
    return lax.dot_general(a, b, (((1,), (0,)), ((), ())), preferred_element_type=F32)


def dot_nt(a, b):
    return lax.dot_general(a, b, (((1,), (1,)), ((), ())), preferred_element_type=F32)


def dot_tn(a, b):
    return lax.dot_general(a, b, (((0,), (0,)), ((), ())), preferred_element_type=F32)


def adam_step(weight, grad_value, mean_old, square_old, learn_rate, weight_decay):
    mean_new = BETA_ONE * mean_old + (1.0 - BETA_ONE) * grad_value
    square_new = BETA_TWO * square_old + (1.0 - BETA_TWO) * grad_value * grad_value
    mean_hat = mean_new / (1.0 - BETA_ONE**STEP)
    square_hat = square_new / (1.0 - BETA_TWO**STEP)
    weight_new = weight - learn_rate * (
        mean_hat / (jnp.sqrt(square_hat) + ADAM_EPS) + weight_decay * weight
    )
    return (weight_new, mean_new, square_new)


class Cube:
    def __init__(self, count):
        self.count = count
        self.bits = count.bit_length() - 1
        self.top = self.bits - 1
        self.index = lax.axis_index("fsdp")
        chip = list(range(1, self.top))
        third = max(1, len(chip) // 3)
        self.orders = [chip[third * k :] + chip[: third * k] for k in range(3)]

    def bit(self, b):
        return (self.index >> b) & 1

    def swap(self, value, b):
        pairs = [(i, i ^ (1 << b)) for i in range(self.count)]
        return lax.ppermute(value, "fsdp", pairs)

    def gather(self, value, bits, lead=0):
        have = []
        for b in bits:
            other = self.swap(value, b)
            mine = self.bit(b) == 1
            axis = lead + sum(1 for h in have if h > b)
            low = jnp.where(mine, other, value)
            high = jnp.where(mine, value, other)
            value = jnp.stack([low, high], axis=axis)
            have.append(b)
        return value

    def reduce(self, value, have, bits, lead=0, last=F32):
        have = list(have)
        for step, b in enumerate(bits):
            axis = lead + sum(1 for h in have if h > b)
            mine = self.bit(b)
            send = lax.dynamic_index_in_dim(value, 1 - mine, axis, keepdims=False).astype(BF)
            keep = lax.dynamic_index_in_dim(value, mine, axis, keepdims=False)
            other = self.swap(send, b)
            value = keep.astype(F32) + other.astype(F32)
            if step < len(bits) - 1:
                value = value.astype(BF)
            have.remove(b)
        return value.astype(last)

    def total(self, value):
        for b in range(self.bits):
            value = value + self.swap(value, b)
        return value


def cuts(width, parts=3, unit=128):
    units = width // unit
    sizes = [units // parts + (1 if k < units % parts else 0) for k in range(parts)]
    edges = [0]
    for size in sizes:
        edges.append(edges[-1] + size * unit)
    return edges


def local_general(
    count,
    tokens,
    depth_count,
    cotangent,
    joint_weight,
    output_weight,
    expand_weight,
    shrink_weight,
    norm_gains,
    joint_mean,
    joint_square,
    output_mean,
    output_square,
    expand_mean,
    expand_square,
    shrink_mean,
    shrink_square,
    gains_mean,
    gains_square,
):
    cube = Cube(count)
    half = count // 2
    own_bits = cube.top
    frames, positions, width = tokens.shape
    run = positions // SETS
    in_set = cube.bit(cube.top)
    upper = in_set == 1
    all_frames = 2 * frames
    rows = all_frames * run
    hidden_width = expand_weight.shape[1] // 2
    head_dim = width // HEADS

    def to_sets(value):
        first, second = value[:, :run], value[:, run:]
        other = cube.swap(jnp.where(upper, first, second), cube.top)
        own = jnp.where(upper, second, first)
        low = jnp.where(upper, other, own)
        high = jnp.where(upper, own, other)
        return jnp.concatenate([low, high], axis=0)

    def from_sets(value):
        value = value.reshape(2, frames, run, value.shape[-1])
        own = jnp.where(upper, value[1], value[0])
        other = cube.swap(jnp.where(upper, value[0], value[1]), cube.top)
        first = jnp.where(upper, other, own)
        second = jnp.where(upper, own, other)
        return jnp.concatenate([first, second], axis=1)

    position_index = jnp.arange(positions)
    live_here = (position_index[None, :] < depth_count[:, None]).astype(F32)[:, :, None]
    masked = (cotangent.astype(F32) * live_here).astype(BF)

    gains_local = norm_gains.astype(BF)
    gains_all = cube.gather(gains_local, range(cube.bits), lead=1)
    gains_all = gains_all.reshape(2, width).astype(F32)

    def gather_matrix(shard, order, lead=0):
        return cube.gather(shard, list(order) + [0], lead=lead)

    joint_low = joint_weight.astype(BF)
    joint_parts = [
        gather_matrix(joint_low[:, k * width : (k + 1) * width], cube.orders[k]).reshape(width, width)
        for k in range(3)
    ]
    x_rows = to_sets(tokens).reshape(rows, width).astype(F32)
    live = to_sets(live_here).reshape(rows, 1)
    cot = to_sets(masked).reshape(rows, width)

    output_low = output_weight.astype(BF)
    expand_low = expand_weight.astype(BF)
    wide = hidden_width // 4
    edge = [0, wide, (wide + hidden_width) // 2, hidden_width]
    expand_shards = []
    for k in range(3):
        gate_cols = expand_low[:, edge[k] : edge[k + 1]]
        up_cols = expand_low[:, hidden_width + edge[k] : hidden_width + edge[k + 1]]
        parts = ([output_low] if k == 0 else []) + [gate_cols, up_cols]
        expand_shards.append(jnp.concatenate(parts, axis=1))
    expand_parts = [
        gather_matrix(expand_shards[k], cube.orders[k]).reshape(width, -1) for k in range(3)
    ]
    output_full = expand_parts[0][:, :width]
    gate_full = [expand_parts[0][:, width : 2 * width]] + [
        expand_parts[k][:, : edge[k + 1] - edge[k]] for k in (1, 2)
    ]
    up_full = [expand_parts[0][:, 2 * width :]] + [
        expand_parts[k][:, edge[k + 1] - edge[k] :] for k in (1, 2)
    ]

    shrink_low = shrink_weight.astype(BF)
    shrink_mine = jnp.where(upper, shrink_low[1], shrink_low[0])
    shrink_send = jnp.where(upper, shrink_low[0], shrink_low[1])
    shrink_other = cube.swap(shrink_send, cube.top)
    shrink_pair = jnp.stack(
        [jnp.where(upper, shrink_other, shrink_mine), jnp.where(upper, shrink_mine, shrink_other)]
    )
    col = cuts(width)
    shrink_parts = [
        gather_matrix(shrink_pair[:, :, col[k] : col[k + 1]], cube.orders[k], lead=1).reshape(
            hidden_width, -1
        )
        for k in range(3)
    ]

    inv_one = lax.rsqrt(jnp.mean(x_rows * x_rows, axis=-1, keepdims=True) + NORM_EPS)
    first = (x_rows * inv_one * gains_all[0]).astype(BF)
    query, key_own, value_own = [dot(first, joint_parts[k]).astype(BF) for k in range(3)]
    key_value = cube.swap(jnp.concatenate([key_own, value_own], axis=1), cube.top)

    def heads(value):
        return value.reshape(all_frames, run, HEADS, head_dim)

    q_h = heads(query)
    k_h = jnp.concatenate([heads(key_value[:, :width]), heads(key_own)], axis=1)
    v_h = jnp.concatenate([heads(key_value[:, width:]), heads(value_own)], axis=1)
    scale = head_dim ** (-0.5)
    scores = jnp.einsum("fphd,fkhd->fhpk", q_h, k_h, preferred_element_type=F32) * scale
    row = jnp.arange(run)[:, None]
    column = jnp.arange(2 * run)[None, :]
    seen = jnp.where(column < run, upper, row >= column - run)
    scores = jnp.where(seen, scores, -1e30)
    exp_scores = jnp.exp(scores - jnp.max(scores, axis=-1, keepdims=True))
    attention = exp_scores / jnp.sum(exp_scores, axis=-1, keepdims=True)
    attention_low = attention.astype(BF)
    context = (
        jnp.einsum("fhpk,fkhd->fphd", attention_low, v_h, preferred_element_type=F32)
        .reshape(rows, width)
        .astype(BF)
    )
    middle = x_rows + live * dot(context, output_full)
    inv_two = lax.rsqrt(jnp.mean(middle * middle, axis=-1, keepdims=True) + NORM_EPS)
    second = (middle * inv_two * gains_all[1]).astype(BF)
    gate = [dot(second, w) for w in gate_full]
    up = [dot(second, w) for w in up_full]
    hidden = jnp.concatenate(
        [(jax.nn.silu(g) * u).astype(BF) for g, u in zip(gate, up)], axis=1
    )
    shrunk = jnp.concatenate([dot(hidden, w) for w in shrink_parts], axis=1)
    result = from_sets((middle + live * shrunk).astype(BF))

    def reduce_matrix(grad, order, lead=0, block=None):
        bits = list(range(own_bits))
        shape = grad.shape
        if lead:
            grad = grad.reshape((2,) + (2,) * own_bits + (shape[0] // 2 // half, shape[1]))
        else:
            grad = grad.reshape((2,) * own_bits + (shape[0] // half, shape[1]))
        return cube.reduce(grad, bits, [0] + list(order), lead=lead)

    grad_shrink_parts = [
        reduce_matrix(dot_tn(hidden, cot[:, col[k] : col[k + 1]]).astype(BF), cube.orders[k], lead=1)
        for k in range(3)
    ]
    grad_shrink_pair = jnp.concatenate(grad_shrink_parts, axis=-1)
    shrink_keep = jnp.where(upper, grad_shrink_pair[1], grad_shrink_pair[0])
    shrink_give = jnp.where(upper, grad_shrink_pair[0], grad_shrink_pair[1]).astype(BF)
    shrink_got = cube.swap(shrink_give, cube.top).astype(F32)
    grad_shrink = jnp.stack(
        [jnp.where(upper, shrink_got, shrink_keep), jnp.where(upper, shrink_keep, shrink_got)]
    )

    grad_hidden = sum(dot_nt(cot[:, col[k] : col[k + 1]], shrink_parts[k]) for k in range(3))
    grad_second = 0.0
    grad_expand_parts = []
    for k in range(3):
        d_hid = grad_hidden[:, edge[k] : edge[k + 1]]
        sig = jax.nn.sigmoid(gate[k])
        d_gate = (d_hid * up[k] * sig * (1.0 + gate[k] * (1.0 - sig))).astype(BF)
        d_up = (d_hid * gate[k] * sig).astype(BF)
        both = jnp.concatenate([d_gate, d_up], axis=1)
        weight_pair = jnp.concatenate([gate_full[k], up_full[k]], axis=1)
        grad_second = grad_second + dot_nt(both, weight_pair)
        grad_expand_parts.append(
            reduce_matrix(dot_tn(second, both).astype(BF), cube.orders[k])
        )
    grad_expand = jnp.concatenate(
        [grad_expand_parts[k][:, : edge[k + 1] - edge[k]] for k in range(3)]
        + [grad_expand_parts[k][:, edge[k + 1] - edge[k] :] for k in range(3)],
        axis=1,
    )

    def normalize_back(values, inverse, gain_row, grad_out):
        scaled = grad_out * gain_row
        grad_in = inverse * scaled - values * inverse * inverse * inverse * jnp.mean(
            scaled * values, axis=-1, keepdims=True
        )
        return (grad_in, jnp.sum(grad_out * values * inverse, axis=0))

    grad_mid_norm, grad_gain_two = normalize_back(middle, inv_two, gains_all[1], grad_second)
    grad_middle = cot.astype(F32) + grad_mid_norm
    grad_branch = (grad_middle * live).astype(BF)
    grad_context = dot_nt(grad_branch, output_full).astype(BF)

    g_h = heads(grad_context)
    grad_attention = jnp.einsum("fphd,fkhd->fhpk", g_h, v_h, preferred_element_type=F32)
    grad_value = jnp.einsum("fhpk,fphd->fkhd", attention_low, g_h, preferred_element_type=F32)
    grad_scores = attention * (
        grad_attention - jnp.sum(grad_attention * attention, axis=-1, keepdims=True)
    )
    grad_scores = grad_scores.astype(BF)
    grad_query = (
        jnp.einsum("fhpk,fkhd->fphd", grad_scores, k_h, preferred_element_type=F32) * scale
    )
    grad_key = jnp.einsum("fhpk,fphd->fkhd", grad_scores, q_h, preferred_element_type=F32) * scale
    give = jnp.concatenate(
        [grad_key[:, :run].reshape(rows, width), grad_value[:, :run].reshape(rows, width)], axis=1
    ).astype(BF)
    got = cube.swap(give, cube.top).astype(F32)
    got = jnp.where(upper, 0.0, got)
    d_query = grad_query.reshape(rows, width).astype(BF)
    d_key = (grad_key[:, run:].reshape(rows, width) + got[:, :width]).astype(BF)
    d_value = (grad_value[:, run:].reshape(rows, width) + got[:, width:]).astype(BF)

    grad_output = reduce_matrix(dot_tn(context, grad_branch).astype(BF), cube.orders[0])
    joint_grads = [
        reduce_matrix(dot_tn(first, d).astype(BF), cube.orders[k])
        for k, d in enumerate((d_query, d_key, d_value))
    ]
    grad_joint = jnp.concatenate(joint_grads, axis=1)
    grad_first = sum(
        dot_nt(d, w) for d, w in zip((d_query, d_key, d_value), joint_parts)
    )
    grad_in_norm, grad_gain_one = normalize_back(x_rows, inv_one, gains_all[0], grad_first)
    grad_inputs = from_sets((grad_middle + grad_in_norm).astype(BF))

    gains_term = jnp.stack([grad_gain_one, grad_gain_two]).reshape((2,) + (2,) * cube.bits + (-1,))
    bits = list(range(cube.bits))
    have = list(bits)
    for b in bits:
        axis = 1 + sum(1 for h in have if h > b)
        mine = cube.bit(b)
        send = lax.dynamic_index_in_dim(gains_term, 1 - mine, axis, keepdims=False)
        keep = lax.dynamic_index_in_dim(gains_term, mine, axis, keepdims=False)
        gains_term = keep + cube.swap(send, b)
        have.remove(b)
    grad_gains = gains_term

    reduced = (grad_joint, grad_output, grad_expand, grad_shrink, grad_gains)
    local_sq = sum(jnp.sum(g * g) for g in reduced)
    total_sq = cube.total(jnp.broadcast_to(local_sq, (8, 128)))[0, 0]
    grad_norm_value = jnp.sqrt(total_sq)
    factor = CLIP_LIMIT / jnp.maximum(grad_norm_value, CLIP_LIMIT)
    joint_new = adam_step(
        joint_weight, factor * reduced[0], joint_mean, joint_square, MATRIX_RATE, MATRIX_DECAY
    )
    output_new = adam_step(
        output_weight, factor * reduced[1], output_mean, output_square, MATRIX_RATE, MATRIX_DECAY
    )
    expand_new = adam_step(
        expand_weight, factor * reduced[2], expand_mean, expand_square, MATRIX_RATE, MATRIX_DECAY
    )
    shrink_new = adam_step(
        shrink_weight, factor * reduced[3], shrink_mean, shrink_square, MATRIX_RATE, MATRIX_DECAY
    )
    gains_new = adam_step(norm_gains, factor * reduced[4], gains_mean, gains_square, GAIN_RATE, 0.0)
    return (
        result,
        grad_inputs,
        grad_norm_value,
        *joint_new,
        *output_new,
        *expand_new,
        *shrink_new,
        *gains_new,
    )


CHIPS = 8
CHAIN_BITS = [[(k + t) % 3 for t in range(3)] for k in range(3)]
CHAIN_MASKS = [
    [sum(((j >> t) & 1) << bits[t] for t in range(3)) for j in range(CHIPS)] for bits in CHAIN_BITS
]
VM = pl.BlockSpec(memory_space=pltpu.VMEM)
HB = pl.BlockSpec(memory_space=pltpu.HBM)
SM = pl.BlockSpec(memory_space=pltpu.SMEM)
MIB = 1 << 20
SMALL = pl.CostEstimate(flops=1, bytes_accessed=1, transcendentals=0)


def aligned(index, size):
    return pl.ds(pl.multiple_of(index * size, size), size)


def after(value, *earlier):
    return lax.optimization_barrier((value, earlier))[0]


def plus(a, b):
    return (a.astype(F32) + b.astype(F32)).astype(BF)


class Jobs:
    def __init__(self, width):
        self.width = width
        self.inputs, self.outputs, self.work = [], [], []

    def source(self, array):
        for i, known in enumerate(self.inputs):
            if known is array:
                return i
        self.inputs.append(array)
        return len(self.inputs) - 1

    def output(self, rows, dtype=BF):
        self.outputs.append(jax.ShapeDtypeStruct((rows, self.width), dtype))
        return len(self.outputs) - 1

    def copy(self, array, row, target, target_row, count):
        self.work.append((self.source(array), row, None, 0, target, target_row, count))

    def add(self, a, a_row, b, b_row, target, target_row, count):
        self.work.append((self.source(a), a_row, self.source(b), b_row, target, target_row, count))

    def run(self, meta, name, *earlier, squares=False, norm=(), waits=()):
        inputs = after(self.inputs, *earlier) if earlier else self.inputs
        adds = [w for w in self.work if w[2] is not None]
        rows = sum(w[6] for w in adds)
        moved = sum(w[6] for w in self.work if w[2] is None)
        scratch = [pltpu.SemaphoreType.DMA((3, len(self.work)))]
        scratch += [pltpu.VMEM((max(moved, 16), self.width), BF)]
        if adds:
            scratch += [pltpu.VMEM((rows, self.width), BF)] * 3
            scratch += [pltpu.VMEM((rows, self.width), F32)]
        shapes = list(self.outputs)
        if squares:
            lines = 1 + (len(norm) - 2) * self.width // 128
            shape = (norm[0], (lines + 7) // 8 * 8, 128) if norm else (8, self.width)
            shapes.append(jax.ShapeDtypeStruct(shape, F32))
        more = list(norm[1:])
        scratch += [pltpu.VMEM((8, self.width), F32)] if squares else []
        return pl.pallas_call(
            functools.partial(
                jobs_kernel, self.work, len(inputs), self.outputs, squares, len(more), len(waits)
            ),
            in_specs=[SM] + [HB] * len(inputs) + [VM] * len(more) + [HB] * len(waits),
            out_specs=[HB] * len(self.outputs) + ([VM] if squares else []),
            out_shape=shapes,
            scratch_shapes=scratch,
            compiler_params=pltpu.CompilerParams(vmem_limit_bytes=60 * MIB),
            cost_estimate=SMALL,
            name=name,
        )(meta, *inputs, *more, *waits)


def jobs_kernel(work, count, outputs, squares, more, waits, meta, *refs):
    sources, norm = refs[:count], refs[count : count + more]
    refs = refs[count + more + waits :]
    targets = refs[: len(outputs)]
    refs = refs[len(outputs) :]
    if squares:
        square_out, square_ref = refs[0], refs[-1]
        refs = refs[1:-1]
    sem = refs[0]
    core = meta[1]

    def part(ref, row, rows):
        if isinstance(row, tuple):
            start = pl.multiple_of(jnp.where(core == 0, row[0], row[1]), 16)
            return ref.at[pl.ds(start, rows)]
        return ref.at[row : row + rows]

    coming, leaving = [], []
    at, moved = 0, 0
    transit = refs[1]
    refs = refs[:1] + refs[2:]
    for i, (a, a_row, b, b_row, target, target_row, rows) in enumerate(work):
        if b is None:
            spot = slice(moved, moved + rows)
            copy = pltpu.make_async_copy(part(sources[a], a_row, rows), transit.at[spot], sem.at[0, i])
            copy.start()
            coming.append(((copy,), spot))
            moved += rows
            continue
        spot = slice(at, at + rows)
        pair = (
            pltpu.make_async_copy(part(sources[a], a_row, rows), refs[1].at[spot], sem.at[0, i]),
            pltpu.make_async_copy(part(sources[b], b_row, rows), refs[2].at[spot], sem.at[1, i]),
        )
        for copy in pair:
            copy.start()
        coming.append((pair, spot))
        at += rows
    if squares:
        square_ref[...] = jnp.zeros_like(square_ref)
    for i, (a, a_row, b, b_row, target, target_row, rows) in enumerate(work):
        pair, spot = coming[i]
        finish(pair)
        if b is None:
            copy = pltpu.make_async_copy(
                transit.at[spot], part(targets[target], target_row, rows), sem.at[2, i]
            )
            copy.start()
            leaving.append(copy)
            continue
        wide = outputs[target].dtype == F32
        store = refs[4] if wide else refs[3]
        if not wide and not squares:
            store[spot] = plus(refs[1][spot], refs[2][spot])
        else:
            total = refs[1][spot].astype(F32) + refs[2][spot].astype(F32)
            store[spot] = total.astype(store.dtype)
            if wide:
                square = (total * total).reshape(rows // 8, 8, total.shape[1])
                square_ref[...] += jnp.sum(square, axis=0)
        copy = pltpu.make_async_copy(
            store.at[spot], part(targets[target], target_row, rows), sem.at[2, i]
        )
        copy.start()
        leaving.append(copy)
    if squares and not norm:
        square_out[...] = square_ref[...]
    if norm:
        total = jnp.sum(square_ref[...]) + jnp.sum(norm[0][...])
        square_out[...] = jnp.zeros_like(square_out)
        square_out[:, 0, :] = jnp.full((square_out.shape[0], 128), total, F32)
        line = 1
        for ref in norm[1:]:
            for low in range(0, ref.shape[1], 128):
                value = jnp.broadcast_to(ref[:, low : low + 128], (square_out.shape[0], 128))
                square_out[:, line, :] = value
                line += 1
    finish(leaving)


class Blocks:
    def __init__(self, own=None, rows=None):
        self.rows = own.shape[0] if rows is None else rows
        self.held = [] if own is None else [(own, 0)]

    def arrived(self, array, row, count):
        for j in range(count):
            self.held.append((array, row + j * self.rows))


def place(jobs, held, rows, target, target_row):
    start = 0
    while start < len(held):
        array, row = held[start]
        stop = start + 1
        while stop < len(held) and held[stop][0] is array and held[stop][1] == row + (stop - start) * rows:
            stop += 1
        jobs.copy(array, row, target, target_row + start * rows, (stop - start) * rows)
        start = stop


class Round:
    def __init__(self, cube, meta, width, name):
        self.cube, self.meta, self.name = cube, meta, name
        self.jobs = Jobs(width)
        self.axis_work = []
        self.core_work = []

    def gather(self, chains, level):
        self.axis_work.append((chains, level))
        return self

    def core(self, chains, others, start, stop):
        self.core_work.append((chains, others, start, stop))
        return self

    def run(self, *earlier, gate=()):
        jobs = self.jobs
        filled = []
        for axis in range(3):
            held = []
            for chains, level in self.axis_work:
                blocks = chains[(axis - level) % 3]
                if blocks is not None:
                    held.append((blocks, blocks.held[: 1 << level]))
            filled.append(held)
        core_held = []
        for chains, others, start, stop in self.core_work:
            for blocks, other in zip(chains, others):
                if blocks is not None:
                    core_held.append((blocks, other, blocks.held[start:stop]))
        direct = not core_held and all(len(h) == 1 and len(h[0][1]) == 1 for h in filled)
        if direct:
            payloads = [h[0][1][0][0] for h in filled]
            if earlier:
                payloads = after(payloads, *earlier)
        else:
            for held in filled:
                if held:
                    target = jobs.output(sum(b.rows * len(h) for b, h in held))
                    row = 0
                    for blocks, part in held:
                        place(jobs, part, blocks.rows, target, row)
                        row += blocks.rows * len(part)
            if core_held:
                target = jobs.output(sum(b.rows * len(h) for b, _, h in core_held))
                row = 0
                for blocks, _, part in core_held:
                    place(jobs, part, blocks.rows, target, row)
                    row += blocks.rows * len(part)
            payloads = jobs.run(self.meta, self.name, *earlier)
            self.packed = payloads
            if gate:
                axes = sum(1 for held in filled if held)
                payloads = after(list(payloads[:axes]), *gate) + list(payloads[axes:])
        got = []
        index = 0
        for axis, held in enumerate(filled):
            if not held:
                continue
            array = self.cube.swap(payloads[index], 1 + axis)
            index += 1
            row = 0
            for blocks, part in held:
                blocks.arrived(array, row, len(part))
                row += blocks.rows * len(part)
            got.append(array)
        self.got = got
        self.core_got = None
        if core_held:
            array = self.cube.swap(payloads[index], 0)
            row = 0
            for blocks, other, part in core_held:
                other.arrived(array, row, len(part))
                row += blocks.rows * len(part)
            self.core_got = array
        self.payloads = payloads
        return self


def operands(*chains):
    arrays, tables = [], []
    for blocks in chains:
        table = []
        for array, row in blocks.held:
            found = [i for i, a in enumerate(arrays) if a is array]
            if not found:
                arrays.append(array)
                found = [len(arrays) - 1]
            table.append((found[0], row))
        tables.append((blocks.rows, table))
    return arrays, tables


class Sums:
    def __init__(self, keep, send, rows, final):
        self.keep, self.send, self.rows, self.count, self.final = keep, send, rows, 4, final


def reduce_round(cube, meta, width, name, work, *earlier, squares=False, gate=(), norm=(), waits=()):
    jobs = Jobs(width)
    filled = []
    direct = all(step == 0 for _, step in work) and len(work) == 1
    for axis in range(3):
        parts = []
        for chains, step in work:
            if step < 3:
                chain = chains[(axis - (2 - step)) % 3]
                if chain is not None:
                    parts.append((chain, step))
        filled.append(parts)
    if direct:
        payloads = [parts[0][0].send[0] for parts in filled]
        if earlier:
            payloads = after(payloads, *earlier)
    else:
        layout = []
        for parts in filled:
            if not parts:
                continue
            rows = 0
            target = None
            sizes = []
            for chain, step in parts:
                size = chain.rows * (4 >> step)
                sizes.append((chain, step, rows, size))
                rows += size
            layout.append((jobs.output(rows), sizes))
        kept = {}
        for target, sizes in layout:
            for chain, step, row, size in sizes:
                if step == 0:
                    jobs.copy(chain.send[0], chain.send[1], target, row, size)
                else:
                    got, got_row = chain.got
                    array, keep_row = chain.keep
                    own = jobs.output(size)
                    jobs.add(got, got_row + size, array, keep_row + size, target, row, size)
                    jobs.add(got, got_row, array, keep_row, own, 0, size)
                    kept[own] = chain
        for chains, step in work:
            if step == 3:
                for chain in chains:
                    if chain is not None:
                        chain.final(jobs, chain.got, chain.keep, chain.rows)
        out = jobs.run(meta, name, *earlier, squares=squares, norm=norm, waits=waits)
        for own, chain in kept.items():
            chain.keep = (out[own], 0)
        payloads = [out[target] for target, _ in layout]
        if gate and payloads:
            payloads = after(payloads, *gate)
    got = []
    index = 0
    for axis, parts in enumerate(filled):
        if not parts:
            continue
        array = cube.swap(payloads[index], 1 + axis)
        index += 1
        row = 0
        for chain, step in parts:
            chain.got = (array, row)
            row += chain.rows * (4 >> step)
        got.append(array)
    return (got, out) if not direct else (got, None)


def first_kernel(joint, q, k, v):
    width = q.shape[1]
    q[...] = joint[:, :width].astype(BF)
    k[...] = joint[:, width : 2 * width].astype(BF)
    v[: joint.shape[0]] = joint[:, 2 * width :].astype(BF)


def first_shards(joint):
    rows, width = joint.shape[0], joint.shape[1] // 3
    return pl.pallas_call(
        first_kernel,
        in_specs=[VM],
        out_specs=[VM] * 3,
        out_shape=[jax.ShapeDtypeStruct((r, width), BF) for r in (rows, rows, rows + 16)],
        compiler_params=pltpu.CompilerParams(vmem_limit_bytes=60 * MIB),
        name="first_shards",
    )(joint)


def split_kernel(meta, expand, shrink, output, own, give, shrink_own, shrink_give, out_a, out_b):
    core, group = meta[1], meta[2]
    rows = expand.shape[0]
    block = expand.shape[1] // (2 * 2 * 2 * CHIPS)
    for turn in range(2):
        part = turn ^ (1 - group)
        for kind in range(2):
            for chip in range(CHIPS):
                base = ((kind * 2 + part) * CHIPS + chip) * 2
                cols = slice(chip * block, (chip + 1) * block)
                r = slice((turn * 2 + kind) * rows, (turn * 2 + kind + 1) * rows)
                own[r, cols] = expand[:, aligned(base + core, block)].astype(BF)
                give[r, cols] = expand[:, aligned(base + 1 - core, block)].astype(BF)
    shrink_own[...] = shrink[group].astype(BF)
    shrink_give[...] = shrink[1 - group].astype(BF)
    out_a[...] = output[: rows // 2].astype(BF)
    out_b[...] = output[rows // 2 :].astype(BF)


def split_weights(meta, expand, shrink, output):
    rows, width = output.shape
    four = jax.ShapeDtypeStruct((4 * rows, width), BF)
    two = jax.ShapeDtypeStruct(shrink.shape[1:], BF)
    half = jax.ShapeDtypeStruct((rows // 2, width), BF)
    return pl.pallas_call(
        split_kernel,
        in_specs=[SM, VM, VM, VM],
        out_specs=[VM] * 6,
        out_shape=[four, four, two, two, half, half],
        compiler_params=pltpu.CompilerParams(vmem_limit_bytes=60 * MIB),
        name="split_weights",
    )(meta, expand, shrink, output)


def load_blocks(table, refs, w, k, chip, sem):
    copies = []
    rows, places = table
    for j, (index, row) in enumerate(places):
        target = w.at[aligned(chip ^ CHAIN_MASKS[k][j], rows), :]
        copy = pltpu.make_async_copy(refs[index].at[row : row + rows], target, sem.at[j])
        copy.start()
        copies.append(copy)
    return copies


def store_blocks(w, pieces, rows, k, chip, sem):
    copies = []
    for j in range(CHIPS):
        source = w.at[aligned(chip ^ CHAIN_MASKS[k][j], rows), :]
        row = (j % 4) * rows
        copy = pltpu.make_async_copy(source, pieces[j // 4].at[row : row + rows], sem.at[j])
        copy.start()
        copies.append(copy)
    return copies


def finish(copies):
    for copy in copies:
        copy.wait()


TILE = 256


def ffn_rows_kernel(first, count, tables, meta, n2m, n2o, cm, co, *refs):
    pieces = refs[:count]
    refs = refs[count:]
    if not first:
        dn_in = refs[0]
        refs = refs[1:]
    if first:
        dn_out, hid, dg, du, n2, c, wg, wu, ws, sem = refs
    else:
        dn_out, dn_send, hid, dg, du, n2, c, wg, wu, ws, sem = refs
    chip = meta[0]
    mats = (wg, wu, ws)
    coming = [load_blocks(tables[k], pieces, mats[k], k, chip, sem.at[k]) for k in range(3)]
    rows = n2m.shape[0]
    n2[:rows] = n2m[...]
    n2[rows:] = n2o[...]
    c[:rows] = cm[...]
    c[rows:] = co[...]
    for copies in coming:
        finish(copies)
    width = wg.shape[1]

    def gates(t, _):
        cols = aligned(t, TILE)
        g = dot(n2[...], wg[:, cols])
        u = dot(n2[...], wu[:, cols])
        dh = dot_nt(c[...], ws[cols, :])
        sig = jax.nn.sigmoid(g)
        silu = g * sig
        hid[:, cols] = (silu * u).astype(BF)
        du[:, cols] = (dh * silu).astype(BF)
        dg[:, cols] = (dh * u * sig * (1.0 + g * (1.0 - sig))).astype(BF)
        return 0

    lax.fori_loop(0, width // TILE, gates, 0, unroll=True)

    def back(t, _):
        cols = aligned(t, TILE)
        d = dot_nt(dg[...], wg[cols, :]) + dot_nt(du[...], wu[cols, :])
        if first:
            dn_out[:, cols] = d
        else:
            d = d + dn_in[:, cols]
            dn_out[:, cols] = d[:rows]
            dn_send[:, cols] = d[rows:]
        return 0

    lax.fori_loop(0, width // TILE, back, 0, unroll=True)


def ffn_rows(meta, n2m, n2o, cm, co, chains, carried):
    first = carried is None
    arrays, tables = operands(*chains)
    rows, width = 2 * n2m.shape[0], n2m.shape[1]
    low = jax.ShapeDtypeStruct((rows, width), BF)
    return pl.pallas_call(
        functools.partial(ffn_rows_kernel, first, len(arrays), tables),
        in_specs=[SM] + [VM] * 4 + [HB] * len(arrays) + ([] if first else [VM]),
        out_specs=[VM] * (4 if first else 5),
        out_shape=(
            [jax.ShapeDtypeStruct((rows, width), F32)]
            if first
            else [jax.ShapeDtypeStruct((rows // 2, width), F32)] * 2
        )
        + [low, low, low],
        scratch_shapes=[pltpu.VMEM((rows, width), BF)] * 2
        + [pltpu.VMEM((width, width), BF)] * 3
        + [pltpu.SemaphoreType.DMA((3, CHIPS))],
        compiler_params=pltpu.CompilerParams(vmem_limit_bytes=60 * MIB),
        cost_estimate=SMALL,
        name="ffn_rows",
    )(meta, n2m, n2o, cm, co, *arrays, *(() if first else (carried,)))


def ffn_weights_kernel(first, count, table, meta, n2m, n2o, cm, co, hid, dg, du, *refs):
    pieces = refs[:count]
    refs = refs[count:]
    if not first:
        f_in = refs[0]
        refs = refs[1:]
    f_out = refs[0]
    if not first:
        f_send = refs[1]
        refs = refs[1:]
    outs = refs[1:7]
    n2, c, ws, dwg, dwu, dws, in_sem, out_sem = refs[7:]
    chip = meta[0]
    coming = load_blocks(table, pieces, ws, 2, chip, in_sem)
    rows = n2m.shape[0]
    n2[:rows] = n2m[...]
    n2[rows:] = n2o[...]
    c[:rows] = cm[...]
    c[rows:] = co[...]
    width = ws.shape[1]
    leaving = []
    for k, (lhs, rhs, dw) in enumerate(((n2, dg, dwg), (n2, du, dwu), (hid, c, dws))):

        def step(t, _, lhs=lhs, rhs=rhs, dw=dw):
            cols = aligned(t, TILE)
            dw[cols, :] = dot_tn(lhs[:, cols], rhs[...]).astype(BF)
            return 0

        lax.fori_loop(0, width // TILE, step, 0, unroll=True)
        leaving += store_blocks(dw, outs[2 * k : 2 * k + 2], table[0], k, chip, out_sem.at[k])
    finish(coming)

    def down(t, _):
        cols = aligned(t, TILE)
        f = dot(hid[...], ws[:, cols])
        if first:
            f_out[:, cols] = f
        else:
            f = f + f_in[:, cols]
            f_out[:, cols] = f[:rows]
            f_send[:, cols] = f[rows:].astype(BF)
        return 0

    lax.fori_loop(0, width // TILE, down, 0, unroll=True)
    finish(leaving)


def ffn_weights(meta, n2m, n2o, cm, co, hid, dg, du, chain, carried):
    first = carried is None
    arrays, tables = operands(chain)
    rows, width = 2 * n2m.shape[0], n2m.shape[1]
    piece = jax.ShapeDtypeStruct((4 * chain.rows, width), BF)
    return pl.pallas_call(
        functools.partial(ffn_weights_kernel, first, len(arrays), tables[0]),
        in_specs=[SM] + [VM] * 7 + [HB] * len(arrays) + ([] if first else [VM]),
        out_specs=[VM] * (1 if first else 2) + [HB] * 6,
        out_shape=(
            [jax.ShapeDtypeStruct((rows, width), F32)]
            if first
            else [
                jax.ShapeDtypeStruct((rows // 2, width), F32),
                jax.ShapeDtypeStruct((rows // 2, width), BF),
            ]
        )
        + [piece] * 6,
        scratch_shapes=[pltpu.VMEM((rows, width), BF)] * 2
        + [pltpu.VMEM((width, width), BF)] * 4
        + [pltpu.SemaphoreType.DMA((CHIPS,)), pltpu.SemaphoreType.DMA((3, CHIPS))],
        compiler_params=pltpu.CompilerParams(vmem_limit_bytes=60 * MIB),
        cost_estimate=SMALL,
        name="ffn_weights",
    )(meta, n2m, n2o, cm, co, hid, dg, du, *arrays, *(() if first else (carried,)))


OUTPUT_CHAINS = (1, 2)


def load_devices(table, refs, k, side, shard, row, count, target, lo, meta, sem, used):
    chip, core = meta[0], meta[1]
    copies = []
    for j, (index, base) in enumerate(table[1]):
        device = (chip ^ CHAIN_MASKS[k][j]) * 2 + (core if side == 0 else 1 - core)
        start = pl.multiple_of(device * shard + row, 16)
        copy = pltpu.make_async_copy(
            refs[index].at[base : base + count],
            target.at[pl.ds(start, count), lo : lo + target.shape[0]],
            sem.at[used + j],
        )
        copy.start()
        copies.append(copy)
    return copies


def load_joint(tables, refs, target, meta, sem):
    width = target.shape[0]
    shard = width // (2 * CHIPS)
    copies = []
    for k in range(3):
        for side in range(2):
            copies += load_devices(
                tables[3 * side + k], refs, k, side, shard, 0, shard, target, k * width, meta, sem, len(copies)
            )
    return copies


def load_output(tables, refs, target, meta, sem):
    shard = target.shape[0] // (2 * CHIPS)
    half = shard // 2
    copies = []
    for i, k in enumerate(OUTPUT_CHAINS):
        for side in range(2):
            copies += load_devices(
                tables[2 * side + i], refs, k, side, shard, i * half, half, target, 0, meta, sem, len(copies)
            )
    return copies


PAIR_COPIES = 128
PAD = 16


def joint_kernel(count, tables, meta, x, *refs):
    pieces = refs[:count]
    first, query, pair, gains, w, gain_rows, sem, gain_sem = refs[count:]
    width = x.shape[1]
    coming = load_joint(tables, pieces, w, meta, sem)
    shard = width // (2 * CHIPS)
    gain_copies = []
    for side in range(2):
        for j, (index, base) in enumerate(tables[3 * side + 2][1]):
            copy = pltpu.make_async_copy(
                pieces[index].at[base + shard : base + shard + 16],
                gain_rows.at[side * CHIPS + j],
                gain_sem.at[side * CHIPS + j],
            )
            copy.start()
            gain_copies.append(copy)
    value = x[...].astype(F32)
    inverse = lax.rsqrt(jnp.mean(value * value, axis=-1, keepdims=True) + NORM_EPS)
    finish(gain_copies)
    whole = jnp.sum(gain_rows[...].astype(F32), axis=0)
    gains[...] = whole[:8]
    first[...] = (value * inverse * whole[0:1]).astype(BF)
    finish(coming)
    tiles = width // TILE
    rows = x.shape[0]
    pair[2 * rows :] = jnp.zeros((PAD, width), BF)
    for part, (out, low) in enumerate(((query, 0), (pair, 0), (pair, rows))):

        def step(t, _, part=part, out=out, low=low):
            weight = w[:, aligned(t + part * tiles, TILE)]
            out[low : low + rows, aligned(t, TILE)] = dot(first[...], weight).astype(BF)
            return 0

        lax.fori_loop(0, tiles, step, 0, unroll=True)


def joint_forward(meta, x, chains):
    rows, width = x.shape
    arrays, tables = operands(*chains)
    low = jax.ShapeDtypeStruct((rows, width), BF)
    return pl.pallas_call(
        functools.partial(joint_kernel, len(arrays), tables),
        in_specs=[SM, VM] + [HB] * len(arrays),
        out_specs=[VM] * 4,
        out_shape=[
            low,
            low,
            jax.ShapeDtypeStruct((2 * rows + PAD, width), BF),
            jax.ShapeDtypeStruct((8, width), F32),
        ],
        scratch_shapes=[
            pltpu.VMEM((width, 3 * width), BF),
            pltpu.VMEM((2 * CHIPS, 16, width), BF),
            pltpu.SemaphoreType.DMA((PAIR_COPIES,)),
            pltpu.SemaphoreType.DMA((2 * CHIPS,)),
        ],
        compiler_params=pltpu.CompilerParams(vmem_limit_bytes=60 * MIB),
        cost_estimate=SMALL,
        name="joint_forward",
    )(meta, x, *arrays)


CHUNK = 128


def bias_into(bias, run, upper):
    size = 2 * CHUNK
    row = lax.broadcasted_iota(jnp.int32, (size, size), 0) & (CHUNK - 1)
    column = lax.broadcasted_iota(jnp.int32, (size, size), 1)
    own = column < CHUNK
    column = column & (CHUNK - 1)
    shift = run.bit_length() - 1
    same = (row >> shift) == (column >> shift)
    reach = jnp.where(upper, CHUNK, 0)
    seen = same & ((own & (row >= column)) | (~own & (row < reach)))
    bias[...] = jnp.where(seen, 0.0, -1e30)


def stacked(value, left):
    zero = jnp.zeros_like(value)
    return jnp.concatenate([jnp.where(left, value, zero), jnp.where(left, zero, value)], axis=0)


def probabilities(q_st, k_all, bias, scale):
    scores = dot_nt(q_st, k_all) * scale + bias[...]
    exp_scores = jnp.exp(scores - jnp.max(scores, axis=-1, keepdims=True))
    return exp_scores / jnp.sum(exp_scores, axis=-1, keepdims=True)


def context_kernel(run, head_dim, count, tables, meta, query, own, other, x, live, gains, *refs):
    pieces = refs[:count]
    ctx, h_out, n2, wo, bias, sem = refs[count:]
    rows, width = x.shape
    coming = load_output(tables, pieces, wo, meta, sem)
    bias_into(bias, run, meta[2] == 1)
    scale = head_dim ** (-0.5)
    lanes = 2 * head_dim
    left = lax.broadcasted_iota(jnp.int32, (CHUNK, lanes), 1) < head_dim

    def pair(p, _):
        cols = aligned(p, lanes)
        for chunk in range(rows // CHUNK):
            r = slice(chunk * CHUNK, (chunk + 1) * CHUNK)
            r_v = slice(rows + chunk * CHUNK, rows + (chunk + 1) * CHUNK)
            q_st = stacked(query[r, cols], left)
            k_all = jnp.concatenate([own[r, cols], other[r, cols]], axis=0)
            v_all = jnp.concatenate([own[r_v, cols], other[r_v, cols]], axis=0)
            prob = probabilities(q_st, k_all, bias, scale)
            out = dot(prob.astype(BF), v_all)
            ctx[r, cols] = jnp.where(left, out[:CHUNK], out[CHUNK:]).astype(BF)
        return 0

    lax.fori_loop(0, width // lanes, pair, 0)
    finish(coming)

    def project(t, _):
        cols = aligned(t, TILE)
        h_out[:, cols] = x[:, cols].astype(F32) + live[...] * dot(ctx[...], wo[:, cols])
        return 0

    lax.fori_loop(0, width // TILE, project, 0, unroll=True)
    h = h_out[...]
    inverse = lax.rsqrt(jnp.mean(h * h, axis=-1, keepdims=True) + NORM_EPS)
    n2[...] = (h * inverse * gains[1:2, :]).astype(BF)


def context_forward(
    run, meta, query, own, other, x, live, gains, chains
):
    rows, width = x.shape
    arrays, tables = operands(*chains)
    low = jax.ShapeDtypeStruct((rows, width), BF)
    return pl.pallas_call(
        functools.partial(context_kernel, run, width // HEADS, len(arrays), tables),
        in_specs=[SM] + [VM] * 6 + [HB] * len(arrays),
        out_specs=[VM] * 3,
        out_shape=[low, jax.ShapeDtypeStruct((rows, width), F32), low],
        scratch_shapes=[
            pltpu.VMEM((width, width), BF),
            pltpu.VMEM((2 * CHUNK, 2 * CHUNK), F32),
            pltpu.SemaphoreType.DMA((PAIR_COPIES,)),
        ],
        compiler_params=pltpu.CompilerParams(vmem_limit_bytes=60 * MIB),
        cost_estimate=SMALL,
        name="context_forward",
    )(meta, query, own, other, x, live, gains, *arrays)


def norm_back(value, gain, grad):
    inverse = lax.rsqrt(jnp.mean(value * value, axis=-1, keepdims=True) + NORM_EPS)
    scaled = grad * gain
    mean = jnp.mean(scaled * value, axis=-1, keepdims=True)
    grad_in = inverse * scaled - value * (inverse * inverse * inverse) * mean
    return grad_in, jnp.sum(grad * value * inverse, axis=0, keepdims=True)


def context_back_kernel(
    run, head_dim, count, tables, meta, dn_own, dn_got, h, cot, live, gains, query, *refs
):
    own, other = refs[:2]
    pieces = refs[2 : 2 + count]
    dh, dg2, da, dq, dkv, give, wo, bias, dctx, sem = refs[2 + count :]
    rows, width = h.shape
    coming = load_output(tables, pieces, wo, meta, sem)
    bias_into(bias, run, meta[2] == 1)
    give[2 * rows :] = jnp.zeros((PAD, width), BF)
    grad_in, dg2[...] = norm_back(h[...], gains[1:2, :], dn_own[...] + dn_got[...])
    grad = cot[...].astype(F32) + grad_in
    dh[...] = grad
    da[...] = (grad * live[...]).astype(BF)
    finish(coming)

    def project(t, _):
        cols = aligned(t, TILE)
        dctx[:, cols] = dot_nt(da[...], wo[cols, :]).astype(BF)
        return 0

    lax.fori_loop(0, width // TILE, project, 0, unroll=True)
    scale = head_dim ** (-0.5)
    lanes = 2 * head_dim
    pairs = width // lanes
    left = lax.broadcasted_iota(jnp.int32, (CHUNK, lanes), 1) < head_dim

    def pair(p, _):
        cols = aligned(p, lanes)
        v_cols = aligned(p + pairs, lanes)
        for chunk in range(rows // CHUNK):
            r = slice(chunk * CHUNK, (chunk + 1) * CHUNK)
            r_v = slice(rows + chunk * CHUNK, rows + (chunk + 1) * CHUNK)
            q_st = stacked(query[r, cols], left)
            g_st = stacked(dctx[r, cols], left)
            k_all = jnp.concatenate([own[r, cols], other[r, cols]], axis=0)
            v_all = jnp.concatenate([own[r_v, cols], other[r_v, cols]], axis=0)
            prob = probabilities(q_st, k_all, bias, scale)
            d_prob = dot_nt(g_st, v_all)
            d_score = prob * (d_prob - jnp.sum(d_prob * prob, axis=-1, keepdims=True))
            d_score = d_score.astype(BF)
            d_query = dot(d_score, k_all) * scale
            d_key = dot_tn(d_score, q_st) * scale
            d_value = dot_tn(prob.astype(BF), g_st)
            dq[r, cols] = jnp.where(left, d_query[:CHUNK], d_query[CHUNK:]).astype(BF)
            dkv[r, cols] = d_key[:CHUNK]
            dkv[r, v_cols] = d_value[:CHUNK]
            give[r, cols] = d_key[CHUNK:].astype(BF)
            give[r_v, cols] = d_value[CHUNK:].astype(BF)
        return 0

    lax.fori_loop(0, pairs, pair, 0, unroll=2)


def context_back(
    run, meta, dn_own, dn_got, h, cot, live, gains, query, own, other, chains
):
    rows, width = h.shape
    arrays, tables = operands(*chains)
    low = jax.ShapeDtypeStruct((rows, width), BF)
    return pl.pallas_call(
        functools.partial(context_back_kernel, run, width // HEADS, len(arrays), tables),
        in_specs=[SM] + [VM] * 9 + [HB] * len(arrays),
        out_specs=[VM] * 6,
        out_shape=[
            jax.ShapeDtypeStruct((rows, width), F32),
            jax.ShapeDtypeStruct((1, width), F32),
            low,
            low,
            jax.ShapeDtypeStruct((rows, 2 * width), F32),
            jax.ShapeDtypeStruct((2 * rows + PAD, width), BF),
        ],
        scratch_shapes=[
            pltpu.VMEM((width, width), BF),
            pltpu.VMEM((2 * CHUNK, 2 * CHUNK), F32),
            pltpu.VMEM((rows, width), BF),
            pltpu.SemaphoreType.DMA((PAIR_COPIES,)),
        ],
        compiler_params=pltpu.CompilerParams(vmem_limit_bytes=60 * MIB),
        cost_estimate=SMALL,
        name="context_back",
    )(
        meta,
        dn_own,
        dn_got,
        h,
        cot,
        live,
        gains,
        query,
        own,
        other,
        *arrays,
    )


def shard_grads(lhs, rhs_cols, dw):
    width = lhs.shape[1]
    for i, rhs in enumerate(rhs_cols):

        def step(t, _, rhs=rhs, i=i):
            cols = aligned(t, TILE)
            dw[i, cols, :] = dot_tn(lhs[:, cols], rhs()).astype(BF)
            return 0

        lax.fori_loop(0, width // TILE, step, 0, unroll=True)


def store_devices(dw, matrix, row, count, k, targets, base, meta, sem, used):
    chip, core = meta[0], meta[1]
    shard = dw.shape[1] // (2 * CHIPS)
    copies = []
    for side, target in enumerate(targets):
        for j in range(CHIPS):
            device = (chip ^ CHAIN_MASKS[k][j]) * 2 + (1 - core if side == 0 else core)
            start = pl.multiple_of(device * shard + row, 16)
            low = base + j * count
            copy = pltpu.make_async_copy(
                dw.at[matrix, pl.ds(start, count), :],
                target.at[low : low + count],
                sem.at[used + len(copies)],
            )
            copy.start()
            copies.append(copy)
    return copies


def output_grad_kernel(meta, context, grad, give, keep, dw, sem):
    shard_grads(context, (lambda: grad[...],), dw)
    half = dw.shape[1] // (4 * CHIPS)
    leaving = []
    for i, k in enumerate(OUTPUT_CHAINS):
        base = i * CHIPS * half
        leaving += store_devices(
            dw, 0, i * half, half, k, (give, keep), base, meta, sem, len(leaving)
        )
    finish(leaving)


def output_grad(meta, context, grad):
    rows, width = context.shape
    part = jax.ShapeDtypeStruct((width // 2, width), BF)
    return pl.pallas_call(
        output_grad_kernel,
        in_specs=[SM, VM, VM],
        out_specs=[HB, HB],
        out_shape=[part, part],
        scratch_shapes=[
            pltpu.VMEM((1, width, width), BF),
            pltpu.SemaphoreType.DMA((PAIR_COPIES,)),
        ],
        compiler_params=pltpu.CompilerParams(vmem_limit_bytes=60 * MIB),
        cost_estimate=SMALL,
        name="output_grad",
    )(meta, context, grad)


def joint_grad_kernel(meta, first, dq, dkv_own, dkv_got, give, keep, dkv):
    width = first.shape[1]
    rows = first.shape[0]
    chip, core = meta[0], meta[1]
    for part in range(2):
        cols = slice(part * width, (part + 1) * width)
        got = dkv_got[part * rows : (part + 1) * rows, :]
        more = jnp.where(meta[2] == 1, 0.0, got.astype(F32))
        dkv[:, cols] = (dkv_own[:, cols] + more).astype(BF)
    rights = (lambda: dq[...], lambda: dkv[:, :width], lambda: dkv[:, width:])
    shard = width // (2 * CHIPS)
    for k in range(3):
        for j in range(CHIPS):
            grad = dot_tn(first[:, aligned(chip ^ CHAIN_MASKS[k][j], 2 * shard)], rights[k]())
            low, high = grad[:shard].astype(BF), grad[shard:].astype(BF)
            at = slice((k * CHIPS + j) * shard, (k * CHIPS + j + 1) * shard)
            give[at] = jnp.where(core == 0, high, low)
            keep[at] = jnp.where(core == 0, low, high)


def joint_grad(meta, first, dq, dkv_own, dkv_got):
    rows, width = first.shape
    part = jax.ShapeDtypeStruct((3 * width // 2, width), BF)
    return pl.pallas_call(
        joint_grad_kernel,
        in_specs=[SM] + [VM] * 4,
        out_specs=[VM] * 3,
        out_shape=[part, part, jax.ShapeDtypeStruct((rows, 2 * width), BF)],
        compiler_params=pltpu.CompilerParams(vmem_limit_bytes=60 * MIB),
        cost_estimate=SMALL,
        name="joint_grad",
    )(meta, first, dq, dkv_own, dkv_got)


def input_back_kernel(count, tables, meta, dq, dkv, dh, x, gains, *refs):
    pieces = refs[:count]
    out, dg1, w, dn, sem = refs[count:]
    rows, width = x.shape
    finish(load_joint(tables, pieces, w, meta, sem))

    def step(t, _):
        cols = aligned(t, TILE)
        dn[:, cols] = dot_nt(dq[...], w[cols, :width]) + dot_nt(dkv[...], w[cols, width:])
        return 0

    lax.fori_loop(0, width // TILE, step, 0, unroll=True)
    grad_in, dg1[...] = norm_back(x[...].astype(F32), gains[0:1, :], dn[...])
    out[...] = (dh[...] + grad_in).astype(BF)


def input_back(meta, dq, dkv, dh, x, gains, chains):
    rows, width = x.shape
    arrays, tables = operands(*chains)
    return pl.pallas_call(
        functools.partial(input_back_kernel, len(arrays), tables),
        in_specs=[SM] + [VM] * 5 + [HB] * len(arrays),
        out_specs=[VM, VM],
        out_shape=[
            jax.ShapeDtypeStruct((rows, width), BF),
            jax.ShapeDtypeStruct((1, width), F32),
        ],
        scratch_shapes=[
            pltpu.VMEM((width, 3 * width), BF),
            pltpu.VMEM((rows, width), F32),
            pltpu.SemaphoreType.DMA((PAIR_COPIES,)),
        ],
        compiler_params=pltpu.CompilerParams(vmem_limit_bytes=60 * MIB),
        cost_estimate=SMALL,
        name="input_back",
    )(meta, dq, dkv, dh, x, gains, *arrays)


def adam_in_place(k, w, m, v, grad, where, rate, decay):
    grad = k * grad
    mean = BETA_ONE * m[where] + (1.0 - BETA_ONE) * grad
    square = BETA_TWO * v[where] + (1.0 - BETA_TWO) * grad * grad
    root = jnp.sqrt(square * (1.0 / (1.0 - BETA_TWO**STEP))) + ADAM_EPS
    old = w[where]
    move = mean * (rate / (1.0 - BETA_ONE**STEP)) / root
    w[where] = old - (move + (rate * decay) * old)
    m[where] = mean
    v[where] = square


def adam_kernel(meta, squares, *refs):
    sources, targets, held = refs[:21], refs[21:33], refs[33:54]
    in_sem, out_sem = refs[54:]
    core, group = meta[1], meta[2]
    (ew, em, ev, own_a, own_b, got_a, got_b, jw, jm, jv, jg, ow, om, ov, og_a, og_b) = held[:16]
    (sw, sm, sv, sg_mine, sg_got) = held[16:]
    width = own_a.shape[1]
    rows = ew.shape[0]
    started = []

    def load(index, where):
        copy = pltpu.make_async_copy(
            sources[index].at[where], held[index].at[where], in_sem.at[len(started)]
        )
        copy.start()
        started.append(copy)
        return copy

    def whole(ref):
        return (slice(None),) * len(ref.shape)

    pieces = []
    gradients = [load(i, whole(held[i])) for i in (3, 4, 5, 6)]
    for c in range(4):
        where = (slice(None), slice(2 * c * width, 2 * (c + 1) * width))
        pieces.append(("expand", c, where, [load(i, where) for i in (0, 1, 2)]))
    copies = [load(i, whole(held[i])) for i in (10, 7, 8, 9)]
    pieces.append(("joint", 0, whole(jw), copies))
    copies = [load(i, whole(held[i])) for i in (14, 15, 11, 12, 13)]
    pieces.append(("output", 0, None, copies))
    more = [load(i, whole(held[i])) for i in (19, 20)]
    for c in range(sw.shape[0]):
        pieces.append(("shrink", c, (c,), (more if c == 0 else []) + [load(i, (c,)) for i in (16, 17, 18)]))

    sums = jnp.sum(squares[...], axis=0)
    total = sums[0:1, 0:1] + jnp.sum(sums[1:] * sums[1:])
    k = CLIP_LIMIT / jnp.maximum(jnp.sqrt(total), CLIP_LIMIT)
    finish(gradients)
    leaving = []

    def store(target, index, where):
        copy = pltpu.make_async_copy(
            held[index].at[where], targets[target].at[where], out_sem.at[len(leaving)]
        )
        copy.start()
        leaving.append(copy)

    block = width // CHIPS
    for kind, c, where, copies in pieces:
        finish(copies)
        if kind == "expand":
            turn = (c % 2) ^ (1 - group)
            r = slice((c // 2) * rows, (c // 2 + 1) * rows)
            for q in range(2 * CHIPS):
                near = (r, slice((q // 2) * block, (q // 2 + 1) * block))
                own = jnp.where(turn == 0, own_a[near], own_b[near])
                got = jnp.where(turn == 0, got_a[near], got_b[near])
                grad = jnp.where(core == q % 2, own, got)
                low = 2 * c * width + q * block
                cols = (slice(None), slice(low, low + block))
                adam_in_place(k, ew, em, ev, grad, cols, MATRIX_RATE, MATRIX_DECAY)
            for i in range(3):
                store(i, i, where)
        elif kind == "joint":
            for part in range(jg.shape[0]):
                cols = (slice(None), slice(part * width, (part + 1) * width))
                adam_in_place(k, jw, jm, jv, jg[part], cols, MATRIX_RATE, MATRIX_DECAY)
            for i in range(3):
                store(3 + i, 7 + i, where)
        elif kind == "output":
            half = og_a.shape[0]
            for part, grad in enumerate((og_a, og_b)):
                at = (slice(part * half, (part + 1) * half),)
                adam_in_place(k, ow, om, ov, grad[...], at, MATRIX_RATE, MATRIX_DECAY)
            for i in range(3):
                store(6 + i, 11 + i, whole(ow))
        else:
            grad = jnp.where(group == c, sg_mine[...], sg_got[...].astype(F32))
            adam_in_place(k, sw, sm, sv, grad, where, MATRIX_RATE, MATRIX_DECAY)
            for i in range(3):
                store(9 + i, 16 + i, where)
    finish(leaving)


def adam_matrices(meta, squares, expand, joint, output, shrink):
    arrays = (*expand, *joint, *output, *shrink)
    shapes = [jax.ShapeDtypeStruct(p[0].shape, F32) for p in (expand, joint, output, shrink)]
    return pl.pallas_call(
        adam_kernel,
        in_specs=[SM, VM] + [HB] * len(arrays),
        out_specs=[HB] * 12,
        out_shape=[s for s in shapes for _ in range(3)],
        scratch_shapes=[pltpu.VMEM(a.shape, a.dtype) for a in arrays]
        + [pltpu.SemaphoreType.DMA((64,)), pltpu.SemaphoreType.DMA((64,))],
        compiler_params=pltpu.CompilerParams(vmem_limit_bytes=60 * MIB),
        cost_estimate=SMALL,
        name="adam_matrices",
    )(meta, squares, *arrays)


def local_cube(
    count,
    tokens,
    depth_count,
    cotangent,
    joint_weight,
    output_weight,
    expand_weight,
    shrink_weight,
    norm_gains,
    joint_mean,
    joint_square,
    output_mean,
    output_square,
    expand_mean,
    expand_square,
    shrink_mean,
    shrink_square,
    gains_mean,
    gains_square,
):
    cube = Cube(count)
    frames, positions, width = tokens.shape
    run = positions // SETS
    group = cube.bit(cube.top)
    core = cube.bit(0)
    upper = group == 1
    second_core = core == 1
    all_frames = 2 * frames
    rows = all_frames * run
    chip = (cube.index >> 1) & (CHIPS - 1)
    meta = jnp.stack([chip, core, group]).astype(jnp.int32)

    def halves(own, other):
        return jnp.concatenate([jnp.where(upper, other, own), jnp.where(upper, own, other)], axis=0)

    def parted(value):
        first, second = value[:, :run], value[:, run:]
        own, other = jnp.where(upper, second, first), jnp.where(upper, first, second)
        return own.reshape(rows // 2, width), other.reshape(rows // 2, width)

    def from_sets(value):
        value = value.reshape(2, frames, run, width)
        own = jnp.where(upper, value[1], value[0])
        other = cube.swap(jnp.where(upper, value[0], value[1]), cube.top)
        first = jnp.where(upper, other, own)
        second = jnp.where(upper, own, other)
        return jnp.concatenate([first, second], axis=1)

    shard_rows = joint_weight.shape[0]
    lane = norm_gains.shape[1]
    small = jnp.concatenate([norm_gains.astype(BF).reshape(-1), depth_count.astype(BF)])
    small_other = cube.swap(small.reshape(1, -1), cube.top)[0]
    depth_all = halves(small[2 * lane :], small_other[2 * lane :]).astype(jnp.int32)
    gain_pair = halves(small[None, : 2 * lane], small_other[None, : 2 * lane])
    gain_pair = gain_pair.reshape(2, 2, lane).transpose(1, 0, 2)
    spread = jnp.broadcast_to(gain_pair[:, :, None, :], (2, 2, 2 * CHIPS, lane)).reshape(2, width)
    mine = (jnp.arange(width) // lane) % (2 * CHIPS) == (cube.index & (2 * CHIPS - 1))
    gain_rows = jnp.pad(jnp.where(mine[None, :], spread, 0), ((0, 14), (0, 0)))
    shards = list(first_shards(joint_weight))
    shards[2] = lax.dynamic_update_slice(shards[2], gain_rows, (shard_rows, 0))
    joint = [Blocks(shard) for shard in shards]
    x_own, x_give = parted(tokens)
    x_got = cube.swap(x_give, cube.top)
    x_rows = halves(x_own, x_got)

    def begin(name):
        return Round(cube, meta, width, name)

    one = begin("pack_one").gather(joint, 0).run(x_give)
    own_cols, give_cols, shrink_keep, shrink_give, out_a, out_b = split_weights(
        meta, expand_weight, shrink_weight, output_weight
    )
    output = [None, Blocks(out_a), Blocks(out_b)]
    joint_other = [Blocks(rows=blocks.rows) for blocks in joint]
    output_other = [None] + [Blocks(rows=blocks.rows) for blocks in output[1:]]
    two = begin("pack_two").gather(joint, 1).gather(output, 0).run(one.got, give_cols)
    shrink_other = cube.swap(after(shrink_give, two.got, x_got), cube.top)
    got_cols = cube.swap(after(give_cols, two.got, x_got), 0)
    three = begin("pack_three").gather(joint, 2).gather(output, 1)
    three = three.core(joint, joint_other, 0, 4).run(two.got, x_got)
    units = Jobs(width)
    unit_rows = 2 * shard_rows
    for kind in range(2):
        target = units.output(2 * unit_rows)
        for turn_index in range(2):
            unit = turn_index * 2 + kind
            base = turn_index * unit_rows
            low, high = (base, base + shard_rows), (base + shard_rows, base)
            units.copy(own_cols, unit * shard_rows, target, low, shard_rows)
            units.copy(got_cols, unit * shard_rows, target, high, shard_rows)
    target = units.output(2 * unit_rows)
    units.copy(shrink_other, 0, target, 0, unit_rows)
    units.copy(shrink_keep, 0, target, unit_rows, unit_rows)
    units = units.run(meta, "expand_units", three.packed)
    part_a = [Blocks(unit, unit_rows) for unit in units]
    part_b = [Blocks(rows=unit_rows) for unit in units]
    for blocks, unit in zip(part_b, units):
        blocks.arrived(unit, unit_rows, 1)

    cot_own, cot_give = parted(cotangent)
    cot_got = cube.swap(after(cot_give, three.packed, shrink_other), cube.top)
    late = begin("pack_late").core(joint, joint_other, 4, 8)
    late = late.run(three.got, three.core_got, units, x_rows)
    first_units = after(units, three.got, three.core_got)
    got_four = [cube.swap(unit, 1 + axis) for axis, unit in enumerate(first_units)]
    for k in range(3):
        part_a[k].arrived(got_four[k], 0, 1)
        part_b[k].arrived(got_four[k], unit_rows, 1)

    position = group * run + jnp.arange(run)
    live = (position[None, :] < depth_all[:, None]).astype(F32).reshape(rows, 1)

    first, query, key_value, gains_all = joint_forward(meta, x_rows, joint + joint_other)
    key_value_other = cube.swap(key_value, cube.top)
    five = begin("pack_five").gather(part_a, 1).gather(part_b, 1).run(got_four, key_value, cot_got)
    last = begin("pack_output").gather(output, 2).run(five.packed)
    output_core = begin("pack_core").core(output, output_other, 0, 8).run(last.got)
    seven = begin("pack_seven").gather(part_a, 2)
    seven = seven.run(five.got, key_value_other, output_core.packed)
    cot_live = (halves(cot_own, after(cot_got, key_value)).astype(F32) * live).astype(BF)
    cot_other = cube.swap(after(cot_live, five.got, key_value_other), 0)

    output_chains = output[1:] + output_other[1:]
    context, middle, second = context_forward(
        run,
        meta,
        query,
        key_value,
        key_value_other,
        x_rows,
        live,
        gains_all,
        output_chains,
    )
    second_other = cube.swap(second, 0)
    eight = begin("pack_eight").gather(part_b, 2).run(
        seven.packed, cot_other, gate=(seven.got, second_other)
    )
    row_args = (meta, second, second_other, cot_live, cot_other)
    dn_a, *kept_a = ffn_rows(*row_args, part_a, None)
    f_a, *grad_a = ffn_weights(*row_args, *kept_a, part_a[2], None)
    dn_own, dn_send, *kept_b = ffn_rows(*row_args, part_b, after(dn_a, f_a))
    dn_got = cube.swap(dn_send, 0)
    f_own, f_send, *grad_b = ffn_weights(*row_args, *kept_b, part_b[2], f_a)

    outcome = {}

    def expand_final(key, kind):
        def final(jobs, got, keep, count):
            if key not in outcome:
                outcome[key] = (jobs.output(2 * shard_rows, F32), jobs.output(2 * shard_rows, F32))
            own, give = outcome[key]
            half = count // 2
            for target, offset in ((own, (0, half)), (give, (half, 0))):
                got_at = tuple(got[1] + o for o in offset)
                keep_at = tuple(keep[1] + o for o in offset)
                jobs.add(got[0], got_at, keep[0], keep_at, target, kind * shard_rows, half)

        return final

    def plain_final(key):
        def final(jobs, got, keep, count):
            outcome[key] = jobs.output(count, F32)
            jobs.add(got[0], got[1], keep[0], keep[1], outcome[key], 0, count)

        return final

    def ffn_sums(grads, name):
        finals = (expand_final(name, 0), expand_final(name, 1), plain_final(name + "_shrink"))
        block = grads[0].shape[0] // 4
        return [Sums((grads[2 * k], 0), (grads[2 * k + 1], 0), block, finals[k]) for k in range(3)]

    def turn(name, work, *earlier, **options):
        return reduce_round(cube, meta, width, name, work, *earlier, **options)

    def core_sums(name, tensors, *waits):
        jobs = Jobs(width)
        result = []
        payload = []
        for k in range(3):
            rows_out = sum(4 * c for *_, chains in tensors for kk, c in chains if kk == k)
            payload.append(jobs.output(rows_out))
        filled_rows = [0, 0, 0]
        for key, got, keep, chains in tensors:
            row, sums = 0, [None] * 3
            for k, c in chains:
                own = jobs.output(4 * c)
                send_row = filled_rows[k]
                jobs.add(got, row + 4 * c, keep, row + 4 * c, payload[k], send_row, 4 * c)
                jobs.add(got, row, keep, row, own, 0, 4 * c)
                filled_rows[k] += 4 * c
                sums[k] = (own, send_row, c)
                row += CHIPS * c
            result.append((key, sums))
        out = jobs.run(meta, name, waits=waits)
        made = []
        for key, sums in result:
            made.append(
                [
                    None
                    if s is None
                    else Sums((out[s[0]], 0), (out[payload[k]], s[1]), s[2], plain_final((key, k)))
                    for k, s in enumerate(sums)
                ]
            )
        return made, [out[p] for p in payload]

    shrunk_got = cube.swap(f_send, 0)
    shrunk = f_own + shrunk_got.astype(F32)
    result_rows = (middle + live * shrunk).astype(BF).reshape(2, frames, run, width)
    result_own = jnp.where(upper, result_rows[1], result_rows[0])
    result_give = jnp.where(upper, result_rows[0], result_rows[1])
    result_got = cube.swap(result_give, cube.top)
    result = jnp.concatenate(
        [jnp.where(upper, result_got, result_own), jnp.where(upper, result_own, result_got)], axis=1
    )
    sums_a = ffn_sums(grad_a, "a")
    sums_b = ffn_sums(grad_b, "b")
    turn_one, _ = turn("turn_one", [(sums_a, 0)], eight.got)
    turn_two, _ = turn("turn_two", [(sums_b, 0)], turn_one)

    grad_middle, grad_gain_two, grad_branch, d_query, dkv_own, dkv_give = context_back(
        run,
        meta,
        after(dn_own, result_give, turn_one),
        dn_got,
        middle,
        cot_live,
        live,
        gains_all,
        query,
        key_value,
        key_value_other,
        output_chains,
    )
    turn_three, packed_three = turn(
        "turn_three", [(sums_a, 1), (sums_b, 1)], turn_two, dkv_give, result_got
    )
    dkv_got = cube.swap(dkv_give, cube.top)
    output_give, output_keep = output_grad(meta, context, after(grad_branch, packed_three))
    joint_give, joint_keep, dkv = joint_grad(
        meta, first, d_query, dkv_own, after(dkv_got, output_give)
    )
    turn_four, packed_four = turn(
        "turn_four", [(sums_a, 2), (sums_b, 2)], turn_three, dkv_got, waits=(joint_give,)
    )
    joint_got = cube.swap(after(joint_give, packed_four), 0)
    output_got = cube.swap(after(output_give, packed_four), 0)
    grad_inputs, grad_gain_one = input_back(
        meta,
        d_query,
        after(dkv, packed_four),
        grad_middle,
        x_rows,
        gains_all,
        joint + joint_other,
    )
    half_shard = shard_rows // 2
    (sums_j, sums_o), sends = core_sums(
        "joint_core",
        [
            ("joint", joint_got, joint_keep, [(k, shard_rows) for k in range(3)]),
            ("output", output_got, output_keep, [(k, half_shard) for k in OUTPUT_CHAINS]),
        ],
        grad_inputs,
    )
    turn_seven = []
    for axis in range(3):
        k = (axis - 2) % 3
        array = cube.swap(sends[k], 1 + axis)
        turn_seven.append(array)
        for sums in (sums_j, sums_o):
            if sums[k] is not None:
                sums[k].got = (array, sums[k].send[1])
    grad_inputs = from_sets(after(grad_inputs, sends[0]))
    _, out_five = turn(
        "turn_five",
        [(sums_a, 3), (sums_b, 3)],
        turn_four,
        sends[0],
        squares=True,
    )
    expand_own_a, expand_give_a = (out_five[i] for i in outcome["a"])
    expand_own_b, expand_give_b = (out_five[i] for i in outcome["b"])
    shrink_first = out_five[outcome["a_shrink"]]
    shrink_mine = out_five[outcome["b_shrink"]]
    expand_got_a = cube.swap(after(expand_give_a, sends[0]), 0)
    expand_got_b = cube.swap(after(expand_give_b, expand_got_a), 0)
    turn_nine, out_nine = turn(
        "turn_nine",
        [(sums_o, 1), (sums_j, 1)],
        turn_seven,
        grad_inputs,
        waits=(out_five[-1],),
    )
    shrink_got = cube.swap(after(shrink_first.astype(BF), out_nine[0]), cube.top)
    turn_ten, out_ten = turn(
        "turn_ten", [(sums_o, 2), (sums_j, 2)], turn_nine, shrink_got
    )
    _, out_last = turn(
        "turn_last",
        [(sums_o, 3), (sums_j, 3)],
        turn_ten,
        squares=True,
        norm=(count, out_five[-1], grad_gain_one, grad_gain_two),
    )
    grad_output = [out_last[outcome[("output", k)]] for k in OUTPUT_CHAINS]
    grad_joint = jnp.stack([out_last[outcome[("joint", k)]] for k in range(3)])

    squares = lax.all_to_all(out_last[-1], "fsdp", 0, 0, tiled=True)
    gains_sum = jnp.sum(squares[:, 1 : 1 + 2 * width // 128], axis=0)
    total_sq = jnp.sum(squares[:, 0, 0]) + jnp.sum(gains_sum * gains_sum)
    grad_gains = lax.dynamic_index_in_dim(
        gains_sum.reshape(2, count, lane), cube.index, 1, keepdims=False
    )
    grad_norm_value = jnp.sqrt(total_sq)
    factor = CLIP_LIMIT / jnp.maximum(grad_norm_value, CLIP_LIMIT)
    new = adam_matrices(
        meta,
        squares,
        (
            expand_weight,
            expand_mean,
            expand_square,
            expand_own_a,
            expand_own_b,
            expand_got_a,
            expand_got_b,
        ),
        (joint_weight, joint_mean, joint_square, grad_joint),
        (output_weight, output_mean, output_square, *grad_output),
        (shrink_weight, shrink_mean, shrink_square, shrink_mine, shrink_got),
    )
    expand_new, joint_new, output_new, shrink_new = (new[i : i + 3] for i in (0, 3, 6, 9))
    gains_new = adam_step(norm_gains, factor * grad_gains, gains_mean, gains_square, GAIN_RATE, 0.0)
    return (
        result,
        grad_inputs,
        grad_norm_value,
        *joint_new,
        *output_new,
        *expand_new,
        *shrink_new,
        *gains_new,
    )


def solution(mesh):
    rows = P("fsdp", None)
    cube = P("fsdp", None, None)
    inner = P(None, "fsdp", None)
    gains = P(None, "fsdp")
    count = mesh.shape["fsdp"]

    def body(*args):
        return (local_cube if count == 4 * CHIPS else local_general)(count, *args)

    return jax.shard_map(
        body,
        mesh=mesh,
        in_specs=(cube, P("fsdp"), cube, rows, rows, rows, inner, gains)
        + (rows,) * 6
        + (inner, inner, gains, gains),
        out_specs=(cube, cube, P()) + (rows,) * 9 + (inner,) * 3 + (gains,) * 3,
        check_vma=False,
    )
```
